128 devices in a mesh: comp: 2 (over y_hi), gx: 16 (over z, x), gy: 4 (over y_lo, core).
Axes of the slice: x: 4, y: 4 (y_hi: 2, y_lo: 2; y = y_hi * 2 + y_lo), z: 4, core: 2. Of those that a mesh axis runs over, the one named last changes fastest.
Arguments:
- state: float32 [2, 16, 512, 2048], P('comp', None, 'gx', 'gy'), may hold values from -5 to 8
- guess: bfloat16 [2, 6, 512, 2048], P('comp', None, 'gx', 'gy'), may hold values from -5 to 5
- diffusion: float32 [2, 16], P('comp'), may hold values from 0.05 to 0.22
- mixing: float32 [2, 15], P('comp'), may hold values from 0.15 to 0.24
- coupling: float32 [2, 512, 2048], P('comp', 'gx', 'gy'), may hold values from 0.3 to 0.6
- land_temp: float32 [512, 2048], P('gx', 'gy'), may hold values from -6 to 6
- land_mask: int32 [512, 2048], P('gx', 'gy'), may hold values from 0 to 1
- weights: bfloat16 [2, 2048, 128, 128], P('comp', ('gx', 'gy')), may hold values from -0.375 to 0.375
- source_block: int32 [2, 512, 16, 2], P('comp', 'gx', 'gy'), may hold values from 0 to 127
- pattern: int32 [2, 512, 16, 2], P('comp', 'gx', 'gy'), may hold values from 0 to 31
Outputs:
- final_state: float32 [2, 16, 512, 2048], P('comp', None, 'gx', 'gy')
- forcing: float32 [2, 6, 512, 2048], P('comp', None, 'gx', 'gy')
The draws below stay inside these ranges and needn't reach their ends.
Inputs may be any that keep to these rules, and one draw needn't show every extreme that they name: `source_block`: a block number of the same tile. `pattern`: a weight block of the same tile.
All inputs are finite; a program needn't handle non-finite values.
Results may differ from the reference program's by a relative error of at most 0.0023.
The reference program's roundings to bfloat16 on the way count: a program that leaves them out, or rounds other values in their place, can miss the bound.
Values may be sent and summed in bfloat16 or wider, within the bound.
No kernel may reach another device: no remote copies, remote signals or barrier semaphores. Data moves between devices by JAX's collectives and lax.ppermute only.
A program may use at most 128 MiB of HBM per device.

```python
import math
import jax
import jax.numpy as jnp
from jax import lax

LEVELS = 16
SUB = 6
ITERS = 2
SOURCES = 2
PATTERNS = 32
CX = 32
CY = 512
NX = 512
NY = 2048
TILES = 64
N_GX = 16
N_GY = 4


def draw_state(key, part):
    key = jax.random.fold_in(key, 11)
    shape = (2, LEVELS, NX, NY)
    rows = jnp.arange(NX, dtype=jnp.int32)
    offset = jnp.where(rows // CX % 2 == 0, 5.0, -2.0).astype(jnp.float32)
    noise = jnp.clip(jax.random.normal(key, shape, jnp.float32), -2.5, 2.5)
    values = offset[None, None, :, None] + noise
    return values.astype(jnp.float32)


def draw_land_mask(key, part):
    key = jax.random.fold_in(key, 23)
    side_key, base_key, cell_key = jax.random.split(key, 3)
    side = jax.random.randint(side_key, (), 0, 2, dtype=jnp.int32)
    base = 150 + 300 * side + jax.random.randint(base_key, (), 0, 100, dtype=jnp.int32)
    rows = jnp.arange(NX, dtype=jnp.int32)
    threshold = base + 400 * rows // max(NX - 1, 1)
    drawn = jax.random.randint(cell_key, (NX, NY), 0, 1000, dtype=jnp.int32)
    inner = (drawn < threshold[:, None]).astype(jnp.int32)
    local_row = rows % CX
    on_edge = (local_row == 0) | (local_row == CX - 1)
    even_tile = (rows // CX % 2 == 0).astype(jnp.int32)
    edge_value = jnp.broadcast_to(even_tile[:, None], (NX, NY))
    return jnp.where(on_edge[:, None], edge_value, inner).astype(jnp.int32)


def with_ends(values, key, smallest, top_value):
    longest = values.shape.index(max(values.shape))
    spots = []
    for shift in (0, 1):
        where = [jax.random.randint(jax.random.fold_in(key, axis), (), 0, length) for axis, length in enumerate(values.shape)]
        where[longest] = (where[longest] + shift) % values.shape[longest]
        spots.append(tuple(where))
    return values.at[spots[0]].set(smallest).at[spots[1]].set(top_value)


def steps_of(own_key, dims, pieces, smallest, high):
    level = 1.0
    for dim, parts in pieces:
        steps = jax.random.uniform(jax.random.fold_in(jax.random.fold_in(own_key, 6), dim), (parts,), jnp.float32, smallest / len(pieces), high / len(pieces))
        level = level * jnp.repeat(jnp.exp(steps), dims[dim] // parts).reshape((-1,) + (1,) * (len(dims) - 1 - dim))
    return level


def normal_values(key, dims, width, limit, cuts=(), held_as=jnp.bfloat16):
    values = width * jax.random.normal(key, dims, jnp.float32)
    if cuts:
        values = values * steps_of(key, dims, cuts, -0.22, 0.18)
    return jnp.clip(values, -limit, limit).astype(held_as)


def setup_inputs(seed: int = 0) -> dict:
    splits = jax.random.split(jax.random.key(seed), 11)
    return {
        "state": draw_state(jax.random.fold_in(splits[10], 71), 0),
        "guess": jnp.clip(jax.random.uniform(splits[1], (2, SUB, NX, NY), jnp.float32, -5.0, 5.0) * steps_of(splits[1], (2, SUB, NX, NY), ((0, 2), (2, 16), (3, 4)), -0.4, 0.0), -5.0, 5.0).astype(jnp.bfloat16),
        "diffusion": jnp.clip(jnp.exp(math.log(0.22) - 1.48160452 * jax.random.uniform(splits[2], (2, LEVELS), jnp.float32) ** steps_of(splits[2], (2, LEVELS), ((0, 2),), -0.2, 0.2)), 0.05, 0.22),
        "mixing": jnp.clip(0.15 + 0.08999999 * jax.random.uniform(splits[3], (2, LEVELS - 1), jnp.float32) ** steps_of(splits[3], (2, LEVELS - 1), ((0, 2),), -0.2, 0.2), 0.15, 0.24),
        "coupling": jnp.clip(jnp.exp(math.log(0.6) - 0.6931472 * jax.random.uniform(splits[4], (2, NX, NY), jnp.float32) ** steps_of(splits[4], (2, NX, NY), ((0, 2), (1, 16), (2, 4)), -0.2, 0.2)), 0.3, 0.6),
        "land_temp": normal_values(splits[5], (NX, NY), 1.0, 6.0, ((0, 16), (1, 4)), jnp.float32),
        "land_mask": draw_land_mask(jax.random.fold_in(splits[10], 71), 0),
        "weights": normal_values(splits[7], (2, TILES * PATTERNS, 128, 128), (128 * SOURCES) ** -0.5, 0.375, ((0, 2), (1, 64))),
        "source_block": with_ends(jax.random.randint(splits[8], (2, NX, NY // 128, SOURCES), 0, CX * (CY // 128)), jax.random.fold_in(splits[8], 1), 0, (CX * (CY // 128)) - 1).astype(jnp.int32),
        "pattern": with_ends(jax.random.randint(splits[9], (2, NX, NY // 128, SOURCES), 0, PATTERNS), jax.random.fold_in(splits[9], 1), 0, PATTERNS - 1).astype(jnp.int32),
    }


def vertical_mix(spread, mixing_row):
    upward = mixing_row[:, None, None] * (spread[1:] - spread[:-1])
    zero_layer = jnp.zeros_like(spread[:1])
    return spread + jnp.concatenate([upward, zero_layer], 0) - jnp.concatenate([zero_layer, upward], 0)


def diffuse(current, diffusion_row, mixing_row):
    padded = jnp.pad(current, ((0, 0), (0, 0), (1, 1)))
    laplace = jnp.roll(current, 1, 1) + jnp.roll(current, -1, 1)
    laplace = laplace + padded[:, :, 2:] + padded[:, :, :-2] - 4.0 * current
    spread = current + diffusion_row[:, None, None] * laplace
    return vertical_mix(spread, mixing_row)


def run_component(start, forcing_series, diffusion_row, mixing_row, exchange_rate, maskf, land_temp, ocean_side):
    current = start
    emitted = []
    for instant in range(SUB):
        mixed = diffuse(current, diffusion_row, mixing_row)
        surface = mixed[0]
        if ocean_side:
            top_level = surface + exchange_rate * maskf * forcing_series[instant]
            emitted.append(maskf * top_level)
        else:
            below = maskf * forcing_series[instant] + (1.0 - maskf) * land_temp
            flux_value = exchange_rate * (surface - below)
            top_level = surface - flux_value
            emitted.append(flux_value)
        current = jnp.concatenate([top_level[None], mixed[1:]], 0)
    return current, jnp.stack(emitted).astype(jnp.bfloat16)


def to_tiles(array, last):
    blocks_row = CY // 128
    shaped = array.reshape(N_GX, CX, N_GY, blocks_row, last)
    return shaped.transpose(0, 2, 1, 3, 4).reshape(N_GX * N_GY, CX * blocks_row, last)


def regrid(received, table, source_block, pattern):
    blocks_row = CY // 128
    tiles = received.reshape(SUB, N_GX, CX, N_GY, blocks_row, 128)
    tiles = tiles.transpose(1, 3, 0, 2, 4, 5).reshape(N_GX * N_GY, SUB, CX * blocks_row, 128)
    source_idx = to_tiles(source_block, SOURCES)
    pattern_idx = to_tiles(pattern, SOURCES)
    tables = table.reshape(N_GX * N_GY, PATTERNS, 128, 128)

    def per_tile(members):
        tile_series, source_row, pattern_row, tile_table = members
        picked = tile_series[:, source_row].astype(jnp.float32)
        chosen = tile_table[pattern_row].astype(jnp.float32)
        return jnp.einsum('sbki,bkij->sbj', picked, chosen)

    result = lax.map(per_tile, (tiles, source_idx, pattern_idx, tables))
    result = result.reshape(N_GX, N_GY, SUB, CX, blocks_row, 128)
    return result.transpose(2, 0, 3, 1, 4, 5).reshape(SUB, NX, NY)


def conserve(received, regridded, maskf, wet):
    source_sum = jnp.sum(maskf * received.astype(jnp.float32), axis=(1, 2))
    target_sum = jnp.sum(maskf * regridded, axis=(1, 2))
    return regridded + maskf * ((source_sum - target_sum) / wet)[:, None, None]


def reference(state, guess, diffusion, mixing, coupling, land_temp, land_mask, weights, source_block, pattern):
    maskf = land_mask.astype(jnp.float32)
    wet = jnp.sum(maskf)
    forcing = guess.astype(jnp.float32)
    final_atmos = state[0]
    final_ocean = state[1]
    for iteration in range(ITERS):
        final_atmos, atmos_series = run_component(state[0], forcing[0], diffusion[0], mixing[0], coupling[0], maskf, land_temp, False)
        final_ocean, ocean_series = run_component(state[1], forcing[1], diffusion[1], mixing[1], coupling[1], maskf, land_temp, True)
        into_atmos = regrid(ocean_series, weights[0], source_block[0], pattern[0])
        into_ocean = regrid(atmos_series, weights[1], source_block[1], pattern[1])
        forcing = jnp.stack([conserve(ocean_series, into_atmos, maskf, wet), conserve(atmos_series, into_ocean, maskf, wet)])
    return jnp.stack([final_atmos, final_ocean]), forcing
```

```python
import jax
import jax.numpy as jnp
from jax import lax
from jax.experimental import pallas as pl
from jax.experimental.pallas import tpu as pltpu
from jax.sharding import PartitionSpec as P

F32 = jnp.float32
BF16 = jnp.bfloat16
SUB = 6
LEVELS = 16
CX = 32
CY = 512
LANES = 128
OWN_TILES = CY // LANES
COLS = CY + LANES
ROWS = CX + 32
BAND = CX + 16
PATTERNS = 32
BLOCKS = CX * OWN_TILES
VMEM_LIMIT = 48 * 1024 * 1024

N_FIELDS = LEVELS + 3 + SUB - 1
AT_COUPLING, AT_LAND, AT_MASK, AT_GUESS = LEVELS, LEVELS + 1, LEVELS + 2, LEVELS + 3
PACK_LANES = 256

VM = pl.BlockSpec(memory_space=pltpu.VMEM)
SM = pl.BlockSpec(memory_space=pltpu.SMEM)


def shape(*dims, dtype=F32):
    return jax.ShapeDtypeStruct(dims, dtype)


def call(body, outs, scratch, ins, out_specs=None, **kw):
    return pl.pallas_call(
        body,
        out_shape=outs,
        in_specs=ins,
        out_specs=[VM] * len(outs) if out_specs is None else out_specs,
        scratch_shapes=scratch,
        compiler_params=pltpu.CompilerParams(vmem_limit_bytes=VMEM_LIMIT),
        **kw,
    )


def iotas():
    row = lax.broadcasted_iota(jnp.int32, (8, LANES), 0)
    lane = lax.broadcasted_iota(jnp.int32, (8, LANES), 1)
    return row, lane


def roll_lanes(x, shift):
    shift %= LANES
    return x if shift == 0 else pltpu.roll(x, shift, 1)


def pack_columns(fields, one, three, even):
    _, lane = iotas()
    groups = PACK_LANES // LANES if len(fields) > 16 else 1
    for tile in range(6):
        for g in range(groups):
            left = jnp.zeros((8, LANES), F32)
            right = jnp.zeros((8, LANES), F32)
            for f in range(g * 16, min(len(fields), g * 16 + 16)):
                at = (f % 16) * 8
                head, tail = fields[f](tile)
                left = jnp.where((lane >= at) & (lane < at + 8), roll_lanes(head, at), left)
                right = jnp.where((lane >= at) & (lane < at + 8), roll_lanes(tail, at + 8), right)
            span = (slice(tile * 8, tile * 8 + 8), slice(g * LANES, (g + 1) * LANES))
            one[span] = jnp.where(even, right, left)
            three[span] = jnp.where(even, left, right)


def side_halos(one, three, even, first, last, tile, g):
    span = (slice(tile * 8, tile * 8 + 8), slice(g * LANES, (g + 1) * LANES))
    a, b = one[span], three[span]
    right = jnp.where(last, 0.0, jnp.where(even, a, b))
    left = jnp.where(first, 0.0, jnp.where(even, b, a))
    return right, left


def side_tile(right, left, f, lane):
    at = (f % 16) * 8
    return jnp.where(
        lane < 6,
        roll_lanes(right, -at),
        jnp.where(lane >= LANES - 6, roll_lanes(left, LANES - 8 - at), 0.0),
    )


def place_sides(dst_of, fields, one, three, even, first, last):
    _, lane = iotas()
    for tile in range(6):
        packs = {}
        for f in fields:
            g = f // 16
            if g not in packs:
                packs[g] = side_halos(one, three, even, first, last, tile, g)
            dst_of(f, tile, side_tile(*packs[g], f, lane))


def place_rows(dst, own, upper, lower):
    dst[8:16, :CY] = upper
    dst[16 : 16 + CX, :CY] = own
    dst[16 + CX : 24 + CX, :CY] = lower


def zero_pads(ref, count):
    for l in range(count):
        ref[l, 0:8, :] = jnp.zeros((8, COLS), F32)
        ref[l, ROWS - 8 : ROWS, :] = jnp.zeros((8, COLS), F32)


def position():
    gy = lax.axis_index("gy")
    return gy % 2 == 0, gy == 0, gy == lax.axis_size("gy") - 1


class Strip:
    def __init__(self, r, first, last):
        self.r = r
        row, lane = iotas()
        self.row_first, self.row_last = row == 0, row == 7
        self.lane_first, self.lane_last = lane == 0, lane == LANES - 1
        self.inside = ((lane < 6) & jnp.logical_not(last)) | (
            (lane >= LANES - 6) & jnp.logical_not(first)
        )

    def load(self, ref, l, shift=0):
        rows = pl.ds(self.r * 8 + shift, 8)
        return [ref[l, rows, k * LANES : (k + 1) * LANES] for k in range(OWN_TILES + 1)]

    def spread(self, ref, l, d):
        x = self.load(ref, l)
        above = self.load(ref, l, -8)
        below = self.load(ref, l, 8)
        out = []
        n = len(x)
        for k in range(n):
            c = x[k]
            up = pltpu.roll(jnp.where(self.row_last, above[k], c), 1, 0)
            down = pltpu.roll(jnp.where(self.row_first, below[k], c), 7, 0)
            left = pltpu.roll(jnp.where(self.lane_last, x[k - 1], c), 1, 1)
            right = pltpu.roll(jnp.where(self.lane_first, x[(k + 1) % n], c), LANES - 1, 1)
            out.append(c + d * (((up + down) + (left + right)) - 4.0 * c))
        return out

    def store(self, ref, l, values):
        rows = pl.ds(self.r * 8, 8)
        for k, v in enumerate(values):
            if k == OWN_TILES:
                v = jnp.where(self.inside, v, 0.0)
            ref[l, rows, k * LANES : (k + 1) * LANES] = v

    def save(self, ref, l, values):
        rows = pl.ds(self.r * 8 - 8, 8)
        for k, v in enumerate(values):
            ref[l, rows, k * LANES : (k + 1) * LANES] = v

    def recall(self, ref, l):
        return self.load(ref, l, -8)


def flux_between(mix, lower, upper):
    return [mix * (a - b) for a, b in zip(lower, upper)]


def added(a, b):
    return [x + y for x, y in zip(a, b)]


def less(a, b):
    return [x - y for x, y in zip(a, b)]


def surface(v, f, c, m, ml, ocean):
    new, emitted = [], []
    for vk, fk, ck, mk, lk in zip(v, f, c, m, ml):
        mf = mk * fk
        flux = ck * (vk - (mf + lk))
        warmed = vk + ck * mf
        new.append(jnp.where(ocean, warmed, vk - flux))
        emitted.append(jnp.where(ocean, mk * warmed, flux))
    return new, emitted


def strips(t):
    return (1, 7) if t < SUB - 1 else (2, 6)


def write_series(series, emitted):
    for t in range(SUB):
        for half in range(CX // 16):
            rows = slice(8 + half * 16, 24 + half * 16)
            series[t, half * 16 : half * 16 + 16, :] = emitted[t, rows, :CY].astype(BF16)


def pack_first(state, guess, coupling, land, mask, upper, lower, one, three):
    even, _, _ = position()

    def field(f):
        def of(tile):
            if tile == 0:
                block = upper.at[f]
                rows = slice(0, 8)
            elif tile == 5:
                block = lower.at[f]
                rows = slice(0, 8)
            else:
                rows = slice(tile * 8 - 8, tile * 8)
                if f < LEVELS:
                    block = state.at[f]
                elif f == AT_COUPLING:
                    block = coupling
                elif f == AT_LAND:
                    block = land
                elif f == AT_MASK:
                    block = mask
                else:
                    block = guess.at[f - AT_GUESS]
            if f >= AT_GUESS and 0 < tile < 5:
                base = (tile - 1) // 2 * 16
                part = slice((tile - 1) % 2 * 8, (tile - 1) % 2 * 8 + 8)
                head = block[base : base + 16, :LANES].astype(F32)[part]
                tail = block[base : base + 16, CY - LANES :].astype(F32)[part]
                return head, tail
            head, tail = block[rows, :LANES], block[rows, CY - LANES :]
            return head.astype(F32), tail.astype(F32)

        return of

    pack_columns([field(f) for f in range(N_FIELDS)], one, three, even)


CONE = SUB + 1


def first_cone(
    diff, mix, state, guess, coupling, land, mask, upper, lower, one, three,
    series, hd, ud, hs, us, fixed,
    s0, s1, g, emitted,
):
    even, first, last = position()
    ocean = lax.axis_index("comp") == 1
    zero_pads(s0, CONE)
    zero_pads(s1, CONE - 1)
    for l in range(CONE):
        place_rows(s0.at[l], state[l], upper[l], lower[l])

    def rows_of(ref, k, f, own):
        ref[k, 0:8, :CY] = upper[f]
        ref[k, 8 : 8 + CX, :CY] = own
        ref[k, 8 + CX : 16 + CX, :CY] = lower[f]

    rows_of(fixed, 0, AT_COUPLING, coupling[...])
    rows_of(fixed, 1, AT_MASK, mask[...].astype(F32))
    rows_of(fixed, 2, AT_LAND, land[...])
    for t in range(SUB - 1):
        rows_of(g, t, AT_GUESS + t, guess[t].astype(F32))
    g[SUB - 1, 8 : 8 + CX, :CY] = guess[SUB - 1].astype(F32)

    side = slice(CY, COLS)
    slot = {AT_COUPLING: 0, AT_MASK: 1, AT_LAND: 2}

    def put(f, tile, value):
        rows = slice(tile * 8, tile * 8 + 8)
        if f < LEVELS:
            s0[f, tile * 8 + 8 : tile * 8 + 16, side] = value
        elif f < AT_GUESS:
            fixed[slot[f], rows, side] = value
        else:
            g[f - AT_GUESS, rows, side] = value

    fields = [*range(CONE), *range(LEVELS, N_FIELDS)]
    place_sides(put, fields, one, three, even, first, last)
    g[SUB - 1, :, side] = jnp.zeros((BAND, LANES), F32)
    fixed[2] = (1.0 - fixed[1]) * fixed[2]

    for t in range(SUB):
        src, dst = (s0, s1) if t % 2 == 0 else (s1, s0)

        @pl.loop(*strips(t))
        def _(r, t=t, src=src, dst=dst):
            strip = Strip(r, first, last)
            h = strip.spread(src, 0, diff[0])
            u_prev = None
            for l in range(SUB - t):
                h_next = strip.spread(src, l + 1, diff[l + 1])
                u = flux_between(mix[l], h_next, h)
                v = added(h, u)
                if l == t and t < 3:
                    strip.save(us, t, v)
                    strip.save(hs, t, h)
                if u_prev is not None:
                    v = less(v, u_prev)
                if l == 0:
                    c, m, ml = (strip.recall(fixed, i) for i in range(3))
                    v, e = surface(v, strip.recall(g, t), c, m, ml, ocean)
                    strip.save(emitted, t, e[:OWN_TILES])
                if t < SUB - 1:
                    strip.store(dst, l, v)
                h, u_prev = h_next, u
            strip.save(hd, t, h)
            strip.save(ud, t, u_prev)

    write_series(series, emitted)


def first_rest(
    diff, mix, state, upper, lower, one, three, hd, ud,
    final, hs, us,
    s0, s1,
):
    even, first, last = position()
    zero_pads(s0, LEVELS)
    zero_pads(s1, LEVELS)
    for l in range(CONE, LEVELS):
        place_rows(s0.at[l], state[l], upper[l], lower[l])

    def put(f, tile, value):
        s0[f, tile * 8 + 8 : tile * 8 + 16, CY:COLS] = value

    place_sides(put, list(range(CONE, LEVELS)), one, three, even, first, last)

    for t in range(SUB):
        src, dst = (s0, s1) if t % 2 == 0 else (s1, s0)

        @pl.loop(*strips(t))
        def _(r, t=t, src=src, dst=dst):
            strip = Strip(r, first, last)
            h = strip.recall(hd, t)
            u_prev = strip.recall(ud, t)
            for l in range(SUB - t, LEVELS):
                if l < LEVELS - 1:
                    h_next = strip.spread(src, l + 1, diff[l + 1])
                    u = flux_between(mix[l], h_next, h)
                    v = added(h, u)
                else:
                    h_next = u = None
                    v = h
                if l == t and t >= 3:
                    strip.save(us, t - 3, v)
                    strip.save(hs, t - 3, h)
                v = less(v, u_prev)
                if t < SUB - 1:
                    strip.store(dst, l, v)
                elif l >= SUB:
                    rows = pl.ds(r * 8 - 16, 8)
                    for k in range(OWN_TILES):
                        final[l, rows, k * LANES : (k + 1) * LANES] = v[k]
                h, u_prev = h_next, u


def regrid(
    src, pat, received, weights, mask,
    out, top, bottom, gap,
    x, y,
):
    partial = [jnp.zeros((8, LANES), F32) for _ in range(SUB)]
    wet = jnp.zeros((8, LANES), F32)
    for half in range(CX // 16):
        for j in range(OWN_TILES):
            cols = slice(j * LANES, (j + 1) * LANES)
            m16 = mask[half * 16 : half * 16 + 16, cols].astype(F32)
            wet += m16[:8] + m16[8:]
            for t in range(SUB):
                v16 = received[t, half * 16 : half * 16 + 16, cols].astype(F32)
                partial[t] += m16[:8] * v16[:8] + m16[8:] * v16[8:]
                for part in range(2):
                    row = half * 16 + part * 8
                    start = (row * OWN_TILES + j) * 8 + t
                    x[pl.ds(start, 8, stride=OWN_TILES * 8), :] = v16[part * 8 : part * 8 + 8]

    @pl.loop(0, BLOCKS, unroll=8)
    def _(q):
        a = [x[pl.ds(pl.multiple_of(src[q, k] * 8, 8), 8), :].astype(BF16) for k in range(2)]
        w = [weights[pat[q, k]] for k in range(2)]
        r = jnp.dot(
            jnp.concatenate(a, 1), jnp.concatenate(w, 0), preferred_element_type=F32
        )
        y[pl.ds(q, 8, stride=BLOCKS), :] = r

    for t in range(SUB):
        for part in range(CX // 8):
            for j in range(OWN_TILES):
                cols = slice(j * LANES, (j + 1) * LANES)
                rows = slice(part * 8, part * 8 + 8)
                v = y[pl.ds(t * BLOCKS + part * 8 * OWN_TILES + j, 8, stride=OWN_TILES), :]
                out[t, rows, cols] = v
                partial[t] -= mask[rows, cols].astype(F32) * v
                if t < SUB - 1:
                    if part == 0:
                        top[t, :, cols] = v
                    if part == CX // 8 - 1:
                        bottom[t, :, cols] = v
    _, lane = iotas()
    total = jnp.zeros((8, LANES), F32)
    for t, value in enumerate([*partial, wet]):
        summed = jnp.sum(value, axis=(0, 1), keepdims=True)
        total = jnp.where(lane == t, summed, total)
    for k in range(gap.shape[0]):
        gap[k] = total[:1]


def pack_second(out, upper, lower, one, three):
    even, _, _ = position()

    def field(t):
        def of(tile):
            if tile == 0:
                block, rows = upper.at[t], slice(0, 8)
            elif tile == 5:
                block, rows = lower.at[t], slice(0, 8)
            else:
                block, rows = out.at[t], slice(tile * 8 - 8, tile * 8)
            return block[rows, :LANES], block[rows, CY - LANES :]

        return of

    pack_columns([field(t) for t in range(SUB - 1)], one, three, even)


def gap_means(gap):
    total = jnp.sum(gap[...], axis=0)
    lane = lax.broadcasted_iota(jnp.int32, (1, LANES), 1)
    wet = jnp.sum(jnp.where(lane == SUB, total, 0.0), axis=1, keepdims=True)
    return [
        jnp.sum(jnp.where(lane == t, total, 0.0), axis=1, keepdims=True) / wet for t in range(SUB)
    ]


def second_cone(
    diff, mix, fixed, regridded, upper, lower, one, three, gap, hs, hd, us,
    series, final0, hx, ux,
    s0, s1, g, emitted,
):
    even, first, last = position()
    ocean = lax.axis_index("comp") == 1
    zero_pads(s0, 3)
    zero_pads(s1, 3)
    for t in range(SUB):
        if t < SUB - 1:
            g[t, 0:8, :CY] = upper[t]
            g[t, 8 + CX : 16 + CX, :CY] = lower[t]
        g[t, 8 : 8 + CX, :CY] = regridded[t]

    def put(f, tile, value):
        g[f, tile * 8 : tile * 8 + 8, CY:COLS] = value

    place_sides(put, list(range(SUB - 1)), one, three, even, first, last)
    g[SUB - 1, :, CY:COLS] = jnp.zeros((BAND, LANES), F32)
    means = [jnp.broadcast_to(v, (8, LANES)) for v in gap_means(gap)]

    for t in range(SUB):
        src, dst = (s0, s1) if t % 2 == 0 else (s1, s0)

        @pl.loop(*strips(t))
        def _(r, t=t, src=src, dst=dst):
            strip = Strip(r, first, last)
            h = strip.spread(src, 0, diff[0]) if t else None
            u_prev = None
            for l in range(min(t, SUB - 1 - t) + 1):
                if l < t:
                    if l + 1 < t:
                        h_next = strip.spread(src, l + 1, diff[l + 1])
                    else:
                        h_next = strip.recall(hd if t == 3 else hs, t)
                    u = flux_between(mix[l], h_next, h)
                    v = added(h, u)
                else:
                    v = strip.recall(us, t)
                if u_prev is not None:
                    v = less(v, u_prev)
                if l == 0:
                    c, m, ml = (strip.recall(fixed, i) for i in range(3))
                    f = [a + b * means[t] for a, b in zip(strip.recall(g, t), m)]
                    v, e = surface(v, f, c, m, ml, ocean)
                    strip.save(emitted, t, e[:OWN_TILES])
                    if t == SUB - 1:
                        rows = pl.ds(r * 8 - 16, 8)
                        for k in range(OWN_TILES):
                            final0[rows, k * LANES : (k + 1) * LANES] = v[k]
                if t < SUB - 1:
                    strip.store(dst, l, v)
                if l < t:
                    h, u_prev = h_next, u
            if t >= 3:
                strip.save(hx, t - 3, h)
                strip.save(ux, t - 3, u_prev)

    write_series(series, emitted)


def second_rest(
    diff, mix, hx, ux, hs, us, final0, whole,
    final,
    s0, s1,
):
    del whole
    gy = lax.axis_index("gy")
    first, last = gy == 0, gy == lax.axis_size("gy") - 1
    zero_pads(s0, SUB)
    zero_pads(s1, SUB)
    final[0] = final0[...]
    for t in range(3, SUB):
        src, dst = (s0, s1) if t % 2 == 0 else (s1, s0)

        @pl.loop(*strips(t))
        def _(r, t=t, src=src, dst=dst):
            strip = Strip(r, first, last)
            h = strip.recall(hx, t - 3)
            u_prev = strip.recall(ux, t - 3)
            for l in range(SUB - t, t + 1):
                if l < t:
                    if l + 1 < t:
                        h_next = strip.spread(src, l + 1, diff[l + 1])
                    else:
                        h_next = strip.recall(hs, t - 3)
                    u = flux_between(mix[l], h_next, h)
                    v = added(h, u)
                    h = h_next
                else:
                    u = None
                    v = strip.recall(us, t - 3)
                v = less(v, u_prev)
                u_prev = u
                if t < SUB - 1:
                    strip.store(dst, l, v)
                else:
                    rows = pl.ds(r * 8 - 16, 8)
                    for k in range(OWN_TILES):
                        final[l, rows, k * LANES : (k + 1) * LANES] = v[k]


def finish(regridded, mask, gap, forcing):
    for t, mean in enumerate(gap_means(gap)):
        forcing[t] = regridded[t] + mask[...].astype(F32) * mean


def shifted(value, axis, by):
    n = lax.axis_size(axis)
    return lax.ppermute(value, axis, [(i, (i + by) % n) for i in range(n)])


def paired(value, axis, mask):
    return lax.ppermute(value, axis, [(i, i ^ mask) for i in range(lax.axis_size(axis))])


def per_device(
    state, guess, diffusion, mixing, coupling, land_temp, land_mask, weights, source_block, pattern
):
    state, guess, diff, mix, coupling = state[0], guess[0], diffusion[0], mixing[0], coupling[0]
    weights = weights[0]
    src = source_block[0].reshape(BLOCKS, 2)
    pat = pattern[0].reshape(BLOCKS, 2)
    peers = lax.axis_size("gx") * lax.axis_size("gy")
    band = lambda n: shape(n, BAND, COLS)
    field_buf = lambda n: pltpu.VMEM((n, ROWS, COLS), F32)
    band_buf = lambda n: pltpu.VMEM((n, BAND, COLS), F32)

    def edge(rows):
        return jnp.concatenate(
            [
                state[:, rows],
                coupling[None, rows],
                land_temp[None, rows],
                land_mask[None, rows].astype(F32),
                guess[: SUB - 1, rows].astype(F32),
            ]
        )

    lower = shifted(edge(slice(0, 8)), "gx", -1)
    upper = shifted(edge(slice(CX - 8, CX)), "gx", 1)
    packed = shape(BAND, PACK_LANES)
    one, three = call(pack_first, [packed, packed], [], [VM] * 7)(
        state, guess, coupling, land_temp, land_mask, upper, lower
    )
    one, three = paired(one, "gy", 1), paired(three, "gy", 3)

    series, hd, ud, hs, us, fixed = call(
        first_cone,
        [shape(SUB, CX, CY, dtype=BF16), band(SUB), band(SUB), band(3), band(3), band(3)],
        [field_buf(CONE), field_buf(CONE), band_buf(SUB), band_buf(SUB)],
        [SM, SM] + [VM] * 9,
    )(diff, mix, state, guess, coupling, land_temp, land_mask, upper, lower, one, three)

    def exchange(series):
        received = paired(series, "comp", 1)
        edges = shape(SUB - 1, 8, CY)
        out, top, bottom, gap = call(
            regrid,
            [shape(SUB, CX, CY), edges, edges, shape(peers, 1, LANES)],
            [pltpu.VMEM((BLOCKS * 8, LANES), F32), pltpu.VMEM((BLOCKS * 8, LANES), F32)],
            [SM, SM, VM, VM, VM],
        )(src, pat, received, weights, land_mask)
        return out, top, bottom, gap

    whole, hs_rest, us_rest = call(
        first_rest,
        [shape(LEVELS, CX, CY), band(3), band(3)],
        [field_buf(LEVELS), field_buf(LEVELS)],
        [SM, SM] + [VM] * 7,
    )(diff, mix, state, upper, lower, one, three, hd, ud)

    out, top, bottom, gap = exchange(series)
    lower, upper = shifted(top, "gx", -1), shifted(bottom, "gx", 1)
    gap = lax.all_to_all(gap, ("gx", "gy"), 0, 0)
    packed = shape(BAND, LANES)
    one, three = call(pack_second, [packed, packed], [], [VM] * 3)(out, upper, lower)
    one, three = paired(one, "gy", 1), paired(three, "gy", 3)

    series, final0, hx, ux = call(
        second_cone,
        [shape(SUB, CX, CY, dtype=BF16), shape(CX, CY), band(3), band(3)],
        [field_buf(3), field_buf(3), band_buf(SUB), band_buf(SUB)],
        [SM, SM] + [VM] * 10,
    )(diff, mix, fixed, out, upper, lower, one, three, gap, hs, hd, us)

    (whole,) = call(
        second_rest,
        [shape(LEVELS, CX, CY)],
        [field_buf(SUB), field_buf(SUB)],
        [SM, SM] + [VM] * 5 + [pl.BlockSpec(memory_space=pl.ANY)],
        out_specs=[pl.BlockSpec((SUB, CX, CY), lambda i: (0, 0, 0))],
        grid=(1,),
        input_output_aliases={7: 0},
    )(diff, mix, hx, ux, hs_rest, us_rest, final0, whole)

    out, _, _, gap = exchange(series)
    gap = lax.all_to_all(gap, ("gx", "gy"), 0, 0)
    (forcing,) = call(finish, [shape(SUB, CX, CY)], [], [VM] * 3)(out, land_mask, gap)
    return whole[None], forcing[None]


def solution(mesh):
    placed = (
        P("comp", None, "gx", "gy"),
        P("comp", None, "gx", "gy"),
        P("comp", None),
        P("comp", None),
        P("comp", "gx", "gy"),
        P("gx", "gy"),
        P("gx", "gy"),
        P("comp", ("gx", "gy"), None, None),
        P("comp", "gx", "gy", None),
        P("comp", "gx", "gy", None),
    )
    return jax.shard_map(
        per_device,
        mesh=mesh,
        in_specs=placed,
        out_specs=(P("comp", None, "gx", "gy"), P("comp", None, "gx", "gy")),
        check_vma=False,
    )
```

```python
import jax
import jax.numpy as jnp
from jax import lax
from jax.experimental import pallas as pl
from jax.experimental.pallas import tpu as pltpu
from jax.sharding import PartitionSpec as P

F32 = jnp.float32
BF16 = jnp.bfloat16
SUB = 6
LEVELS = 16
CX = 32
CY = 512
LANES = 128
OWN_TILES = CY // LANES
COLS = CY + LANES
ROWS = CX + 32
BAND = CX + 16
PATTERNS = 32
BLOCKS = CX * OWN_TILES
VMEM_LIMIT = 10 * 1024 * 1024

N_FIELDS = LEVELS + 3 + SUB - 1
AT_COUPLING, AT_LAND, AT_MASK, AT_GUESS = LEVELS, LEVELS + 1, LEVELS + 2, LEVELS + 3
PACK_LANES = 256

VM = pl.BlockSpec(memory_space=pltpu.VMEM)
SM = pl.BlockSpec(memory_space=pltpu.SMEM)


def shape(*dims, dtype=F32):
    return jax.ShapeDtypeStruct(dims, dtype)


def call(body, outs, scratch, ins, out_specs=None, **kw):
    return pl.pallas_call(
        body,
        out_shape=outs,
        in_specs=ins,
        out_specs=[VM] * len(outs) if out_specs is None else out_specs,
        scratch_shapes=scratch,
        compiler_params=pltpu.CompilerParams(vmem_limit_bytes=VMEM_LIMIT),
        **kw,
    )


def iotas():
    row = lax.broadcasted_iota(jnp.int32, (8, LANES), 0)
    lane = lax.broadcasted_iota(jnp.int32, (8, LANES), 1)
    return row, lane


def roll_lanes(x, shift):
    shift %= LANES
    return x if shift == 0 else pltpu.roll(x, shift, 1)


def pack_columns(fields, one, three, even):
    _, lane = iotas()
    groups = PACK_LANES // LANES if len(fields) > 16 else 1
    for tile in range(6):
        for g in range(groups):
            left = jnp.zeros((8, LANES), F32)
            right = jnp.zeros((8, LANES), F32)
            for f in range(g * 16, min(len(fields), g * 16 + 16)):
                at = (f % 16) * 8
                head, tail = fields[f](tile)
                left = jnp.where((lane >= at) & (lane < at + 8), roll_lanes(head, at), left)
                right = jnp.where((lane >= at) & (lane < at + 8), roll_lanes(tail, at + 8), right)
            span = (slice(tile * 8, tile * 8 + 8), slice(g * LANES, (g + 1) * LANES))
            one[span] = jnp.where(even, right, left)
            three[span] = jnp.where(even, left, right)


def side_halos(one, three, even, first, last, tile, g):
    span = (slice(tile * 8, tile * 8 + 8), slice(g * LANES, (g + 1) * LANES))
    a, b = one[span], three[span]
    right = jnp.where(last, 0.0, jnp.where(even, a, b))
    left = jnp.where(first, 0.0, jnp.where(even, b, a))
    return right, left


def side_tile(right, left, f, lane):
    at = (f % 16) * 8
    return jnp.where(
        lane < 6,
        roll_lanes(right, -at),
        jnp.where(lane >= LANES - 6, roll_lanes(left, LANES - 8 - at), 0.0),
    )


def place_sides(dst_of, fields, one, three, even, first, last):
    _, lane = iotas()
    for tile in range(6):
        packs = {}
        for f in fields:
            g = f // 16
            if g not in packs:
                packs[g] = side_halos(one, three, even, first, last, tile, g)
            dst_of(f, tile, side_tile(*packs[g], f, lane))


def place_rows(dst, own, upper, lower):
    dst[8:16, :CY] = upper
    dst[16 : 16 + CX, :CY] = own
    dst[16 + CX : 24 + CX, :CY] = lower


def zero_pads(ref, count):
    for l in range(count):
        ref[l, 0:8, :] = jnp.zeros((8, COLS), F32)
        ref[l, ROWS - 8 : ROWS, :] = jnp.zeros((8, COLS), F32)


def position():
    gy = lax.axis_index("gy")
    return gy % 2 == 0, gy == 0, gy == lax.axis_size("gy") - 1


class Strip:
    def __init__(self, r, first, last):
        self.r = r
        row, lane = iotas()
        self.row_first, self.row_last = row == 0, row == 7
        self.lane_first, self.lane_last = lane == 0, lane == LANES - 1
        self.inside = ((lane < 6) & jnp.logical_not(last)) | (
            (lane >= LANES - 6) & jnp.logical_not(first)
        )

    def load(self, ref, l, shift=0):
        rows = pl.ds(self.r * 8 + shift, 8)
        return [ref[l, rows, k * LANES : (k + 1) * LANES] for k in range(OWN_TILES + 1)]

    def spread(self, ref, l, d):
        x = self.load(ref, l)
        above = self.load(ref, l, -8)
        below = self.load(ref, l, 8)
        out = []
        n = len(x)
        for k in range(n):
            c = x[k]
            up = pltpu.roll(jnp.where(self.row_last, above[k], c), 1, 0)
            down = pltpu.roll(jnp.where(self.row_first, below[k], c), 7, 0)
            left = pltpu.roll(jnp.where(self.lane_last, x[k - 1], c), 1, 1)
            right = pltpu.roll(jnp.where(self.lane_first, x[(k + 1) % n], c), LANES - 1, 1)
            out.append(c + d * (((up + down) + (left + right)) - 4.0 * c))
        return out

    def store(self, ref, l, values):
        rows = pl.ds(self.r * 8, 8)
        for k, v in enumerate(values):
            if k == OWN_TILES:
                v = jnp.where(self.inside, v, 0.0)
            ref[l, rows, k * LANES : (k + 1) * LANES] = v

    def save(self, ref, l, values):
        rows = pl.ds(self.r * 8 - 8, 8)
        for k, v in enumerate(values):
            ref[l, rows, k * LANES : (k + 1) * LANES] = v

    def recall(self, ref, l):
        return self.load(ref, l, -8)


def flux_between(mix, lower, upper):
    return [mix * (a - b) for a, b in zip(lower, upper)]


def added(a, b):
    return [x + y for x, y in zip(a, b)]


def less(a, b):
    return [x - y for x, y in zip(a, b)]


def surface(v, f, c, m, ml, ocean):
    new, emitted = [], []
    for vk, fk, ck, mk, lk in zip(v, f, c, m, ml):
        mf = mk * fk
        flux = ck * (vk - (mf + lk))
        warmed = vk + ck * mf
        new.append(jnp.where(ocean, warmed, vk - flux))
        emitted.append(jnp.where(ocean, mk * warmed, flux))
    return new, emitted


def strips(t):
    return (1, 7) if t < SUB - 1 else (2, 6)


def write_series(series, emitted):
    for t in range(SUB):
        for half in range(CX // 16):
            rows = slice(8 + half * 16, 24 + half * 16)
            series[t, half * 16 : half * 16 + 16, :] = emitted[t, rows, :CY].astype(BF16)


def pack_first(state, guess, coupling, land, mask, upper, lower, one, three):
    even, _, _ = position()

    def field(f):
        def of(tile):
            if tile == 0:
                block = upper.at[f]
                rows = slice(0, 8)
            elif tile == 5:
                block = lower.at[f]
                rows = slice(0, 8)
            else:
                rows = slice(tile * 8 - 8, tile * 8)
                if f < LEVELS:
                    block = state.at[f]
                elif f == AT_COUPLING:
                    block = coupling
                elif f == AT_LAND:
                    block = land
                elif f == AT_MASK:
                    block = mask
                else:
                    block = guess.at[f - AT_GUESS]
            if f >= AT_GUESS and 0 < tile < 5:
                base = (tile - 1) // 2 * 16
                part = slice((tile - 1) % 2 * 8, (tile - 1) % 2 * 8 + 8)
                head = block[base : base + 16, :LANES].astype(F32)[part]
                tail = block[base : base + 16, CY - LANES :].astype(F32)[part]
                return head, tail
            head, tail = block[rows, :LANES], block[rows, CY - LANES :]
            return head.astype(F32), tail.astype(F32)

        return of

    pack_columns([field(f) for f in range(N_FIELDS)], one, three, even)


CONE = SUB + 1


def first_cone(
    diff, mix, state, guess, coupling, land, mask, upper, lower, one, three,
    series, hd, ud, hs, us, fixed,
    s0, s1, g, emitted,
):
    even, first, last = position()
    ocean = lax.axis_index("comp") == 1
    zero_pads(s0, CONE)
    zero_pads(s1, CONE - 1)
    for l in range(CONE):
        place_rows(s0.at[l], state[l], upper[l], lower[l])

    def rows_of(ref, k, f, own):
        ref[k, 0:8, :CY] = upper[f]
        ref[k, 8 : 8 + CX, :CY] = own
        ref[k, 8 + CX : 16 + CX, :CY] = lower[f]

    rows_of(fixed, 0, AT_COUPLING, coupling[...])
    rows_of(fixed, 1, AT_MASK, mask[...].astype(F32))
    rows_of(fixed, 2, AT_LAND, land[...])
    for t in range(SUB - 1):
        rows_of(g, t, AT_GUESS + t, guess[t].astype(F32))
    g[SUB - 1, 8 : 8 + CX, :CY] = guess[SUB - 1].astype(F32)

    side = slice(CY, COLS)
    slot = {AT_COUPLING: 0, AT_MASK: 1, AT_LAND: 2}

    def put(f, tile, value):
        rows = slice(tile * 8, tile * 8 + 8)
        if f < LEVELS:
            s0[f, tile * 8 + 8 : tile * 8 + 16, side] = value
        elif f < AT_GUESS:
            fixed[slot[f], rows, side] = value
        else:
            g[f - AT_GUESS, rows, side] = value

    fields = [*range(CONE), *range(LEVELS, N_FIELDS)]
    place_sides(put, fields, one, three, even, first, last)
    g[SUB - 1, :, side] = jnp.zeros((BAND, LANES), F32)
    fixed[2] = (1.0 - fixed[1]) * fixed[2]

    for t in range(SUB):
        src, dst = (s0, s1) if t % 2 == 0 else (s1, s0)

        @pl.loop(*strips(t))
        def _(r, t=t, src=src, dst=dst):
            strip = Strip(r, first, last)
            h = strip.spread(src, 0, diff[0])
            u_prev = None
            for l in range(SUB - t):
                h_next = strip.spread(src, l + 1, diff[l + 1])
                u = flux_between(mix[l], h_next, h)
                v = added(h, u)
                if l == t and t < 3:
                    strip.save(us, t, v)
                    strip.save(hs, t, h)
                if u_prev is not None:
                    v = less(v, u_prev)
                if l == 0:
                    c, m, ml = (strip.recall(fixed, i) for i in range(3))
                    v, e = surface(v, strip.recall(g, t), c, m, ml, ocean)
                    strip.save(emitted, t, e[:OWN_TILES])
                if t < SUB - 1:
                    strip.store(dst, l, v)
                h, u_prev = h_next, u
            strip.save(hd, t, h)
            strip.save(ud, t, u_prev)

    write_series(series, emitted)


def first_rest(
    diff, mix, state, upper, lower, one, three, hd, ud,
    final, hs, us, token,
    s0, s1,
):
    token[...] = jnp.zeros_like(token)
    even, first, last = position()
    zero_pads(s0, LEVELS)
    zero_pads(s1, LEVELS)
    for l in range(CONE, LEVELS):
        place_rows(s0.at[l], state[l], upper[l], lower[l])

    def put(f, tile, value):
        s0[f, tile * 8 + 8 : tile * 8 + 16, CY:COLS] = value

    place_sides(put, list(range(CONE, LEVELS)), one, three, even, first, last)

    for t in range(SUB):
        src, dst = (s0, s1) if t % 2 == 0 else (s1, s0)

        @pl.loop(*strips(t))
        def _(r, t=t, src=src, dst=dst):
            strip = Strip(r, first, last)
            h = strip.recall(hd, t)
            u_prev = strip.recall(ud, t)
            for l in range(SUB - t, LEVELS):
                if l < LEVELS - 1:
                    h_next = strip.spread(src, l + 1, diff[l + 1])
                    u = flux_between(mix[l], h_next, h)
                    v = added(h, u)
                else:
                    h_next = u = None
                    v = h
                if l == t and t >= 3:
                    strip.save(us, t - 3, v)
                    strip.save(hs, t - 3, h)
                v = less(v, u_prev)
                if t < SUB - 1:
                    strip.store(dst, l, v)
                elif l >= SUB:
                    rows = pl.ds(r * 8 - 16, 8)
                    for k in range(OWN_TILES):
                        final[l, rows, k * LANES : (k + 1) * LANES] = v[k]
                h, u_prev = h_next, u


def regrid(
    src, pat, received, weights, mask, before,
    out, top, bottom, gap,
    x, y,
):
    del before
    partial = [jnp.zeros((8, LANES), F32) for _ in range(SUB)]
    wet = jnp.zeros((8, LANES), F32)
    for half in range(CX // 16):
        for j in range(OWN_TILES):
            cols = slice(j * LANES, (j + 1) * LANES)
            m16 = mask[half * 16 : half * 16 + 16, cols].astype(F32)
            wet += m16[:8] + m16[8:]
            for t in range(SUB):
                v16 = received[t, half * 16 : half * 16 + 16, cols].astype(F32)
                partial[t] += m16[:8] * v16[:8] + m16[8:] * v16[8:]
                for part in range(2):
                    row = half * 16 + part * 8
                    start = (row * OWN_TILES + j) * 8 + t
                    x[pl.ds(start, 8, stride=OWN_TILES * 8), :] = v16[part * 8 : part * 8 + 8]

    @pl.loop(0, BLOCKS, unroll=8)
    def _(q):
        a = [x[pl.ds(pl.multiple_of(src[q, k] * 8, 8), 8), :].astype(BF16) for k in range(2)]
        w = [weights[pat[q, k]] for k in range(2)]
        r = jnp.dot(
            jnp.concatenate(a, 1), jnp.concatenate(w, 0), preferred_element_type=F32
        )
        y[pl.ds(q, 8, stride=BLOCKS), :] = r

    for t in range(SUB):
        for part in range(CX // 8):
            for j in range(OWN_TILES):
                cols = slice(j * LANES, (j + 1) * LANES)
                rows = slice(part * 8, part * 8 + 8)
                v = y[pl.ds(t * BLOCKS + part * 8 * OWN_TILES + j, 8, stride=OWN_TILES), :]
                out[t, rows, cols] = v
                partial[t] -= mask[rows, cols].astype(F32) * v
                if t < SUB - 1:
                    if part == 0:
                        top[t, :, cols] = v
                    if part == CX // 8 - 1:
                        bottom[t, :, cols] = v
    _, lane = iotas()
    total = jnp.zeros((8, LANES), F32)
    for t, value in enumerate([*partial, wet]):
        summed = jnp.sum(value, axis=(0, 1), keepdims=True)
        total = jnp.where(lane == t, summed, total)
    for k in range(gap.shape[0]):
        gap[k] = total[:1]


def pack_second(out, upper, lower, one, three):
    even, _, _ = position()

    def field(t):
        def of(tile):
            if tile == 0:
                block, rows = upper.at[t], slice(0, 8)
            elif tile == 5:
                block, rows = lower.at[t], slice(0, 8)
            else:
                block, rows = out.at[t], slice(tile * 8 - 8, tile * 8)
            return block[rows, :LANES], block[rows, CY - LANES :]

        return of

    pack_columns([field(t) for t in range(SUB - 1)], one, three, even)


def gap_means(gap):
    total = jnp.sum(gap[...], axis=0)
    lane = lax.broadcasted_iota(jnp.int32, (1, LANES), 1)
    wet = jnp.sum(jnp.where(lane == SUB, total, 0.0), axis=1, keepdims=True)
    return [
        jnp.sum(jnp.where(lane == t, total, 0.0), axis=1, keepdims=True) / wet for t in range(SUB)
    ]


def second_cone(
    diff, mix, fixed, regridded, upper, lower, one, three, gap, hs, hd, us,
    series, final0, hx, ux,
    s0, s1, g, emitted,
):
    even, first, last = position()
    ocean = lax.axis_index("comp") == 1
    zero_pads(s0, 3)
    zero_pads(s1, 3)
    for t in range(SUB):
        if t < SUB - 1:
            g[t, 0:8, :CY] = upper[t]
            g[t, 8 + CX : 16 + CX, :CY] = lower[t]
        g[t, 8 : 8 + CX, :CY] = regridded[t]

    def put(f, tile, value):
        g[f, tile * 8 : tile * 8 + 8, CY:COLS] = value

    place_sides(put, list(range(SUB - 1)), one, three, even, first, last)
    g[SUB - 1, :, CY:COLS] = jnp.zeros((BAND, LANES), F32)
    means = [jnp.broadcast_to(v, (8, LANES)) for v in gap_means(gap)]

    for t in range(SUB):
        src, dst = (s0, s1) if t % 2 == 0 else (s1, s0)

        @pl.loop(*strips(t))
        def _(r, t=t, src=src, dst=dst):
            strip = Strip(r, first, last)
            h = strip.spread(src, 0, diff[0]) if t else None
            u_prev = None
            for l in range(min(t, SUB - 1 - t) + 1):
                if l < t:
                    if l + 1 < t:
                        h_next = strip.spread(src, l + 1, diff[l + 1])
                    else:
                        h_next = strip.recall(hd if t == 3 else hs, t)
                    u = flux_between(mix[l], h_next, h)
                    v = added(h, u)
                else:
                    v = strip.recall(us, t)
                if u_prev is not None:
                    v = less(v, u_prev)
                if l == 0:
                    c, m, ml = (strip.recall(fixed, i) for i in range(3))
                    f = [a + b * means[t] for a, b in zip(strip.recall(g, t), m)]
                    v, e = surface(v, f, c, m, ml, ocean)
                    strip.save(emitted, t, e[:OWN_TILES])
                    if t == SUB - 1:
                        rows = pl.ds(r * 8 - 16, 8)
                        for k in range(OWN_TILES):
                            final0[rows, k * LANES : (k + 1) * LANES] = v[k]
                if t < SUB - 1:
                    strip.store(dst, l, v)
                if l < t:
                    h, u_prev = h_next, u
            if t >= 3:
                strip.save(hx, t - 3, h)
                strip.save(ux, t - 3, u_prev)

    write_series(series, emitted)


def second_rest(
    diff, mix, hx, ux, hs, us, final0, whole,
    final, token,
    s0, s1,
):
    del whole
    token[...] = jnp.zeros_like(token)
    gy = lax.axis_index("gy")
    first, last = gy == 0, gy == lax.axis_size("gy") - 1
    zero_pads(s0, SUB)
    zero_pads(s1, SUB)
    final[0] = final0[...]
    for t in range(3, SUB):
        src, dst = (s0, s1) if t % 2 == 0 else (s1, s0)

        @pl.loop(*strips(t))
        def _(r, t=t, src=src, dst=dst):
            strip = Strip(r, first, last)
            h = strip.recall(hx, t - 3)
            u_prev = strip.recall(ux, t - 3)
            for l in range(SUB - t, t + 1):
                if l < t:
                    if l + 1 < t:
                        h_next = strip.spread(src, l + 1, diff[l + 1])
                    else:
                        h_next = strip.recall(hs, t - 3)
                    u = flux_between(mix[l], h_next, h)
                    v = added(h, u)
                    h = h_next
                else:
                    u = None
                    v = strip.recall(us, t - 3)
                v = less(v, u_prev)
                u_prev = u
                if t < SUB - 1:
                    strip.store(dst, l, v)
                else:
                    rows = pl.ds(r * 8 - 16, 8)
                    for k in range(OWN_TILES):
                        final[l, rows, k * LANES : (k + 1) * LANES] = v[k]


def finish(regridded, mask, gap, forcing):
    for t, mean in enumerate(gap_means(gap)):
        forcing[t] = regridded[t] + mask[...].astype(F32) * mean


def shifted(value, axis, by):
    n = lax.axis_size(axis)
    return lax.ppermute(value, axis, [(i, (i + by) % n) for i in range(n)])


def paired(value, axis, mask):
    return lax.ppermute(value, axis, [(i, i ^ mask) for i in range(lax.axis_size(axis))])


def per_device(
    state, guess, diffusion, mixing, coupling, land_temp, land_mask, weights, source_block, pattern
):
    state, guess, diff, mix, coupling = state[0], guess[0], diffusion[0], mixing[0], coupling[0]
    weights = weights[0]
    src = source_block[0].reshape(BLOCKS, 2)
    pat = pattern[0].reshape(BLOCKS, 2)
    peers = lax.axis_size("gx") * lax.axis_size("gy")
    band = lambda n: shape(n, BAND, COLS)
    field_buf = lambda n: pltpu.VMEM((n, ROWS, COLS), F32)
    band_buf = lambda n: pltpu.VMEM((n, BAND, COLS), F32)

    def edge(rows):
        return jnp.concatenate(
            [
                state[:, rows],
                coupling[None, rows],
                land_temp[None, rows],
                land_mask[None, rows].astype(F32),
                guess[: SUB - 1, rows].astype(F32),
            ]
        )

    lower = shifted(edge(slice(0, 8)), "gx", -1)
    upper = shifted(edge(slice(CX - 8, CX)), "gx", 1)
    packed = shape(BAND, PACK_LANES)
    one, three = call(pack_first, [packed, packed], [], [VM] * 7)(
        state, guess, coupling, land_temp, land_mask, upper, lower
    )
    one, three = paired(one, "gy", 1), paired(three, "gy", 3)

    series, hd, ud, hs, us, fixed = call(
        first_cone,
        [shape(SUB, CX, CY, dtype=BF16), band(SUB), band(SUB), band(3), band(3), band(3)],
        [field_buf(CONE), field_buf(CONE), band_buf(SUB), band_buf(SUB)],
        [SM, SM] + [VM] * 9,
    )(diff, mix, state, guess, coupling, land_temp, land_mask, upper, lower, one, three)

    def exchange(series, before):
        received = paired(series, "comp", 1)
        edges = shape(SUB - 1, 8, CY)
        out, top, bottom, gap = call(
            regrid,
            [shape(SUB, CX, CY), edges, edges, shape(peers, 1, LANES)],
            [pltpu.VMEM((BLOCKS * 8, LANES), F32), pltpu.VMEM((BLOCKS * 8, LANES), F32)],
            [SM, SM, VM, VM, VM, VM],
        )(src, pat, received, weights, land_mask, before)
        return out, top, bottom, gap

    whole, hs_rest, us_rest, token = call(
        first_rest,
        [shape(LEVELS, CX, CY), band(3), band(3), shape(8, LANES)],
        [field_buf(LEVELS), field_buf(LEVELS)],
        [SM, SM] + [VM] * 7,
    )(diff, mix, state, upper, lower, one, three, hd, ud)

    out, top, bottom, gap = exchange(series, token)
    lower, upper = shifted(top, "gx", -1), shifted(bottom, "gx", 1)
    gap = lax.all_to_all(gap, ("gx", "gy"), 0, 0)
    packed = shape(BAND, LANES)
    one, three = call(pack_second, [packed, packed], [], [VM] * 3)(out, upper, lower)
    one, three = paired(one, "gy", 1), paired(three, "gy", 3)

    series, final0, hx, ux = call(
        second_cone,
        [shape(SUB, CX, CY, dtype=BF16), shape(CX, CY), band(3), band(3)],
        [field_buf(3), field_buf(3), band_buf(SUB), band_buf(SUB)],
        [SM, SM] + [VM] * 10,
    )(diff, mix, fixed, out, upper, lower, one, three, gap, hs, hd, us)

    whole, token = call(
        second_rest,
        [shape(LEVELS, CX, CY), shape(8, LANES)],
        [field_buf(SUB), field_buf(SUB)],
        [SM, SM] + [VM] * 5 + [pl.BlockSpec(memory_space=pl.ANY)],
        out_specs=[pl.BlockSpec((SUB, CX, CY), lambda i: (0, 0, 0)), VM],
        grid=(1,),
        input_output_aliases={7: 0},
    )(diff, mix, hx, ux, hs_rest, us_rest, final0, whole)

    out, _, _, gap = exchange(series, token)
    gap = lax.all_to_all(gap, ("gx", "gy"), 0, 0)
    (forcing,) = call(finish, [shape(SUB, CX, CY)], [], [VM] * 3)(out, land_mask, gap)
    return whole[None], forcing[None]


def solution(mesh):
    placed = (
        P("comp", None, "gx", "gy"),
        P("comp", None, "gx", "gy"),
        P("comp", None),
        P("comp", None),
        P("comp", "gx", "gy"),
        P("gx", "gy"),
        P("gx", "gy"),
        P("comp", ("gx", "gy"), None, None),
        P("comp", "gx", "gy", None),
        P("comp", "gx", "gy", None),
    )
    return jax.shard_map(
        per_device,
        mesh=mesh,
        in_specs=placed,
        out_specs=(P("comp", None, "gx", "gy"), P("comp", None, "gx", "gy")),
        check_vma=False,
    )
```

```python
import jax
import jax.numpy as jnp
from jax import lax
from jax.experimental import pallas as pl
from jax.experimental.pallas import tpu as pltpu
from jax.sharding import PartitionSpec as P

F32 = jnp.float32
BF16 = jnp.bfloat16
SUB = 6
LEVELS = 16
CX = 32
CY = 512
LANES = 128
OWN_TILES = CY // LANES
COLS = CY + LANES
ROWS = CX + 32
BAND = CX + 16
PATTERNS = 32
BLOCKS = CX * OWN_TILES
VMEM_LIMIT = 12 * 1024 * 1024

N_FIELDS = LEVELS + 3 + SUB - 1
AT_COUPLING, AT_LAND, AT_MASK, AT_GUESS = LEVELS, LEVELS + 1, LEVELS + 2, LEVELS + 3
PACK_LANES = 256

VM = pl.BlockSpec(memory_space=pltpu.VMEM)
SM = pl.BlockSpec(memory_space=pltpu.SMEM)
HBM = pl.BlockSpec(memory_space=pltpu.HBM)


def shape(*dims, dtype=F32):
    return jax.ShapeDtypeStruct(dims, dtype)


def call(body, outs, scratch, ins, out_specs=None, **kw):
    return pl.pallas_call(
        body,
        out_shape=outs,
        in_specs=ins,
        out_specs=[VM] * len(outs) if out_specs is None else out_specs,
        scratch_shapes=scratch,
        compiler_params=pltpu.CompilerParams(vmem_limit_bytes=VMEM_LIMIT),
        **kw,
    )


def iotas():
    row = lax.broadcasted_iota(jnp.int32, (8, LANES), 0)
    lane = lax.broadcasted_iota(jnp.int32, (8, LANES), 1)
    return row, lane


def roll_lanes(x, shift):
    shift %= LANES
    return x if shift == 0 else pltpu.roll(x, shift, 1)


def pack_columns(fields, one, three, even):
    _, lane = iotas()
    groups = PACK_LANES // LANES if len(fields) > 16 else 1
    for tile in range(6):
        for g in range(groups):
            left = jnp.zeros((8, LANES), F32)
            right = jnp.zeros((8, LANES), F32)
            for f in range(g * 16, min(len(fields), g * 16 + 16)):
                at = (f % 16) * 8
                head, tail = fields[f](tile)
                left = jnp.where((lane >= at) & (lane < at + 8), roll_lanes(head, at), left)
                right = jnp.where((lane >= at) & (lane < at + 8), roll_lanes(tail, at + 8), right)
            span = (slice(tile * 8, tile * 8 + 8), slice(g * LANES, (g + 1) * LANES))
            one[span] = jnp.where(even, right, left)
            three[span] = jnp.where(even, left, right)


def side_halos(one, three, even, first, last, tile, g):
    span = (slice(tile * 8, tile * 8 + 8), slice(g * LANES, (g + 1) * LANES))
    a, b = one[span], three[span]
    right = jnp.where(last, 0.0, jnp.where(even, a, b))
    left = jnp.where(first, 0.0, jnp.where(even, b, a))
    return right, left


def side_tile(right, left, f, lane):
    at = (f % 16) * 8
    return jnp.where(
        lane < 6,
        roll_lanes(right, -at),
        jnp.where(lane >= LANES - 6, roll_lanes(left, LANES - 8 - at), 0.0),
    )


def place_sides(dst_of, fields, one, three, even, first, last):
    _, lane = iotas()
    for tile in range(6):
        packs = {}
        for f in fields:
            g = f // 16
            if g not in packs:
                packs[g] = side_halos(one, three, even, first, last, tile, g)
            dst_of(f, tile, side_tile(*packs[g], f, lane))


def place_rows(dst, own, upper, lower):
    dst[8:16, :CY] = upper
    dst[16 : 16 + CX, :CY] = own
    dst[16 + CX : 24 + CX, :CY] = lower


def zero_pads(ref, count):
    for l in range(count):
        ref[l, 0:8, :] = jnp.zeros((8, COLS), F32)
        ref[l, ROWS - 8 : ROWS, :] = jnp.zeros((8, COLS), F32)


def position():
    gy = lax.axis_index("gy")
    return gy % 2 == 0, gy == 0, gy == lax.axis_size("gy") - 1


class Strip:
    def __init__(self, r, first, last):
        self.r = r
        row, lane = iotas()
        self.row_first, self.row_last = row == 0, row == 7
        self.lane_first, self.lane_last = lane == 0, lane == LANES - 1
        self.inside = ((lane < 6) & jnp.logical_not(last)) | (
            (lane >= LANES - 6) & jnp.logical_not(first)
        )

    def load(self, ref, l, shift=0):
        rows = slice(self.r * 8 + shift, self.r * 8 + shift + 8)
        return [ref[l, rows, k * LANES : (k + 1) * LANES] for k in range(OWN_TILES + 1)]

    def spread(self, ref, l, d):
        x = self.load(ref, l)
        above = self.load(ref, l, -8)
        below = self.load(ref, l, 8)
        out = []
        n = len(x)
        for k in range(n):
            c = x[k]
            up = pltpu.roll(jnp.where(self.row_last, above[k], c), 1, 0)
            down = pltpu.roll(jnp.where(self.row_first, below[k], c), 7, 0)
            left = pltpu.roll(jnp.where(self.lane_last, x[k - 1], c), 1, 1)
            right = pltpu.roll(jnp.where(self.lane_first, x[(k + 1) % n], c), LANES - 1, 1)
            out.append(c + d * (((up + down) + (left + right)) - 4.0 * c))
        return out

    def store(self, ref, l, values):
        rows = slice(self.r * 8, self.r * 8 + 8)
        for k, v in enumerate(values):
            if k == OWN_TILES:
                v = jnp.where(self.inside, v, 0.0)
            ref[l, rows, k * LANES : (k + 1) * LANES] = v

    def save(self, ref, l, values):
        rows = slice(self.r * 8 - 8, self.r * 8)
        for k, v in enumerate(values):
            ref[l, rows, k * LANES : (k + 1) * LANES] = v

    def recall(self, ref, l):
        return self.load(ref, l, -8)


def flux_between(mix, lower, upper):
    return [mix * (a - b) for a, b in zip(lower, upper)]


def added(a, b):
    return [x + y for x, y in zip(a, b)]


def less(a, b):
    return [x - y for x, y in zip(a, b)]


def surface(v, f, c, m, ml, ocean):
    new, emitted = [], []
    for vk, fk, ck, mk, lk in zip(v, f, c, m, ml):
        mf = mk * fk
        flux = ck * (vk - (mf + lk))
        warmed = vk + ck * mf
        new.append(jnp.where(ocean, warmed, vk - flux))
        emitted.append(jnp.where(ocean, mk * warmed, flux))
    return new, emitted


def strips(t):
    return (1, 7) if t < SUB - 1 else (2, 6)


def write_series(series, emitted):
    for t in range(SUB):
        for half in range(CX // 16):
            rows = slice(8 + half * 16, 24 + half * 16)
            series[t, half * 16 : half * 16 + 16, :] = emitted[t, rows, :CY].astype(BF16)


AUX = 3 + SUB - 1


def aux_slots():
    n = 0
    for a in range(AUX):
        for i in range(SUB - 1 if a < 3 else SUB - 1 - (a - 3)):
            yield a, i, n // 2, n % 2
            n += 1


def first_edges(
    state, guess, coupling, land, mask, table,
    to_lower, to_upper,
    head, tail, ints, short, sems,
):
    del table
    n = 0
    copies = []

    def copy(src, dst):
        nonlocal n
        c = pltpu.make_async_copy(src, dst, sems.at[n])
        c.start()
        copies.append(c)
        n += 1

    for side, msg, buf in ((0, to_lower, head), (1, to_upper, tail)):
        rows = pl.ds(side * (CX - 8), 8)
        copy(state.at[:, rows, :], msg)
        copy(coupling.at[rows, :], buf.at[0])
        copy(land.at[rows, :], buf.at[1])
        copy(mask.at[rows, :], ints.at[side])
        copy(guess.at[pl.ds(0, SUB - 1), pl.ds(side * (CX - 16), 16), :], short.at[side])
    for c in copies:
        c.wait()
    for side, buf in ((0, head), (1, tail)):
        buf[2] = ints[side].astype(F32)
        for t in range(SUB - 1):
            rows16 = short[side, t].astype(F32)
            buf[3 + t] = rows16[8:] if side else rows16[:8]
    for a, i, tile, spare in aux_slots():
        to_lower[tile, 6 + spare : 7 + spare, :] = head[a, i : i + 1, :]
        to_upper[tile, spare : spare + 1, :] = tail[a, 7 - i : 8 - i, :]


def pack_first(
    state, guess, coupling, land, mask, upper, lower,
    aux, one, three,
):
    even, _, _ = position()
    aux[...] = jnp.zeros_like(aux)
    for a, i, tile, spare in aux_slots():
        aux[a, 7 - i : 8 - i, :] = upper[tile, spare : spare + 1, :]
        aux[a, 8 + i : 9 + i, :] = lower[tile, 6 + spare : 7 + spare, :]

    def field(f):
        def of(tile):
            rows = slice(0, 8)
            if tile in (0, 5):
                if f < LEVELS:
                    block = upper.at[f] if tile == 0 else lower.at[f]
                else:
                    block = aux.at[f - LEVELS]
                    rows = slice(0, 8) if tile == 0 else slice(8, 16)
            else:
                rows = slice(tile * 8 - 8, tile * 8)
                if f < LEVELS:
                    block = state.at[f]
                elif f == AT_COUPLING:
                    block = coupling
                elif f == AT_LAND:
                    block = land
                elif f == AT_MASK:
                    block = mask
                else:
                    block = guess.at[f - AT_GUESS]
                    base = (tile - 1) // 2 * 16
                    part = slice((tile - 1) % 2 * 8, (tile - 1) % 2 * 8 + 8)
                    head = block[base : base + 16, :LANES].astype(F32)[part]
                    tail = block[base : base + 16, CY - LANES :].astype(F32)[part]
                    return head, tail
            head, tail = block[rows, :LANES], block[rows, CY - LANES :]
            return head.astype(F32), tail.astype(F32)

        return of

    pack_columns([field(f) for f in range(N_FIELDS)], one, three, even)


CONE = SUB + 1


def first_cone(
    diff, mix, state, guess, coupling, land, mask, upper, lower, aux, one, three,
    series, hd, ud, hs_out, us_out, fixed_out,
    s0, s1, g, emitted, hs, us, fixed, sems,
):
    writes = []

    def write(src, dst):
        c = pltpu.make_async_copy(src, dst, sems.at[len(writes)])
        c.start()
        writes.append(c)

    even, first, last = position()
    ocean = lax.axis_index("comp") == 1
    zero_pads(s0, CONE)
    zero_pads(s1, CONE - 1)
    for l in range(CONE):
        place_rows(s0.at[l], state[l], upper[l], lower[l])

    def rows_of(ref, k, f, own):
        ref[k, 0:8, :CY] = aux[f - LEVELS, 0:8, :]
        ref[k, 8 : 8 + CX, :CY] = own
        ref[k, 8 + CX : 16 + CX, :CY] = aux[f - LEVELS, 8:16, :]

    rows_of(fixed, 0, AT_COUPLING, coupling[...])
    rows_of(fixed, 1, AT_MASK, mask[...].astype(F32))
    rows_of(fixed, 2, AT_LAND, land[...])
    for t in range(SUB - 1):
        rows_of(g, t, AT_GUESS + t, guess[t].astype(F32))
    g[SUB - 1, 8 : 8 + CX, :CY] = guess[SUB - 1].astype(F32)

    side = slice(CY, COLS)
    slot = {AT_COUPLING: 0, AT_MASK: 1, AT_LAND: 2}

    def put(f, tile, value):
        rows = slice(tile * 8, tile * 8 + 8)
        if f < LEVELS:
            s0[f, tile * 8 + 8 : tile * 8 + 16, side] = value
        elif f < AT_GUESS:
            fixed[slot[f], rows, side] = value
        else:
            g[f - AT_GUESS, rows, side] = value

    fields = [*range(CONE), *range(LEVELS, N_FIELDS)]
    place_sides(put, fields, one, three, even, first, last)
    g[SUB - 1, :, side] = jnp.zeros((BAND, LANES), F32)
    fixed[2] = (1.0 - fixed[1]) * fixed[2]
    write(fixed, fixed_out)

    for t in range(SUB):
        src, dst = (s0, s1) if t % 2 == 0 else (s1, s0)

        for r in range(*strips(t)):
            strip = Strip(r, first, last)
            h = strip.spread(src, 0, diff[0])
            u_prev = None
            for l in range(SUB - t):
                h_next = strip.spread(src, l + 1, diff[l + 1])
                u = flux_between(mix[l], h_next, h)
                v = added(h, u)
                if l == t and t < 3:
                    strip.save(us, t, v)
                    if t:
                        strip.save(hs, t - 1, h)
                if u_prev is not None:
                    v = less(v, u_prev)
                if l == 0:
                    c, m, ml = (strip.recall(fixed, i) for i in range(3))
                    v, e = surface(v, strip.recall(g, t), c, m, ml, ocean)
                    strip.save(emitted, t, e[:OWN_TILES])
                if t < SUB - 1:
                    strip.store(dst, l, v)
                h, u_prev = h_next, u
            strip.save(hd, t, h)
            strip.save(ud, t, u_prev)
            if t == 3:
                strip.save(hs, 2, h)
        if t < 3:
            write(us.at[t], us_out.at[t])
        if 0 < t < 4:
            write(hs.at[t - 1], hs_out.at[t - 1])

    write_series(series, emitted)
    for c in writes:
        c.wait()


def first_rest(
    diff, mix, state, upper, lower, one, three, hd, ud,
    final, hs_out, us_out, token,
    s0, s1, hs, us, sems,
):
    token[...] = jnp.zeros_like(token)
    even, first, last = position()
    zero_pads(s0, LEVELS)
    zero_pads(s1, LEVELS)
    for l in range(CONE, LEVELS):
        place_rows(s0.at[l], state[l], upper[l], lower[l])

    def put(f, tile, value):
        s0[f, tile * 8 + 8 : tile * 8 + 16, CY:COLS] = value

    place_sides(put, list(range(CONE, LEVELS)), one, three, even, first, last)

    for t in range(SUB):
        src, dst = (s0, s1) if t % 2 == 0 else (s1, s0)

        for r in range(*strips(t)):
            strip = Strip(r, first, last)
            h = strip.recall(hd, t)
            u_prev = strip.recall(ud, t)
            for l in range(SUB - t, LEVELS):
                if l < LEVELS - 1:
                    h_next = strip.spread(src, l + 1, diff[l + 1])
                    u = flux_between(mix[l], h_next, h)
                    v = added(h, u)
                else:
                    h_next = u = None
                    v = h
                if l == t and t >= 3:
                    strip.save(us, t - 3, v)
                    strip.save(hs, t - 3, h)
                v = less(v, u_prev)
                if t < SUB - 1:
                    strip.store(dst, l, v)
                elif l >= SUB:
                    rows = slice(r * 8 - 16, r * 8 - 8)
                    for k in range(OWN_TILES):
                        final[l, rows, k * LANES : (k + 1) * LANES] = v[k]
                h, u_prev = h_next, u
    writes = [
        pltpu.make_async_copy(hs, hs_out, sems.at[0]),
        pltpu.make_async_copy(us, us_out, sems.at[1]),
    ]
    for c in writes:
        c.start()
    for c in writes:
        c.wait()


def regrid(
    table, received, weights, mask, before,
    out, top, bottom, gap,
    x, y,
):
    del before
    for half in range(CX // 16):
        for j in range(OWN_TILES):
            cols = slice(j * LANES, (j + 1) * LANES)
            for t in range(SUB):
                v16 = received[t, half * 16 : half * 16 + 16, cols].astype(F32)
                for part in range(2):
                    row = half * 16 + part * 8
                    start = (row * OWN_TILES + j) * 8 + t
                    x[pl.ds(start, 8, stride=OWN_TILES * 8), :] = v16[part * 8 : part * 8 + 8]

    @pl.loop(0, BLOCKS, unroll=32)
    def _(q):
        a, w = [], []
        for k in range(2):
            entry = table[q * 2 + k]
            start = pl.multiple_of((entry // PATTERNS) * 8, 8)
            a.append(x[pl.ds(start, 8), :].astype(BF16))
            w.append(weights[entry % PATTERNS])
        r = jnp.dot(
            jnp.concatenate(a, 1), jnp.concatenate(w, 0), preferred_element_type=F32
        )
        y[pl.ds(q, 8, stride=BLOCKS), :] = r

    partial = [jnp.zeros((8, LANES), F32) for _ in range(SUB)]
    wet = jnp.zeros((8, LANES), F32)
    for half in range(CX // 16):
        for j in range(OWN_TILES):
            cols = slice(j * LANES, (j + 1) * LANES)
            masks = []
            for part in range(2):
                row = half * 16 + part * 8
                masks.append(mask[row : row + 8, cols].astype(F32))
                wet += masks[-1]
            for t in range(SUB):
                v16 = received[t, half * 16 : half * 16 + 16, cols].astype(F32)
                for part in range(2):
                    row = half * 16 + part * 8
                    start = t * BLOCKS + row * OWN_TILES + j
                    v = y[pl.ds(start, 8, stride=OWN_TILES), :]
                    out[t, row : row + 8, cols] = v
                    partial[t] += masks[part] * (v16[part * 8 : part * 8 + 8] - v)
                    if t < SUB - 1 and row == 0:
                        top[t, :, cols] = v
                    if t < SUB - 1 and row == CX - 8:
                        bottom[t, :, cols] = v
    row, lane = iotas()
    total = jnp.zeros((8, LANES), F32)
    for t, value in enumerate([*partial, wet]):
        total = jnp.where(row == t, jnp.sum(value, axis=0, keepdims=True), total)
    total = jnp.sum(total, axis=1, keepdims=True)
    total = jnp.sum(jnp.where(row == lane, total, 0.0), axis=0, keepdims=True)
    for k in range(gap.shape[0]):
        gap[k] = total


def pack_second(out, upper, lower, one, three):
    even, _, _ = position()

    def field(t):
        def of(tile):
            if tile == 0:
                block, rows = upper.at[t], slice(0, 8)
            elif tile == 5:
                block, rows = lower.at[t], slice(0, 8)
            else:
                block, rows = out.at[t], slice(tile * 8 - 8, tile * 8)
            return block[rows, :LANES], block[rows, CY - LANES :]

        return of

    pack_columns([field(t) for t in range(SUB - 1)], one, three, even)


def gap_means(gap):
    total = jnp.sum(gap[...], axis=0)
    lane = lax.broadcasted_iota(jnp.int32, (1, LANES), 1)
    wet = jnp.sum(jnp.where(lane == SUB, total, 0.0), axis=1, keepdims=True)
    return [
        jnp.sum(jnp.where(lane == t, total, 0.0), axis=1, keepdims=True) / wet for t in range(SUB)
    ]


def second_cone(
    diff, mix, fixed_in, regridded, upper, lower, one, three, gap, hs_in, us_in,
    series, final0, hx, ux,
    s0, s1, g, emitted, fixed, hs, us, sems,
):
    reads = []
    for i, (src, dst) in enumerate(((us_in, us), (fixed_in, fixed), (hs_in, hs))):
        reads.append(pltpu.make_async_copy(src, dst, sems.at[i]))
        reads[-1].start()
    even, first, last = position()
    ocean = lax.axis_index("comp") == 1
    zero_pads(s0, 3)
    zero_pads(s1, 3)
    for t in range(SUB):
        if t < SUB - 1:
            g[t, 0:8, :CY] = upper[t]
            g[t, 8 + CX : 16 + CX, :CY] = lower[t]
        g[t, 8 : 8 + CX, :CY] = regridded[t]

    def put(f, tile, value):
        g[f, tile * 8 : tile * 8 + 8, CY:COLS] = value

    place_sides(put, list(range(SUB - 1)), one, three, even, first, last)
    g[SUB - 1, :, CY:COLS] = jnp.zeros((BAND, LANES), F32)
    means = [jnp.broadcast_to(v, (8, LANES)) for v in gap_means(gap)]
    for c in reads:
        c.wait()

    for t in range(SUB):
        src, dst = (s0, s1) if t % 2 == 0 else (s1, s0)

        for r in range(*strips(t)):
            strip = Strip(r, first, last)
            h = strip.spread(src, 0, diff[0]) if t else None
            u_prev = None
            for l in range(min(t, SUB - 1 - t) + 1):
                if l < t:
                    if l + 1 < t:
                        h_next = strip.spread(src, l + 1, diff[l + 1])
                    else:
                        h_next = strip.recall(hs, t - 1)
                    u = flux_between(mix[l], h_next, h)
                    v = added(h, u)
                else:
                    v = strip.recall(us, t)
                if u_prev is not None:
                    v = less(v, u_prev)
                if l == 0:
                    c, m, ml = (strip.recall(fixed, i) for i in range(3))
                    f = [a + b * means[t] for a, b in zip(strip.recall(g, t), m)]
                    v, e = surface(v, f, c, m, ml, ocean)
                    strip.save(emitted, t, e[:OWN_TILES])
                    if t == SUB - 1:
                        rows = slice(r * 8 - 16, r * 8 - 8)
                        for k in range(OWN_TILES):
                            final0[rows, k * LANES : (k + 1) * LANES] = v[k]
                if t < SUB - 1:
                    strip.store(dst, l, v)
                if l < t:
                    h, u_prev = h_next, u
            if t >= 3:
                strip.save(hx, t - 3, h)
                strip.save(ux, t - 3, u_prev)

    write_series(series, emitted)


def second_rest(
    diff, mix, hx, ux, hs_in, us_in, final0, whole,
    final, token,
    s0, s1, hs, us, sems,
):
    del whole
    reads = [
        pltpu.make_async_copy(us_in, us, sems.at[0]),
        pltpu.make_async_copy(hs_in, hs, sems.at[1]),
    ]
    for c in reads:
        c.start()
    token[...] = jnp.zeros_like(token)
    gy = lax.axis_index("gy")
    first, last = gy == 0, gy == lax.axis_size("gy") - 1
    zero_pads(s0, SUB)
    zero_pads(s1, SUB)
    final[0] = final0[...]
    for c in reads:
        c.wait()
    for t in range(3, SUB):
        src, dst = (s0, s1) if t % 2 == 0 else (s1, s0)

        for r in range(*strips(t)):
            strip = Strip(r, first, last)
            h = strip.recall(hx, t - 3)
            u_prev = strip.recall(ux, t - 3)
            for l in range(SUB - t, t + 1):
                if l < t:
                    if l + 1 < t:
                        h_next = strip.spread(src, l + 1, diff[l + 1])
                    else:
                        h_next = strip.recall(hs, t - 3)
                    u = flux_between(mix[l], h_next, h)
                    v = added(h, u)
                    h = h_next
                else:
                    u = None
                    v = strip.recall(us, t - 3)
                v = less(v, u_prev)
                u_prev = u
                if t < SUB - 1:
                    strip.store(dst, l, v)
                else:
                    rows = slice(r * 8 - 16, r * 8 - 8)
                    for k in range(OWN_TILES):
                        final[l, rows, k * LANES : (k + 1) * LANES] = v[k]


def finish(regridded, mask, gap, forcing):
    for t, mean in enumerate(gap_means(gap)):
        forcing[t] = regridded[t] + mask[...].astype(F32) * mean


def shifted(value, axis, by):
    n = lax.axis_size(axis)
    return lax.ppermute(value, axis, [(i, (i + by) % n) for i in range(n)])


def paired(value, axis, mask):
    return lax.ppermute(value, axis, [(i, i ^ mask) for i in range(lax.axis_size(axis))])


def per_device(
    state, guess, diffusion, mixing, coupling, land_temp, land_mask, weights, source_block, pattern
):
    state, guess, diff, mix, coupling = state[0], guess[0], diffusion[0], mixing[0], coupling[0]
    weights = weights[0]
    table = (source_block[0] * PATTERNS + pattern[0]).reshape(2 * BLOCKS)
    peers = lax.axis_size("gx") * lax.axis_size("gy")
    band = lambda n: shape(n, BAND, COLS)
    field_buf = lambda n: pltpu.VMEM((n, ROWS, COLS), F32)
    band_buf = lambda n: pltpu.VMEM((n, BAND, COLS), F32)

    message = shape(LEVELS, 8, CY)
    to_lower, to_upper = call(
        first_edges,
        [message, message],
        [
            pltpu.VMEM((AUX, 8, CY), F32),
            pltpu.VMEM((AUX, 8, CY), F32),
            pltpu.VMEM((2, 8, CY), jnp.int32),
            pltpu.VMEM((2, SUB - 1, 16, CY), BF16),
            pltpu.SemaphoreType.DMA((10,)),
        ],
        [HBM] * 5 + [SM],
    )(state, guess, coupling, land_temp, land_mask, table)
    lower, upper = shifted(to_lower, "gx", -1), shifted(to_upper, "gx", 1)
    packed = shape(BAND, PACK_LANES)
    aux, one, three = call(pack_first, [shape(AUX, 16, CY), packed, packed], [], [VM] * 7)(
        state, guess, coupling, land_temp, land_mask, upper, lower
    )
    one, three = paired(one, "gy", 1), paired(three, "gy", 3)

    series, hd, ud, hs, us, fixed = call(
        first_cone,
        [shape(SUB, CX, CY, dtype=BF16), band(SUB), band(SUB), band(3), band(3), band(3)],
        [
            field_buf(CONE), field_buf(CONE), band_buf(SUB), band_buf(SUB),
            band_buf(3), band_buf(3), band_buf(3), pltpu.SemaphoreType.DMA((7,)),
        ],
        [SM, SM] + [VM] * 10,
        out_specs=[VM] * 3 + [HBM] * 3,
    )(diff, mix, state, guess, coupling, land_temp, land_mask, upper, lower, aux, one, three)

    def exchange(series, before):
        received = paired(series, "comp", 1)
        edges = shape(SUB - 1, 8, CY)
        out, top, bottom, gap = call(
            regrid,
            [shape(SUB, CX, CY), edges, edges, shape(peers, 1, LANES)],
            [pltpu.VMEM((BLOCKS * 8, LANES), F32), pltpu.VMEM((BLOCKS * 8, LANES), F32)],
            [SM, VM, VM, VM, VM],
        )(table, received, weights, land_mask, before)
        return out, top, bottom, gap

    whole, hs_rest, us_rest, token = call(
        first_rest,
        [shape(LEVELS, CX, CY), band(3), band(3), shape(8, LANES)],
        [
            field_buf(LEVELS), field_buf(LEVELS),
            band_buf(3), band_buf(3), pltpu.SemaphoreType.DMA((2,)),
        ],
        [SM, SM] + [VM] * 7,
        out_specs=[VM, HBM, HBM, VM],
    )(diff, mix, state, upper, lower, one, three, hd, ud)

    out, top, bottom, gap = exchange(series, token)
    lower, upper = shifted(top, "gx", -1), shifted(bottom, "gx", 1)
    gap = lax.all_to_all(gap, ("gx", "gy"), 0, 0)
    packed = shape(BAND, LANES)
    one, three = call(pack_second, [packed, packed], [], [VM] * 3)(out, upper, lower)
    one, three = paired(one, "gy", 1), paired(three, "gy", 3)

    series, final0, hx, ux = call(
        second_cone,
        [shape(SUB, CX, CY, dtype=BF16), shape(CX, CY), band(3), band(3)],
        [
            field_buf(3), field_buf(3), band_buf(SUB), band_buf(SUB),
            band_buf(3), band_buf(3), band_buf(3), pltpu.SemaphoreType.DMA((3,)),
        ],
        [SM, SM, HBM] + [VM] * 6 + [HBM, HBM],
    )(diff, mix, fixed, out, upper, lower, one, three, gap, hs, us)

    whole, token = call(
        second_rest,
        [shape(LEVELS, CX, CY), shape(8, LANES)],
        [
            field_buf(SUB), field_buf(SUB),
            band_buf(3), band_buf(3), pltpu.SemaphoreType.DMA((2,)),
        ],
        [SM, SM, VM, VM, HBM, HBM, VM, pl.BlockSpec(memory_space=pl.ANY)],
        out_specs=[pl.BlockSpec((SUB, CX, CY), lambda i: (0, 0, 0)), VM],
        grid=(1,),
        input_output_aliases={7: 0},
    )(diff, mix, hx, ux, hs_rest, us_rest, final0, whole)

    out, _, _, gap = exchange(series, token)
    gap = lax.all_to_all(gap, ("gx", "gy"), 0, 0)
    (forcing,) = call(finish, [shape(SUB, CX, CY)], [], [VM] * 3)(out, land_mask, gap)
    return whole[None], forcing[None]


def solution(mesh):
    placed = (
        P("comp", None, "gx", "gy"),
        P("comp", None, "gx", "gy"),
        P("comp", None),
        P("comp", None),
        P("comp", "gx", "gy"),
        P("gx", "gy"),
        P("gx", "gy"),
        P("comp", ("gx", "gy"), None, None),
        P("comp", "gx", "gy", None),
        P("comp", "gx", "gy", None),
    )
    return jax.shard_map(
        per_device,
        mesh=mesh,
        in_specs=placed,
        out_specs=(P("comp", None, "gx", "gy"), P("comp", None, "gx", "gy")),
        check_vma=False,
    )
```

```python
import jax
import jax.numpy as jnp
from jax import lax
from jax.experimental import pallas as pl
from jax.experimental.pallas import tpu as pltpu
from jax.sharding import PartitionSpec as P

F32 = jnp.float32
BF16 = jnp.bfloat16
SUB = 6
LEVELS = 16
CX = 32
CY = 512
LANES = 128
OWN_TILES = CY // LANES
COLS = CY + LANES
ROWS = CX + 32
BAND = CX + 16
PATTERNS = 32
BLOCKS = CX * OWN_TILES
VMEM_LIMIT = 12 * 1024 * 1024
EDGE_GRANT = 60 * 1024 * 1024

N_FIELDS = LEVELS + 3 + SUB - 1
AT_COUPLING, AT_LAND, AT_MASK, AT_GUESS = LEVELS, LEVELS + 1, LEVELS + 2, LEVELS + 3
PACK_LANES = 256

VM = pl.BlockSpec(memory_space=pltpu.VMEM)
SM = pl.BlockSpec(memory_space=pltpu.SMEM)
HBM = pl.BlockSpec(memory_space=pltpu.HBM)


def shape(*dims, dtype=F32):
    return jax.ShapeDtypeStruct(dims, dtype)


def call(body, outs, scratch, ins, out_specs=None, grant=VMEM_LIMIT, **kw):
    return pl.pallas_call(
        body,
        out_shape=outs,
        in_specs=ins,
        out_specs=[VM] * len(outs) if out_specs is None else out_specs,
        scratch_shapes=scratch,
        compiler_params=pltpu.CompilerParams(vmem_limit_bytes=grant),
        **kw,
    )


def iotas():
    row = lax.broadcasted_iota(jnp.int32, (8, LANES), 0)
    lane = lax.broadcasted_iota(jnp.int32, (8, LANES), 1)
    return row, lane


def roll_lanes(x, shift):
    shift %= LANES
    return x if shift == 0 else pltpu.roll(x, shift, 1)


def pack_columns(fields, one, three, even):
    _, lane = iotas()
    groups = PACK_LANES // LANES if len(fields) > 16 else 1
    for tile in range(6):
        for g in range(groups):
            left = jnp.zeros((8, LANES), F32)
            right = jnp.zeros((8, LANES), F32)
            for f in range(g * 16, min(len(fields), g * 16 + 16)):
                at = (f % 16) * 8
                head, tail = fields[f](tile)
                left = jnp.where((lane >= at) & (lane < at + 8), roll_lanes(head, at), left)
                right = jnp.where((lane >= at) & (lane < at + 8), roll_lanes(tail, at + 8), right)
            span = (slice(tile * 8, tile * 8 + 8), slice(g * LANES, (g + 1) * LANES))
            one[span] = jnp.where(even, right, left)
            three[span] = jnp.where(even, left, right)


def side_halos(one, three, even, first, last, tile, g):
    span = (slice(tile * 8, tile * 8 + 8), slice(g * LANES, (g + 1) * LANES))
    a, b = one[span], three[span]
    right = jnp.where(last, 0.0, jnp.where(even, a, b))
    left = jnp.where(first, 0.0, jnp.where(even, b, a))
    return right, left


def side_tile(right, left, f, lane):
    at = (f % 16) * 8
    return jnp.where(
        lane < 6,
        roll_lanes(right, -at),
        jnp.where(lane >= LANES - 6, roll_lanes(left, LANES - 8 - at), 0.0),
    )


def place_sides(dst_of, fields, one, three, even, first, last):
    _, lane = iotas()
    for tile in range(6):
        packs = {}
        for f in fields:
            g = f // 16
            if g not in packs:
                packs[g] = side_halos(one, three, even, first, last, tile, g)
            dst_of(f, tile, side_tile(*packs[g], f, lane))


def place_rows(dst, own, upper, lower):
    dst[8:16, :CY] = upper
    dst[16 : 16 + CX, :CY] = own
    dst[16 + CX : 24 + CX, :CY] = lower


def zero_pads(ref, count):
    for l in range(count):
        ref[l, 0:8, :] = jnp.zeros((8, COLS), F32)
        ref[l, ROWS - 8 : ROWS, :] = jnp.zeros((8, COLS), F32)


def position():
    gy = lax.axis_index("gy")
    return gy % 2 == 0, gy == 0, gy == lax.axis_size("gy") - 1


class Strip:
    def __init__(self, r, first, last):
        self.r = r
        row, lane = iotas()
        self.row_first, self.row_last = row == 0, row == 7
        self.lane_first, self.lane_last = lane == 0, lane == LANES - 1
        self.inside = ((lane < 6) & jnp.logical_not(last)) | (
            (lane >= LANES - 6) & jnp.logical_not(first)
        )

    def load(self, ref, l, shift=0):
        rows = slice(self.r * 8 + shift, self.r * 8 + shift + 8)
        return [ref[l, rows, k * LANES : (k + 1) * LANES] for k in range(OWN_TILES + 1)]

    def spread(self, ref, l, d):
        x = self.load(ref, l)
        above = self.load(ref, l, -8)
        below = self.load(ref, l, 8)
        out = []
        n = len(x)
        for k in range(n):
            c = x[k]
            up = pltpu.roll(jnp.where(self.row_last, above[k], c), 1, 0)
            down = pltpu.roll(jnp.where(self.row_first, below[k], c), 7, 0)
            left = pltpu.roll(jnp.where(self.lane_last, x[k - 1], c), 1, 1)
            right = pltpu.roll(jnp.where(self.lane_first, x[(k + 1) % n], c), LANES - 1, 1)
            out.append(c + d * (((up + down) + (left + right)) - 4.0 * c))
        return out

    def store(self, ref, l, values):
        rows = slice(self.r * 8, self.r * 8 + 8)
        for k, v in enumerate(values):
            if k == OWN_TILES:
                v = jnp.where(self.inside, v, 0.0)
            ref[l, rows, k * LANES : (k + 1) * LANES] = v

    def save(self, ref, l, values):
        rows = slice(self.r * 8 - 8, self.r * 8)
        for k, v in enumerate(values):
            ref[l, rows, k * LANES : (k + 1) * LANES] = v

    def recall(self, ref, l):
        return self.load(ref, l, -8)


def flux_between(mix, lower, upper):
    return [mix * (a - b) for a, b in zip(lower, upper)]


def added(a, b):
    return [x + y for x, y in zip(a, b)]


def less(a, b):
    return [x - y for x, y in zip(a, b)]


def surface(v, f, c, m, ml, ocean):
    new, emitted = [], []
    for vk, fk, ck, mk, lk in zip(v, f, c, m, ml):
        mf = mk * fk
        flux = ck * (vk - (mf + lk))
        warmed = vk + ck * mf
        new.append(jnp.where(ocean, warmed, vk - flux))
        emitted.append(jnp.where(ocean, mk * warmed, flux))
    return new, emitted


class Rows:
    def __init__(self, ref, start):
        self.ref, self.start = ref, start

    def __getitem__(self, l):
        return self.ref[self.start + l]


def coefficients(coeff):
    return Rows(coeff, 0), Rows(coeff, LEVELS)


def strips(t):
    return (1, 7) if t < SUB - 1 else (2, 6)


def write_series(series, emitted):
    for t in range(SUB):
        for half in range(CX // 16):
            rows = slice(8 + half * 16, 24 + half * 16)
            series[t, half * 16 : half * 16 + 16, :] = emitted[t, rows, :CY].astype(BF16)


AUX = 3 + SUB - 1


def aux_slots():
    n = 0
    for a in range(AUX):
        for i in range(SUB - 1 if a < 3 else SUB - 1 - (a - 3)):
            yield a, i, n // 2, n % 2
            n += 1


def first_edges(
    state, guess, coupling, land, mask,
    to_lower, to_upper, token,
    head, tail, ints, short, sems,
):
    token[...] = jnp.zeros_like(token)
    n = 0
    copies = []

    def copy(src, dst):
        nonlocal n
        c = pltpu.make_async_copy(src, dst, sems.at[n])
        c.start()
        copies.append(c)
        n += 1

    for side, msg, buf in ((0, to_lower, head), (1, to_upper, tail)):
        rows = pl.ds(side * (CX - 8), 8)
        copy(state.at[:, rows, :], msg)
        copy(coupling.at[rows, :], buf.at[0])
        copy(land.at[rows, :], buf.at[1])
        copy(mask.at[rows, :], ints.at[side])
        copy(guess.at[pl.ds(0, SUB - 1), pl.ds(side * (CX - 16), 16), :], short.at[side])
    for c in copies:
        c.wait()
    for side, buf in ((0, head), (1, tail)):
        buf[2] = ints[side].astype(F32)
        for t in range(SUB - 1):
            rows16 = short[side, t].astype(F32)
            buf[3 + t] = rows16[8:] if side else rows16[:8]
    for a, i, tile, spare in aux_slots():
        to_lower[tile, 6 + spare : 7 + spare, :] = head[a, i : i + 1, :]
        to_upper[tile, spare : spare + 1, :] = tail[a, 7 - i : 8 - i, :]


def pack_first(
    state, guess, coupling, land, mask, upper, lower, before,
    aux, one, three,
):
    del before
    even, _, _ = position()
    aux[...] = jnp.zeros_like(aux)
    for a, i, tile, spare in aux_slots():
        aux[a, 7 - i : 8 - i, :] = upper[tile, spare : spare + 1, :]
        aux[a, 8 + i : 9 + i, :] = lower[tile, 6 + spare : 7 + spare, :]

    def field(f):
        def of(tile):
            rows = slice(0, 8)
            if tile in (0, 5):
                if f < LEVELS:
                    block = upper.at[f] if tile == 0 else lower.at[f]
                else:
                    block = aux.at[f - LEVELS]
                    rows = slice(0, 8) if tile == 0 else slice(8, 16)
            else:
                rows = slice(tile * 8 - 8, tile * 8)
                if f < LEVELS:
                    block = state.at[f]
                elif f == AT_COUPLING:
                    block = coupling
                elif f == AT_LAND:
                    block = land
                elif f == AT_MASK:
                    block = mask
                else:
                    block = guess.at[f - AT_GUESS]
                    base = (tile - 1) // 2 * 16
                    part = slice((tile - 1) % 2 * 8, (tile - 1) % 2 * 8 + 8)
                    head = block[base : base + 16, :LANES].astype(F32)[part]
                    tail = block[base : base + 16, CY - LANES :].astype(F32)[part]
                    return head, tail
            head, tail = block[rows, :LANES], block[rows, CY - LANES :]
            return head.astype(F32), tail.astype(F32)

        return of

    pack_columns([field(f) for f in range(N_FIELDS)], one, three, even)


CONE = SUB + 1


def first_cone(
    coeff, state, guess, coupling, land, mask, upper, lower, aux, one, three,
    series, hd, ud, hs_out, us_out, fixed_out, coeff_out,
    s0, s1, g, emitted, hs, us, fixed, sems,
):
    diff, mix = coefficients(coeff)
    writes = []

    def write(src, dst):
        c = pltpu.make_async_copy(src, dst, sems.at[len(writes)])
        c.start()
        writes.append(c)

    even, first, last = position()
    ocean = lax.axis_index("comp") == 1
    zero_pads(s0, CONE)
    zero_pads(s1, CONE - 1)
    for l in range(CONE):
        place_rows(s0.at[l], state[l], upper[l], lower[l])

    def rows_of(ref, k, f, own):
        ref[k, 0:8, :CY] = aux[f - LEVELS, 0:8, :]
        ref[k, 8 : 8 + CX, :CY] = own
        ref[k, 8 + CX : 16 + CX, :CY] = aux[f - LEVELS, 8:16, :]

    rows_of(fixed, 0, AT_COUPLING, coupling[...])
    rows_of(fixed, 1, AT_MASK, mask[...].astype(F32))
    rows_of(fixed, 2, AT_LAND, land[...])
    for t in range(SUB - 1):
        rows_of(g, t, AT_GUESS + t, guess[t].astype(F32))
    g[SUB - 1, 8 : 8 + CX, :CY] = guess[SUB - 1].astype(F32)

    side = slice(CY, COLS)
    slot = {AT_COUPLING: 0, AT_MASK: 1, AT_LAND: 2}

    def put(f, tile, value):
        rows = slice(tile * 8, tile * 8 + 8)
        if f < LEVELS:
            s0[f, tile * 8 + 8 : tile * 8 + 16, side] = value
        elif f < AT_GUESS:
            fixed[slot[f], rows, side] = value
        else:
            g[f - AT_GUESS, rows, side] = value

    fields = [*range(CONE), *range(LEVELS, N_FIELDS)]
    place_sides(put, fields, one, three, even, first, last)
    g[SUB - 1, :, side] = jnp.zeros((BAND, LANES), F32)
    fixed[2] = (1.0 - fixed[1]) * fixed[2]
    write(fixed, fixed_out)
    write(coeff, coeff_out)

    for t in range(SUB):
        src, dst = (s0, s1) if t % 2 == 0 else (s1, s0)

        for r in range(*strips(t)):
            strip = Strip(r, first, last)
            h = strip.spread(src, 0, diff[0])
            u_prev = None
            for l in range(SUB - t):
                h_next = strip.spread(src, l + 1, diff[l + 1])
                u = flux_between(mix[l], h_next, h)
                v = added(h, u)
                if l == t and t < 3:
                    strip.save(us, t, v)
                    if t:
                        strip.save(hs, t - 1, h)
                if u_prev is not None:
                    v = less(v, u_prev)
                if l == 0:
                    c, m, ml = (strip.recall(fixed, i) for i in range(3))
                    v, e = surface(v, strip.recall(g, t), c, m, ml, ocean)
                    strip.save(emitted, t, e[:OWN_TILES])
                if t < SUB - 1:
                    strip.store(dst, l, v)
                h, u_prev = h_next, u
            strip.save(hd, t, h)
            strip.save(ud, t, u_prev)
            if t == 3:
                strip.save(hs, 2, h)
        if t < 3:
            write(us.at[t], us_out.at[t])
        if 0 < t < 4:
            write(hs.at[t - 1], hs_out.at[t - 1])

    write_series(series, emitted)
    for c in writes:
        c.wait()


def first_rest(
    coeff, state, upper, lower, one, three, hd, ud,
    final, hs_out, us_out, token,
    s0, s1, hs, us, sems,
):
    diff, mix = coefficients(coeff)
    token[...] = jnp.zeros_like(token)
    even, first, last = position()
    zero_pads(s0, LEVELS)
    zero_pads(s1, LEVELS)
    for l in range(CONE, LEVELS):
        place_rows(s0.at[l], state[l], upper[l], lower[l])

    def put(f, tile, value):
        s0[f, tile * 8 + 8 : tile * 8 + 16, CY:COLS] = value

    place_sides(put, list(range(CONE, LEVELS)), one, three, even, first, last)

    for t in range(SUB):
        src, dst = (s0, s1) if t % 2 == 0 else (s1, s0)

        for r in range(*strips(t)):
            strip = Strip(r, first, last)
            h = strip.recall(hd, t)
            u_prev = strip.recall(ud, t)
            for l in range(SUB - t, LEVELS):
                if l < LEVELS - 1:
                    h_next = strip.spread(src, l + 1, diff[l + 1])
                    u = flux_between(mix[l], h_next, h)
                    v = added(h, u)
                else:
                    h_next = u = None
                    v = h
                if l == t and t >= 3:
                    strip.save(us, t - 3, v)
                    strip.save(hs, t - 3, h)
                v = less(v, u_prev)
                if t < SUB - 1:
                    strip.store(dst, l, v)
                elif l >= SUB:
                    rows = slice(r * 8 - 16, r * 8 - 8)
                    for k in range(OWN_TILES):
                        final[l, rows, k * LANES : (k + 1) * LANES] = v[k]
                h, u_prev = h_next, u
    writes = [
        pltpu.make_async_copy(hs, hs_out, sems.at[0]),
        pltpu.make_async_copy(us, us_out, sems.at[1]),
    ]
    for c in writes:
        c.start()
    for c in writes:
        c.wait()


def balance(
    diff, mix, src, pat, weights, mask, after,
    out, wet, coeff,
    m, z, total, b, sem,
):
    del after
    for l in range(LEVELS):
        coeff[l] = jnp.full((8, LANES), diff[l], F32)
    for l in range(LEVELS - 1):
        coeff[LEVELS + l] = jnp.full((8, LANES), mix[l], F32)
    coeff[2 * LEVELS - 1] = jnp.zeros((8, LANES), F32)
    count = jnp.zeros((8, LANES), F32)
    for part in range(CX // 8):
        for j in range(OWN_TILES):
            v = mask[part * 8 : part * 8 + 8, j * LANES : (j + 1) * LANES].astype(F32)
            count += v
            m[pl.ds(part * 8 * OWN_TILES + j, 8, stride=OWN_TILES), :] = v
    _, lane = iotas()
    count = jnp.sum(count, axis=(0, 1), keepdims=True)
    wet[...] = jnp.where(lane[:1] == SUB, count, 0.0)
    blocks = m[...].astype(BF16)

    @pl.loop(0, PATTERNS)
    def _(p):
        z[p] = lax.dot_general(
            blocks, weights[p], (((1,), (1,)), ((), ())), preferred_element_type=F32
        )

    total[...] = m[...]

    @pl.loop(0, CX)
    def _(r):
        for j in range(OWN_TILES):
            for k in range(2):
                row = pl.ds(src[j, k, r], 1)
                total[row, :] = total[row, :] - z[pat[j, k, r], pl.ds(r * OWN_TILES + j, 1), :]

    for part in range(CX // 8):
        for j in range(OWN_TILES):
            v = total[pl.ds(part * 8 * OWN_TILES + j, 8, stride=OWN_TILES), :]
            b[part * 8 : part * 8 + 8, j * LANES : (j + 1) * LANES] = v
    c = pltpu.make_async_copy(b, out, sem)
    c.start()
    c.wait()


def losses(
    received_in, factor, wet, before,
    gap, token,
    received, rows, sems,
):
    del before
    token[...] = jnp.zeros_like(token)
    c = pltpu.make_async_copy(received_in, received, sems.at[0])
    c.start()
    c.wait()
    partial = [jnp.zeros((8, LANES), F32) for _ in range(SUB)]
    for half in range(CX // 16):
        for j in range(OWN_TILES):
            cols = slice(j * LANES, (j + 1) * LANES)
            f = factor[half * 16 : half * 16 + 16, cols]
            for t in range(SUB):
                p = f * received[t, half * 16 : half * 16 + 16, cols].astype(F32)
                partial[t] += p[:8] + p[8:]
    row, lane = iotas()
    total = jnp.zeros((8, LANES), F32)
    for t, value in enumerate(partial):
        total = jnp.where(row == t, jnp.sum(value, axis=0, keepdims=True), total)
    total = jnp.sum(total, axis=1, keepdims=True)
    total = jnp.sum(jnp.where(row == lane, total, 0.0), axis=0, keepdims=True) + wet[...]
    for k in range(rows.shape[0]):
        rows[k] = total
    c = pltpu.make_async_copy(rows, gap, sems.at[1])
    c.start()
    c.wait()


def edge_slots():
    for t, tile, start in ((0, 0, 0), (2, 0, 5), (1, 1, 0), (3, 1, 4), (4, 1, 6)):
        yield t, SUB - 1 - t, tile, start


def regrid(
    src, pat, received_in, weights_in, before,
    out, top, bottom,
    x, y, received, weights, sems,
):
    del before
    reads = [
        pltpu.make_async_copy(received_in, received, sems.at[0]),
        pltpu.make_async_copy(weights_in, weights, sems.at[1]),
    ]
    for c in reads:
        c.start()
    reads[0].wait()
    for half in range(CX // 16):
        for j in range(OWN_TILES):
            cols = slice(j * LANES, (j + 1) * LANES)
            for t in range(SUB):
                v16 = received[t, half * 16 : half * 16 + 16, cols].astype(F32)
                for part in range(2):
                    row = half * 16 + part * 8
                    start = (row * OWN_TILES + j) * 8 + t
                    x[pl.ds(start, 8, stride=OWN_TILES * 8), :] = v16[part * 8 : part * 8 + 8]
    reads[1].wait()

    @pl.loop(0, CX, unroll=8)
    def _(r):
        for j in range(OWN_TILES):
            a, w = [], []
            for k in range(2):
                start = pl.multiple_of(src[j, k, r] * 8, 8)
                a.append(x[pl.ds(start, 8), :].astype(BF16))
                w.append(weights[pat[j, k, r]])
            product = jnp.dot(
                jnp.concatenate(a, 1), jnp.concatenate(w, 0), preferred_element_type=F32
            )
            y[pl.ds(r * OWN_TILES + j, 8, stride=BLOCKS), :] = product

    for part in range(CX // 8):
        for j in range(OWN_TILES):
            cols = slice(j * LANES, (j + 1) * LANES)
            for t in range(SUB):
                start = t * BLOCKS + part * 8 * OWN_TILES + j
                out[t, part * 8 : part * 8 + 8, cols] = y[pl.ds(start, 8, stride=OWN_TILES), :]
    top[1, 7:8, :] = jnp.zeros((1, CY), F32)
    bottom[1, 7:8, :] = jnp.zeros((1, CY), F32)
    for t, n, tile, start in edge_slots():
        top[tile, start : start + n, :] = out[t, 0:n, :]
        bottom[tile, start : start + n, :] = out[t, CX - n : CX, :]


def halo_rows(halo, upper, lower):
    halo[...] = jnp.zeros_like(halo)
    for t, n, tile, start in edge_slots():
        halo[t, 8 - n : 8, :] = upper[tile, start : start + n, :]
        halo[t, 8 : 8 + n, :] = lower[tile, start : start + n, :]


def pack_second(out, upper, lower, one, three, halo):
    even, _, _ = position()
    halo_rows(halo, upper, lower)

    def field(t):
        def of(tile):
            if tile in (0, 5):
                block, rows = halo.at[t], slice(0, 8) if tile == 0 else slice(8, 16)
            else:
                block, rows = out.at[t], slice(tile * 8 - 8, tile * 8)
            return block[rows, :LANES], block[rows, CY - LANES :]

        return of

    pack_columns([field(t) for t in range(SUB - 1)], one, three, even)


def gap_means(gap):
    total = jnp.sum(gap[...], axis=0)
    lane = lax.broadcasted_iota(jnp.int32, (1, LANES), 1)
    wet = jnp.sum(jnp.where(lane == SUB, total, 0.0), axis=1, keepdims=True)
    return [
        jnp.sum(jnp.where(lane == t, total, 0.0), axis=1, keepdims=True) / wet for t in range(SUB)
    ]


def second_cone(
    coeff_in, fixed_in, regridded, upper, lower, one, three, gap, hs_in, us_in,
    series, final0, hx, ux, coeff_out,
    s0, s1, g, emitted, fixed, hs, us, halo, coeff, sems,
):
    diff, mix = coefficients(coeff)
    reads = []
    pairs = ((us_in, us), (fixed_in, fixed), (coeff_in, coeff), (hs_in, hs))
    for i, (src, dst) in enumerate(pairs):
        reads.append(pltpu.make_async_copy(src, dst, sems.at[i]))
        reads[-1].start()
    even, first, last = position()
    ocean = lax.axis_index("comp") == 1
    zero_pads(s0, 3)
    zero_pads(s1, 3)
    halo_rows(halo, upper, lower)
    for t in range(SUB):
        if t < SUB - 1:
            g[t, 0:8, :CY] = halo[t, 0:8, :]
            g[t, 8 + CX : 16 + CX, :CY] = halo[t, 8:16, :]
        g[t, 8 : 8 + CX, :CY] = regridded[t]

    def put(f, tile, value):
        g[f, tile * 8 : tile * 8 + 8, CY:COLS] = value

    place_sides(put, list(range(SUB - 1)), one, three, even, first, last)
    g[SUB - 1, :, CY:COLS] = jnp.zeros((BAND, LANES), F32)
    means = [jnp.broadcast_to(v, (8, LANES)) for v in gap_means(gap)]
    for c in reads:
        c.wait()
    coeff_out[...] = coeff[...]

    for t in range(SUB):
        src, dst = (s0, s1) if t % 2 == 0 else (s1, s0)

        for r in range(*strips(t)):
            strip = Strip(r, first, last)
            h = strip.spread(src, 0, diff[0]) if t else None
            u_prev = None
            for l in range(min(t, SUB - 1 - t) + 1):
                if l < t:
                    if l + 1 < t:
                        h_next = strip.spread(src, l + 1, diff[l + 1])
                    else:
                        h_next = strip.recall(hs, t - 1)
                    u = flux_between(mix[l], h_next, h)
                    v = added(h, u)
                else:
                    v = strip.recall(us, t)
                if u_prev is not None:
                    v = less(v, u_prev)
                if l == 0:
                    c, m, ml = (strip.recall(fixed, i) for i in range(3))
                    f = [a + b * means[t] for a, b in zip(strip.recall(g, t), m)]
                    v, e = surface(v, f, c, m, ml, ocean)
                    strip.save(emitted, t, e[:OWN_TILES])
                    if t == SUB - 1:
                        rows = slice(r * 8 - 16, r * 8 - 8)
                        for k in range(OWN_TILES):
                            final0[rows, k * LANES : (k + 1) * LANES] = v[k]
                if t < SUB - 1:
                    strip.store(dst, l, v)
                if l < t:
                    h, u_prev = h_next, u
            if t >= 3:
                strip.save(hx, t - 3, h)
                strip.save(ux, t - 3, u_prev)

    write_series(series, emitted)


def second_rest(
    coeff, hx, ux, hs_in, us_in, final0, whole,
    final, token,
    s0, s1, hs, us, sems,
):
    del whole
    diff, mix = coefficients(coeff)
    reads = [
        pltpu.make_async_copy(us_in, us, sems.at[0]),
        pltpu.make_async_copy(hs_in, hs, sems.at[1]),
    ]
    for c in reads:
        c.start()
    token[...] = jnp.zeros_like(token)
    gy = lax.axis_index("gy")
    first, last = gy == 0, gy == lax.axis_size("gy") - 1
    zero_pads(s0, SUB)
    zero_pads(s1, SUB)
    final[0] = final0[...]
    for c in reads:
        c.wait()
    for t in range(3, SUB):
        src, dst = (s0, s1) if t % 2 == 0 else (s1, s0)

        for r in range(*strips(t)):
            strip = Strip(r, first, last)
            h = strip.recall(hx, t - 3)
            u_prev = strip.recall(ux, t - 3)
            for l in range(SUB - t, t + 1):
                if l < t:
                    if l + 1 < t:
                        h_next = strip.spread(src, l + 1, diff[l + 1])
                    else:
                        h_next = strip.recall(hs, t - 3)
                    u = flux_between(mix[l], h_next, h)
                    v = added(h, u)
                    h = h_next
                else:
                    u = None
                    v = strip.recall(us, t - 3)
                v = less(v, u_prev)
                u_prev = u
                if t < SUB - 1:
                    strip.store(dst, l, v)
                else:
                    rows = slice(r * 8 - 16, r * 8 - 8)
                    for k in range(OWN_TILES):
                        final[l, rows, k * LANES : (k + 1) * LANES] = v[k]


def finish(regridded, mask, gap, forcing):
    for t, mean in enumerate(gap_means(gap)):
        forcing[t] = regridded[t] + mask[...].astype(F32) * mean


def shifted(value, axis, by):
    n = lax.axis_size(axis)
    return lax.ppermute(value, axis, [(i, (i + by) % n) for i in range(n)])


def paired(value, axis, mask):
    return lax.ppermute(value, axis, [(i, i ^ mask) for i in range(lax.axis_size(axis))])


def per_device(
    state, guess, diffusion, mixing, coupling, land_temp, land_mask, weights, source_block, pattern
):
    state, guess, diff, mix, coupling = state[0], guess[0], diffusion[0], mixing[0], coupling[0]
    weights = weights[0]
    src = source_block[0].transpose(1, 2, 0)
    pat = pattern[0].transpose(1, 2, 0)
    peers = lax.axis_size("gx") * lax.axis_size("gy")
    band = lambda n: shape(n, BAND, COLS)
    field_buf = lambda n: pltpu.VMEM((n, ROWS, COLS), F32)
    band_buf = lambda n: pltpu.VMEM((n, BAND, COLS), F32)
    numbers = shape(2 * LEVELS, 8, LANES)

    message = shape(LEVELS, 8, CY)
    to_lower, to_upper, token = call(
        first_edges,
        [message, message, shape(8, LANES)],
        [
            pltpu.VMEM((AUX, 8, CY), F32),
            pltpu.VMEM((AUX, 8, CY), F32),
            pltpu.VMEM((2, 8, CY), jnp.int32),
            pltpu.VMEM((2, SUB - 1, 16, CY), BF16),
            pltpu.SemaphoreType.DMA((10,)),
        ],
        [HBM] * 5,
        grant=EDGE_GRANT,
    )(state, guess, coupling, land_temp, land_mask)
    state, guess, coupling, land_temp, mask, table, src, pat, to_lower, to_upper = (
        lax.optimization_barrier(
            (
                state, guess, coupling, land_temp, land_mask, weights, src, pat,
                to_lower, to_upper,
            )
        )
    )
    lower, upper = shifted(to_lower, "gx", -1), shifted(to_upper, "gx", 1)
    factor, wet, coeff = call(
        balance,
        [shape(CX, CY), shape(1, LANES), shape(2 * LEVELS, 8, LANES)],
        [
            pltpu.VMEM((BLOCKS, LANES), F32),
            pltpu.VMEM((PATTERNS, BLOCKS, LANES), F32),
            pltpu.VMEM((BLOCKS, LANES), F32),
            pltpu.VMEM((CX, CY), F32),
            pltpu.SemaphoreType.DMA(()),
        ],
        [SM, SM, SM, SM, VM, VM, VM],
        out_specs=[HBM, VM, VM],
    )(diff, mix, src, pat, table, mask, token)
    packed = shape(BAND, PACK_LANES)
    aux, one, three = call(pack_first, [shape(AUX, 16, CY), packed, packed], [], [VM] * 8)(
        state, guess, coupling, land_temp, mask, upper, lower, wet
    )
    one, three = paired(one, "gy", 1), paired(three, "gy", 3)

    series, hd, ud, hs, us, fixed, numbers_out = call(
        first_cone,
        [
            shape(SUB, CX, CY, dtype=BF16), band(SUB), band(SUB),
            band(3), band(3), band(3), numbers,
        ],
        [
            field_buf(CONE), field_buf(CONE), band_buf(SUB), band_buf(SUB),
            band_buf(3), band_buf(3), band_buf(3), pltpu.SemaphoreType.DMA((8,)),
        ],
        [VM] * 11,
        out_specs=[VM] * 3 + [HBM] * 4,
    )(coeff, state, guess, coupling, land_temp, mask, upper, lower, aux, one, three)

    def exchange(series, before):
        received = paired(series, "comp", 1)
        gap, after = call(
            losses,
            [shape(peers, 1, LANES), shape(8, LANES)],
            [
                pltpu.VMEM((SUB, CX, CY), BF16),
                pltpu.VMEM((peers, 1, LANES), F32),
                pltpu.SemaphoreType.DMA((2,)),
            ],
            [HBM, VM, VM, VM],
            out_specs=[HBM, VM],
        )(received, factor, wet, before)
        gap = lax.all_to_all(gap, ("gx", "gy"), 0, 0)
        edges = shape(2, 8, CY)
        out, top, bottom = call(
            regrid,
            [shape(SUB, CX, CY), edges, edges],
            [
                pltpu.VMEM((BLOCKS * 8, LANES), F32),
                pltpu.VMEM((BLOCKS * 8, LANES), F32),
                pltpu.VMEM((SUB, CX, CY), BF16),
                pltpu.VMEM((PATTERNS, LANES, LANES), BF16),
                pltpu.SemaphoreType.DMA((2,)),
            ],
            [SM, SM, HBM, HBM, VM],
            cost_estimate=pl.CostEstimate(
                flops=2 * BLOCKS * 8 * 2 * LANES * LANES,
                bytes_accessed=BLOCKS * 2 * LANES * LANES * 2,
                transcendentals=0,
            ),
        )(src, pat, received, weights, after)
        return out, top, bottom, gap

    whole, hs_rest, us_rest, token = call(
        first_rest,
        [shape(LEVELS, CX, CY), band(3), band(3), shape(8, LANES)],
        [
            field_buf(LEVELS), field_buf(LEVELS),
            band_buf(3), band_buf(3), pltpu.SemaphoreType.DMA((2,)),
        ],
        [VM] * 8,
        out_specs=[VM, HBM, HBM, VM],
    )(coeff, state, upper, lower, one, three, hd, ud)

    out, top, bottom, gap = exchange(series, token)
    lower, upper = shifted(top, "gx", -1), shifted(bottom, "gx", 1)
    packed = shape(BAND, LANES)
    one, three = call(
        pack_second, [packed, packed], [pltpu.VMEM((SUB - 1, 16, CY), F32)], [VM] * 3
    )(out, upper, lower)
    one, three = paired(one, "gy", 1), paired(three, "gy", 3)

    series, final0, hx, ux, coeff = call(
        second_cone,
        [shape(SUB, CX, CY, dtype=BF16), shape(CX, CY), band(3), band(3), numbers],
        [
            field_buf(3), field_buf(3), band_buf(SUB), band_buf(SUB),
            band_buf(3), band_buf(3), band_buf(3), pltpu.VMEM((SUB - 1, 16, CY), F32),
            pltpu.VMEM(numbers.shape, F32), pltpu.SemaphoreType.DMA((4,)),
        ],
        [HBM, HBM] + [VM] * 6 + [HBM, HBM],
    )(numbers_out, fixed, out, upper, lower, one, three, gap, hs, us)

    whole, token = call(
        second_rest,
        [shape(LEVELS, CX, CY), shape(8, LANES)],
        [
            field_buf(SUB), field_buf(SUB),
            band_buf(3), band_buf(3), pltpu.SemaphoreType.DMA((2,)),
        ],
        [VM, VM, VM, HBM, HBM, VM, pl.BlockSpec(memory_space=pl.ANY)],
        out_specs=[pl.BlockSpec((SUB, CX, CY), lambda i: (0, 0, 0)), VM],
        grid=(1,),
        input_output_aliases={6: 0},
    )(coeff, hx, ux, hs_rest, us_rest, final0, whole)

    out, _, _, gap = exchange(series, token)
    (forcing,) = call(finish, [shape(SUB, CX, CY)], [], [VM] * 3)(out, land_mask, gap)
    return whole[None], forcing[None]


def solution(mesh):
    placed = (
        P("comp", None, "gx", "gy"),
        P("comp", None, "gx", "gy"),
        P("comp", None),
        P("comp", None),
        P("comp", "gx", "gy"),
        P("gx", "gy"),
        P("gx", "gy"),
        P("comp", ("gx", "gy"), None, None),
        P("comp", "gx", "gy", None),
        P("comp", "gx", "gy", None),
    )
    return jax.shard_map(
        per_device,
        mesh=mesh,
        in_specs=placed,
        out_specs=(P("comp", None, "gx", "gy"), P("comp", None, "gx", "gy")),
        check_vma=False,
    )
```

```python
import jax
import jax.numpy as jnp
from jax import lax
from jax.experimental import pallas as pl
from jax.experimental.pallas import tpu as pltpu
from jax.sharding import PartitionSpec as P

F32 = jnp.float32
BF16 = jnp.bfloat16
SUB = 6
LEVELS = 16
CX = 32
CY = 512
LANES = 128
OWN_TILES = CY // LANES
COLS = CY + LANES
ROWS = CX + 32
BAND = CX + 16
PATTERNS = 32
BLOCKS = CX * OWN_TILES
VMEM_LIMIT = 12 * 1024 * 1024
EDGE_GRANT = 60 * 1024 * 1024

N_FIELDS = LEVELS + 3 + SUB - 1
AT_COUPLING, AT_LAND, AT_MASK, AT_GUESS = LEVELS, LEVELS + 1, LEVELS + 2, LEVELS + 3
PACK_LANES = 256

VM = pl.BlockSpec(memory_space=pltpu.VMEM)
SM = pl.BlockSpec(memory_space=pltpu.SMEM)
HBM = pl.BlockSpec(memory_space=pltpu.HBM)


def shape(*dims, dtype=F32):
    return jax.ShapeDtypeStruct(dims, dtype)


def call(body, outs, scratch, ins, out_specs=None, grant=VMEM_LIMIT, **kw):
    return pl.pallas_call(
        body,
        out_shape=outs,
        in_specs=ins,
        out_specs=[VM] * len(outs) if out_specs is None else out_specs,
        scratch_shapes=scratch,
        compiler_params=pltpu.CompilerParams(vmem_limit_bytes=grant),
        **kw,
    )


def iotas():
    row = lax.broadcasted_iota(jnp.int32, (8, LANES), 0)
    lane = lax.broadcasted_iota(jnp.int32, (8, LANES), 1)
    return row, lane


def roll_lanes(x, shift):
    shift %= LANES
    return x if shift == 0 else pltpu.roll(x, shift, 1)


def pack_columns(fields, one, three, even):
    _, lane = iotas()
    groups = PACK_LANES // LANES if len(fields) > 16 else 1
    for tile in range(6):
        for g in range(groups):
            left = jnp.zeros((8, LANES), F32)
            right = jnp.zeros((8, LANES), F32)
            for f in range(g * 16, min(len(fields), g * 16 + 16)):
                at = (f % 16) * 8
                head, tail = fields[f](tile)
                left = jnp.where((lane >= at) & (lane < at + 8), roll_lanes(head, at), left)
                right = jnp.where((lane >= at) & (lane < at + 8), roll_lanes(tail, at + 8), right)
            span = (slice(tile * 8, tile * 8 + 8), slice(g * LANES, (g + 1) * LANES))
            one[span] = jnp.where(even, right, left)
            three[span] = jnp.where(even, left, right)


def side_halos(one, three, even, first, last, tile, g):
    span = (slice(tile * 8, tile * 8 + 8), slice(g * LANES, (g + 1) * LANES))
    a, b = one[span], three[span]
    right = jnp.where(last, 0.0, jnp.where(even, a, b))
    left = jnp.where(first, 0.0, jnp.where(even, b, a))
    return right, left


def side_tile(right, left, f, lane):
    at = (f % 16) * 8
    return jnp.where(
        lane < 6,
        roll_lanes(right, -at),
        jnp.where(lane >= LANES - 6, roll_lanes(left, LANES - 8 - at), 0.0),
    )


def place_sides(dst_of, fields, one, three, even, first, last):
    _, lane = iotas()
    for tile in range(6):
        packs = {}
        for f in fields:
            g = f // 16
            if g not in packs:
                packs[g] = side_halos(one, three, even, first, last, tile, g)
            dst_of(f, tile, side_tile(*packs[g], f, lane))


def place_rows(dst, own, upper, lower):
    dst[8:16, :CY] = upper
    dst[16 : 16 + CX, :CY] = own
    dst[16 + CX : 24 + CX, :CY] = lower


def zero_pads(ref, count):
    for l in range(count):
        ref[l, 0:8, :] = jnp.zeros((8, COLS), F32)
        ref[l, ROWS - 8 : ROWS, :] = jnp.zeros((8, COLS), F32)


def position():
    gy = lax.axis_index("gy")
    return gy % 2 == 0, gy == 0, gy == lax.axis_size("gy") - 1


class Strip:
    def __init__(self, r, first, last):
        self.r = r
        row, lane = iotas()
        self.row_first, self.row_last = row == 0, row == 7
        self.lane_first, self.lane_last = lane == 0, lane == LANES - 1
        self.inside = ((lane < 6) & jnp.logical_not(last)) | (
            (lane >= LANES - 6) & jnp.logical_not(first)
        )

    def load(self, ref, l, shift=0):
        rows = slice(self.r * 8 + shift, self.r * 8 + shift + 8)
        return [ref[l, rows, k * LANES : (k + 1) * LANES] for k in range(OWN_TILES + 1)]

    def spread(self, ref, l, d):
        x = self.load(ref, l)
        above = self.load(ref, l, -8)
        below = self.load(ref, l, 8)
        out = []
        n = len(x)
        for k in range(n):
            c = x[k]
            up = pltpu.roll(jnp.where(self.row_last, above[k], c), 1, 0)
            down = pltpu.roll(jnp.where(self.row_first, below[k], c), 7, 0)
            left = pltpu.roll(jnp.where(self.lane_last, x[k - 1], c), 1, 1)
            right = pltpu.roll(jnp.where(self.lane_first, x[(k + 1) % n], c), LANES - 1, 1)
            out.append(c + d * (((up + down) + (left + right)) - 4.0 * c))
        return out

    def store(self, ref, l, values):
        rows = slice(self.r * 8, self.r * 8 + 8)
        for k, v in enumerate(values):
            if k == OWN_TILES:
                v = jnp.where(self.inside, v, 0.0)
            ref[l, rows, k * LANES : (k + 1) * LANES] = v

    def save(self, ref, l, values):
        rows = slice(self.r * 8 - 8, self.r * 8)
        for k, v in enumerate(values):
            ref[l, rows, k * LANES : (k + 1) * LANES] = v

    def recall(self, ref, l):
        return self.load(ref, l, -8)


def flux_between(mix, lower, upper):
    return [mix * (a - b) for a, b in zip(lower, upper)]


def added(a, b):
    return [x + y for x, y in zip(a, b)]


def less(a, b):
    return [x - y for x, y in zip(a, b)]


def surface(v, f, c, m, ml, ocean):
    new, emitted = [], []
    for vk, fk, ck, mk, lk in zip(v, f, c, m, ml):
        mf = mk * fk
        flux = ck * (vk - (mf + lk))
        warmed = vk + ck * mf
        new.append(jnp.where(ocean, warmed, vk - flux))
        emitted.append(jnp.where(ocean, mk * warmed, flux))
    return new, emitted


def coefficient_place(i):
    rows, cols = i // 5 * 8, i % 5 * LANES
    return slice(rows, rows + 8), slice(cols, cols + LANES)


class Rows:
    def __init__(self, ref, start):
        self.ref, self.start = ref, start

    def __getitem__(self, l):
        return self.ref[self.start + l]


def coefficients(coeff):
    return Rows(coeff, 0), Rows(coeff, LEVELS)


def strips(t):
    return (1, 7) if t < SUB - 1 else (2, 6)


def write_series(series, emitted):
    for t in range(SUB):
        for half in range(CX // 16):
            rows = slice(8 + half * 16, 24 + half * 16)
            series[t, half * 16 : half * 16 + 16, :] = emitted[t, rows, :CY].astype(BF16)


AUX = 3 + SUB - 1


def aux_slots():
    n = 0
    for a in range(AUX):
        for i in range(SUB - 1 if a < 3 else SUB - 1 - (a - 3)):
            yield a, i, n // 2, n % 2
            n += 1


def first_edges(
    state, guess, coupling, land, mask,
    to_lower, to_upper,
    head, tail, ints, short, sems,
):
    n = 0
    copies = []

    def copy(src, dst):
        nonlocal n
        c = pltpu.make_async_copy(src, dst, sems.at[n])
        c.start()
        copies.append(c)
        n += 1

    for side, msg, buf in ((0, to_lower, head), (1, to_upper, tail)):
        rows = pl.ds(side * (CX - 8), 8)
        copy(state.at[:, rows, :], msg)
        copy(coupling.at[rows, :], buf.at[0])
        copy(land.at[rows, :], buf.at[1])
        copy(mask.at[rows, :], ints.at[side])
        copy(guess.at[pl.ds(0, SUB - 1), pl.ds(side * (CX - 16), 16), :], short.at[side])
    for c in copies:
        c.wait()
    for side, buf in ((0, head), (1, tail)):
        buf[2] = ints[side].astype(F32)
        for t in range(SUB - 1):
            rows16 = short[side, t].astype(F32)
            buf[3 + t] = rows16[8:] if side else rows16[:8]
    for a, i, tile, spare in aux_slots():
        to_lower[tile, 6 + spare : 7 + spare, :] = head[a, i : i + 1, :]
        to_upper[tile, spare : spare + 1, :] = tail[a, 7 - i : 8 - i, :]


def pack_first(
    state, guess, coupling, land, mask, upper, lower, before,
    aux, one, three,
):
    del before
    even, _, _ = position()
    aux[...] = jnp.zeros_like(aux)
    for a, i, tile, spare in aux_slots():
        aux[a, 7 - i : 8 - i, :] = upper[tile, spare : spare + 1, :]
        aux[a, 8 + i : 9 + i, :] = lower[tile, 6 + spare : 7 + spare, :]

    def field(f):
        def of(tile):
            rows = slice(0, 8)
            if tile in (0, 5):
                if f < LEVELS:
                    block = upper.at[f] if tile == 0 else lower.at[f]
                else:
                    block = aux.at[f - LEVELS]
                    rows = slice(0, 8) if tile == 0 else slice(8, 16)
            else:
                rows = slice(tile * 8 - 8, tile * 8)
                if f < LEVELS:
                    block = state.at[f]
                elif f == AT_COUPLING:
                    block = coupling
                elif f == AT_LAND:
                    block = land
                elif f == AT_MASK:
                    block = mask
                else:
                    block = guess.at[f - AT_GUESS]
                    base = (tile - 1) // 2 * 16
                    part = slice((tile - 1) % 2 * 8, (tile - 1) % 2 * 8 + 8)
                    head = block[base : base + 16, :LANES].astype(F32)[part]
                    tail = block[base : base + 16, CY - LANES :].astype(F32)[part]
                    return head, tail
            head, tail = block[rows, :LANES], block[rows, CY - LANES :]
            return head.astype(F32), tail.astype(F32)

        return of

    pack_columns([field(f) for f in range(N_FIELDS)], one, three, even)


CONE = SUB + 1


def first_cone(
    coeff, state, guess, coupling, land, mask, upper, lower, aux, one, three,
    series, hd, ud, hs_out, us_out, fixed_out,
    s0, s1, g, emitted, hs, us, fixed, sems,
):
    diff, mix = coefficients(coeff)
    writes = []

    def write(src, dst):
        c = pltpu.make_async_copy(src, dst, sems.at[len(writes)])
        c.start()
        writes.append(c)

    even, first, last = position()
    ocean = lax.axis_index("comp") == 1
    zero_pads(s0, CONE)
    zero_pads(s1, CONE - 1)
    for l in range(CONE):
        place_rows(s0.at[l], state[l], upper[l], lower[l])

    def rows_of(ref, k, f, own):
        ref[k, 0:8, :CY] = aux[f - LEVELS, 0:8, :]
        ref[k, 8 : 8 + CX, :CY] = own
        ref[k, 8 + CX : 16 + CX, :CY] = aux[f - LEVELS, 8:16, :]

    rows_of(fixed, 0, AT_COUPLING, coupling[...])
    rows_of(fixed, 1, AT_MASK, mask[...].astype(F32))
    rows_of(fixed, 2, AT_LAND, land[...])
    for t in range(SUB - 1):
        rows_of(g, t, AT_GUESS + t, guess[t].astype(F32))
    g[SUB - 1, 8 : 8 + CX, :CY] = guess[SUB - 1].astype(F32)

    side = slice(CY, COLS)
    slot = {AT_COUPLING: 0, AT_MASK: 1, AT_LAND: 2}

    def put(f, tile, value):
        rows = slice(tile * 8, tile * 8 + 8)
        if f < LEVELS:
            s0[f, tile * 8 + 8 : tile * 8 + 16, side] = value
        elif f < AT_GUESS:
            fixed[slot[f], rows, side] = value
        else:
            g[f - AT_GUESS, rows, side] = value

    fields = [*range(CONE), *range(LEVELS, N_FIELDS)]
    place_sides(put, fields, one, three, even, first, last)
    g[SUB - 1, :, side] = jnp.zeros((BAND, LANES), F32)
    fixed[2] = (1.0 - fixed[1]) * fixed[2]
    for l in range(SUB):
        for i, start in ((l, 0), (SUB + l, LEVELS)):
            rows, cols = coefficient_place(i)
            fixed[3, rows, cols] = coeff[start + l]
    write(fixed, fixed_out)

    for t in range(SUB):
        src, dst = (s0, s1) if t % 2 == 0 else (s1, s0)

        for r in range(*strips(t)):
            strip = Strip(r, first, last)
            h = strip.spread(src, 0, diff[0])
            u_prev = None
            for l in range(SUB - t):
                h_next = strip.spread(src, l + 1, diff[l + 1])
                u = flux_between(mix[l], h_next, h)
                v = added(h, u)
                if l == t and t < 3:
                    strip.save(us, t, v)
                    if t:
                        strip.save(hs, t - 1, h)
                if u_prev is not None:
                    v = less(v, u_prev)
                if l == 0:
                    c, m, ml = (strip.recall(fixed, i) for i in range(3))
                    v, e = surface(v, strip.recall(g, t), c, m, ml, ocean)
                    strip.save(emitted, t, e[:OWN_TILES])
                if t < SUB - 1:
                    strip.store(dst, l, v)
                h, u_prev = h_next, u
            strip.save(hd, t, h)
            strip.save(ud, t, u_prev)
            if t == 3:
                strip.save(hs, 2, h)
        if t < 3:
            write(us.at[t], us_out.at[t])
        if 0 < t < 4:
            write(hs.at[t - 1], hs_out.at[t - 1])

    write_series(series, emitted)
    for c in writes:
        c.wait()


def first_rest(
    coeff, state, upper, lower, one, three, hd, ud,
    final, hs_out, us_out, token,
    s0, s1, hs, us, sems,
):
    diff, mix = coefficients(coeff)
    token[...] = jnp.zeros_like(token)
    even, first, last = position()
    zero_pads(s0, LEVELS)
    zero_pads(s1, LEVELS)
    for l in range(CONE, LEVELS):
        place_rows(s0.at[l], state[l], upper[l], lower[l])

    def put(f, tile, value):
        s0[f, tile * 8 + 8 : tile * 8 + 16, CY:COLS] = value

    place_sides(put, list(range(CONE, LEVELS)), one, three, even, first, last)

    for t in range(SUB):
        src, dst = (s0, s1) if t % 2 == 0 else (s1, s0)

        for r in range(*strips(t)):
            strip = Strip(r, first, last)
            h = strip.recall(hd, t)
            u_prev = strip.recall(ud, t)
            for l in range(SUB - t, LEVELS):
                if l < LEVELS - 1:
                    h_next = strip.spread(src, l + 1, diff[l + 1])
                    u = flux_between(mix[l], h_next, h)
                    v = added(h, u)
                else:
                    h_next = u = None
                    v = h
                if l == t and t >= 3:
                    strip.save(us, t - 3, v)
                    strip.save(hs, t - 3, h)
                v = less(v, u_prev)
                if t < SUB - 1:
                    strip.store(dst, l, v)
                elif l >= SUB:
                    rows = slice(r * 8 - 16, r * 8 - 8)
                    for k in range(OWN_TILES):
                        final[l, rows, k * LANES : (k + 1) * LANES] = v[k]
                h, u_prev = h_next, u
    writes = [
        pltpu.make_async_copy(hs, hs_out, sems.at[0]),
        pltpu.make_async_copy(us, us_out, sems.at[1]),
    ]
    for c in writes:
        c.start()
    for c in writes:
        c.wait()


def balance(
    diff, mix, src, pat, weights, mask, after,
    out, wet, coeff,
    m, z, b, sem, *totals,
):
    del after
    for l in range(LEVELS):
        coeff[l] = jnp.full((8, LANES), diff[l], F32)
    for l in range(LEVELS - 1):
        coeff[LEVELS + l] = jnp.full((8, LANES), mix[l], F32)
    coeff[2 * LEVELS - 1] = jnp.zeros((8, LANES), F32)
    count = jnp.zeros((8, LANES), F32)
    for part in range(CX // 8):
        for j in range(OWN_TILES):
            v = mask[part * 8 : part * 8 + 8, j * LANES : (j + 1) * LANES].astype(F32)
            count += v
            m[pl.ds(part * 8 * OWN_TILES + j, 8, stride=OWN_TILES), :] = v
    _, lane = iotas()
    count = jnp.sum(count, axis=(0, 1), keepdims=True)
    wet[...] = jnp.where(lane[:1] == SUB, count, 0.0)
    blocks = m[...].astype(BF16)

    @pl.loop(0, PATTERNS, unroll=8)
    def _(p):
        z[p] = lax.dot_general(
            blocks, weights[p], (((1,), (1,)), ((), ())), preferred_element_type=F32
        )

    for j in range(OWN_TILES):
        totals[j][...] = jnp.zeros_like(totals[j])

    @pl.loop(0, CX, unroll=4)
    def _(r):
        for k in range(2):
            for j in range(OWN_TILES):
                row = pl.ds(src[j, k, r], 1)
                line = z[pat[j, k, r], pl.ds(r * OWN_TILES + j, 1), :]
                totals[j][row, :] = totals[j][row, :] + line

    m[...] = m[...] - ((totals[0][...] + totals[1][...]) + (totals[2][...] + totals[3][...]))
    for part in range(CX // 8):
        for j in range(OWN_TILES):
            v = m[pl.ds(part * 8 * OWN_TILES + j, 8, stride=OWN_TILES), :]
            b[part * 8 : part * 8 + 8, j * LANES : (j + 1) * LANES] = v
    c = pltpu.make_async_copy(b, out, sem)
    c.start()
    c.wait()


def losses(
    received_in, factor, wet, before,
    gap, token,
    received, rows, sems,
):
    del before
    token[...] = jnp.zeros_like(token)
    c = pltpu.make_async_copy(received_in, received, sems.at[0])
    c.start()
    c.wait()
    partial = [jnp.zeros((8, LANES), F32) for _ in range(SUB)]
    for half in range(CX // 16):
        for j in range(OWN_TILES):
            cols = slice(j * LANES, (j + 1) * LANES)
            f = factor[half * 16 : half * 16 + 16, cols]
            for t in range(SUB):
                p = f * received[t, half * 16 : half * 16 + 16, cols].astype(F32)
                partial[t] += p[:8] + p[8:]
    row, lane = iotas()
    total = jnp.zeros((8, LANES), F32)
    for t, value in enumerate(partial):
        total = jnp.where(row == t, jnp.sum(value, axis=0, keepdims=True), total)
    total = jnp.sum(total, axis=1, keepdims=True)
    total = jnp.sum(jnp.where(row == lane, total, 0.0), axis=0, keepdims=True) + wet[...]
    for k in range(rows.shape[0]):
        rows[k] = total
    c = pltpu.make_async_copy(rows, gap, sems.at[1])
    c.start()
    c.wait()


def edge_slots():
    for t, tile, start in ((0, 0, 0), (2, 0, 5), (1, 1, 0), (3, 1, 4), (4, 1, 6)):
        yield t, SUB - 1 - t, tile, start


def regrid(
    src, pat, received_in, weights_in, before,
    out, top, bottom,
    x, y, received, weights, sems,
):
    del before
    reads = [
        pltpu.make_async_copy(received_in, received, sems.at[0]),
        pltpu.make_async_copy(weights_in, weights, sems.at[1]),
    ]
    for c in reads:
        c.start()
    reads[0].wait()
    for half in range(CX // 16):
        for j in range(OWN_TILES):
            cols = slice(j * LANES, (j + 1) * LANES)
            for t in range(SUB):
                v16 = received[t, half * 16 : half * 16 + 16, cols].astype(F32)
                for part in range(2):
                    row = half * 16 + part * 8
                    start = (row * OWN_TILES + j) * 8 + t
                    x[pl.ds(start, 8, stride=OWN_TILES * 8), :] = v16[part * 8 : part * 8 + 8]
    reads[1].wait()

    @pl.loop(0, CX, unroll=8)
    def _(r):
        for j in range(OWN_TILES):
            a, w = [], []
            for k in range(2):
                start = pl.multiple_of(src[j, k, r] * 8, 8)
                a.append(x[pl.ds(start, 8), :].astype(BF16))
                w.append(weights[pat[j, k, r]])
            product = jnp.dot(
                jnp.concatenate(a, 1), jnp.concatenate(w, 0), preferred_element_type=F32
            )
            y[pl.ds(r * OWN_TILES + j, 8, stride=BLOCKS), :] = product

    for part in range(CX // 8):
        for j in range(OWN_TILES):
            cols = slice(j * LANES, (j + 1) * LANES)
            for t in range(SUB):
                start = t * BLOCKS + part * 8 * OWN_TILES + j
                out[t, part * 8 : part * 8 + 8, cols] = y[pl.ds(start, 8, stride=OWN_TILES), :]
    top[1, 7:8, :] = jnp.zeros((1, CY), F32)
    bottom[1, 7:8, :] = jnp.zeros((1, CY), F32)
    for t, n, tile, start in edge_slots():
        top[tile, start : start + n, :] = out[t, 0:n, :]
        bottom[tile, start : start + n, :] = out[t, CX - n : CX, :]


def halo_rows(halo, upper, lower):
    halo[...] = jnp.zeros_like(halo)
    for t, n, tile, start in edge_slots():
        halo[t, 8 - n : 8, :] = upper[tile, start : start + n, :]
        halo[t, 8 : 8 + n, :] = lower[tile, start : start + n, :]


def pack_second(out, upper, lower, one, three, halo):
    even, _, _ = position()
    halo_rows(halo, upper, lower)

    def field(t):
        def of(tile):
            if tile in (0, 5):
                block, rows = halo.at[t], slice(0, 8) if tile == 0 else slice(8, 16)
            else:
                block, rows = out.at[t], slice(tile * 8 - 8, tile * 8)
            return block[rows, :LANES], block[rows, CY - LANES :]

        return of

    pack_columns([field(t) for t in range(SUB - 1)], one, three, even)


def gap_means(gap):
    total = jnp.sum(gap[...], axis=0)
    lane = lax.broadcasted_iota(jnp.int32, (1, LANES), 1)
    wet = jnp.sum(jnp.where(lane == SUB, total, 0.0), axis=1, keepdims=True)
    return [
        jnp.sum(jnp.where(lane == t, total, 0.0), axis=1, keepdims=True) / wet for t in range(SUB)
    ]


def second_cone(
    fixed_in, regridded, upper, lower, one, three, gap, hs_in, us_in,
    series, final0, hx, ux, coeff,
    s0, s1, g, emitted, fixed, hs, us, halo, sems,
):
    reads = []
    pairs = ((us_in, us), (fixed_in, fixed), (hs_in, hs))
    for i, (src, dst) in enumerate(pairs):
        reads.append(pltpu.make_async_copy(src, dst, sems.at[i]))
        reads[-1].start()
    even, first, last = position()
    ocean = lax.axis_index("comp") == 1
    zero_pads(s0, 3)
    zero_pads(s1, 3)
    halo_rows(halo, upper, lower)
    for t in range(SUB):
        if t < SUB - 1:
            g[t, 0:8, :CY] = halo[t, 0:8, :]
            g[t, 8 + CX : 16 + CX, :CY] = halo[t, 8:16, :]
        g[t, 8 : 8 + CX, :CY] = regridded[t]

    def put(f, tile, value):
        g[f, tile * 8 : tile * 8 + 8, CY:COLS] = value

    place_sides(put, list(range(SUB - 1)), one, three, even, first, last)
    g[SUB - 1, :, CY:COLS] = jnp.zeros((BAND, LANES), F32)
    means = [jnp.broadcast_to(v, (8, LANES)) for v in gap_means(gap)]
    for c in reads:
        c.wait()
    for l in range(SUB):
        for i, start in ((l, 0), (SUB + l, LEVELS)):
            coeff[start + l] = fixed[(3, *coefficient_place(i))]
    diff, mix = coefficients(coeff)

    for t in range(SUB):
        src, dst = (s0, s1) if t % 2 == 0 else (s1, s0)

        for r in range(*strips(t)):
            strip = Strip(r, first, last)
            h = strip.spread(src, 0, diff[0]) if t else None
            u_prev = None
            for l in range(min(t, SUB - 1 - t) + 1):
                if l < t:
                    if l + 1 < t:
                        h_next = strip.spread(src, l + 1, diff[l + 1])
                    else:
                        h_next = strip.recall(hs, t - 1)
                    u = flux_between(mix[l], h_next, h)
                    v = added(h, u)
                else:
                    v = strip.recall(us, t)
                if u_prev is not None:
                    v = less(v, u_prev)
                if l == 0:
                    c, m, ml = (strip.recall(fixed, i) for i in range(3))
                    f = [a + b * means[t] for a, b in zip(strip.recall(g, t), m)]
                    v, e = surface(v, f, c, m, ml, ocean)
                    strip.save(emitted, t, e[:OWN_TILES])
                    if t == SUB - 1:
                        rows = slice(r * 8 - 16, r * 8 - 8)
                        for k in range(OWN_TILES):
                            final0[rows, k * LANES : (k + 1) * LANES] = v[k]
                if t < SUB - 1:
                    strip.store(dst, l, v)
                if l < t:
                    h, u_prev = h_next, u
            if t >= 3:
                strip.save(hx, t - 3, h)
                strip.save(ux, t - 3, u_prev)

    write_series(series, emitted)


def second_rest(
    coeff, hx, ux, hs_in, us_in, final0, whole,
    final, token,
    s0, s1, hs, us, sems,
):
    del whole
    diff, mix = coefficients(coeff)
    reads = [
        pltpu.make_async_copy(us_in, us, sems.at[0]),
        pltpu.make_async_copy(hs_in, hs, sems.at[1]),
    ]
    for c in reads:
        c.start()
    token[...] = jnp.zeros_like(token)
    gy = lax.axis_index("gy")
    first, last = gy == 0, gy == lax.axis_size("gy") - 1
    zero_pads(s0, SUB)
    zero_pads(s1, SUB)
    final[0] = final0[...]
    for c in reads:
        c.wait()
    for t in range(3, SUB):
        src, dst = (s0, s1) if t % 2 == 0 else (s1, s0)

        for r in range(*strips(t)):
            strip = Strip(r, first, last)
            h = strip.recall(hx, t - 3)
            u_prev = strip.recall(ux, t - 3)
            for l in range(SUB - t, t + 1):
                if l < t:
                    if l + 1 < t:
                        h_next = strip.spread(src, l + 1, diff[l + 1])
                    else:
                        h_next = strip.recall(hs, t - 3)
                    u = flux_between(mix[l], h_next, h)
                    v = added(h, u)
                    h = h_next
                else:
                    u = None
                    v = strip.recall(us, t - 3)
                v = less(v, u_prev)
                u_prev = u
                if t < SUB - 1:
                    strip.store(dst, l, v)
                else:
                    rows = slice(r * 8 - 16, r * 8 - 8)
                    for k in range(OWN_TILES):
                        final[l, rows, k * LANES : (k + 1) * LANES] = v[k]


def finish(regridded, mask, gap, forcing):
    for t, mean in enumerate(gap_means(gap)):
        forcing[t] = regridded[t] + mask[...].astype(F32) * mean


def shifted(value, axis, by):
    n = lax.axis_size(axis)
    return lax.ppermute(value, axis, [(i, (i + by) % n) for i in range(n)])


def paired(value, axis, mask):
    return lax.ppermute(value, axis, [(i, i ^ mask) for i in range(lax.axis_size(axis))])


def per_device(
    state, guess, diffusion, mixing, coupling, land_temp, land_mask, weights, source_block, pattern
):
    state, guess, diff, mix, coupling = state[0], guess[0], diffusion[0], mixing[0], coupling[0]
    weights = weights[0]
    src = source_block[0].transpose(1, 2, 0)
    pat = pattern[0].transpose(1, 2, 0)
    peers = lax.axis_size("gx") * lax.axis_size("gy")
    band = lambda n: shape(n, BAND, COLS)
    field_buf = lambda n: pltpu.VMEM((n, ROWS, COLS), F32)
    band_buf = lambda n: pltpu.VMEM((n, BAND, COLS), F32)
    numbers = shape(2 * LEVELS, 8, LANES)

    message = shape(LEVELS, 8, CY)
    to_lower, to_upper = call(
        first_edges,
        [message, message],
        [
            pltpu.VMEM((AUX, 8, CY), F32),
            pltpu.VMEM((AUX, 8, CY), F32),
            pltpu.VMEM((2, 8, CY), jnp.int32),
            pltpu.VMEM((2, SUB - 1, 16, CY), BF16),
            pltpu.SemaphoreType.DMA((10,)),
        ],
        [HBM] * 5,
        grant=EDGE_GRANT,
    )(state, guess, coupling, land_temp, land_mask)
    state, guess, coupling, land_temp, mask, table, src, pat, to_lower, to_upper = (
        lax.optimization_barrier(
            (
                state, guess, coupling, land_temp, land_mask, weights, src, pat,
                to_lower, to_upper,
            )
        )
    )
    lower, upper = shifted(to_lower, "gx", -1), shifted(to_upper, "gx", 1)
    factor, wet, coeff = call(
        balance,
        [shape(CX, CY), shape(1, LANES), shape(2 * LEVELS, 8, LANES)],
        [
            pltpu.VMEM((BLOCKS, LANES), F32),
            pltpu.VMEM((PATTERNS, BLOCKS, LANES), F32),
            pltpu.VMEM((CX, CY), F32),
            pltpu.SemaphoreType.DMA(()),
            *[pltpu.VMEM((BLOCKS, LANES), F32)] * OWN_TILES,
        ],
        [SM, SM, SM, SM, VM, VM, VM],
        out_specs=[HBM, VM, VM],
    )(diff, mix, src, pat, table, mask, to_lower)
    packed = shape(BAND, PACK_LANES)
    aux, one, three = call(pack_first, [shape(AUX, 16, CY), packed, packed], [], [VM] * 8)(
        state, guess, coupling, land_temp, mask, upper, lower, wet
    )
    one, three = paired(one, "gy", 1), paired(three, "gy", 3)

    series, hd, ud, hs, us, fixed = call(
        first_cone,
        [
            shape(SUB, CX, CY, dtype=BF16), band(SUB), band(SUB),
            band(3), band(3), band(4),
        ],
        [
            field_buf(CONE), field_buf(CONE), band_buf(SUB), band_buf(SUB),
            band_buf(3), band_buf(3), band_buf(4), pltpu.SemaphoreType.DMA((7,)),
        ],
        [VM] * 11,
        out_specs=[VM] * 3 + [HBM] * 3,
    )(coeff, state, guess, coupling, land_temp, mask, upper, lower, aux, one, three)

    def exchange(series, before):
        received = paired(series, "comp", 1)
        gap, after = call(
            losses,
            [shape(peers, 1, LANES), shape(8, LANES)],
            [
                pltpu.VMEM((SUB, CX, CY), BF16),
                pltpu.VMEM((peers, 1, LANES), F32),
                pltpu.SemaphoreType.DMA((2,)),
            ],
            [HBM, VM, VM, VM],
            out_specs=[HBM, VM],
        )(received, factor, wet, before)
        gap = lax.all_to_all(gap, ("gx", "gy"), 0, 0)
        edges = shape(2, 8, CY)
        out, top, bottom = call(
            regrid,
            [shape(SUB, CX, CY), edges, edges],
            [
                pltpu.VMEM((BLOCKS * 8, LANES), F32),
                pltpu.VMEM((BLOCKS * 8, LANES), F32),
                pltpu.VMEM((SUB, CX, CY), BF16),
                pltpu.VMEM((PATTERNS, LANES, LANES), BF16),
                pltpu.SemaphoreType.DMA((2,)),
            ],
            [SM, SM, HBM, HBM, VM],
            cost_estimate=pl.CostEstimate(
                flops=2 * BLOCKS * 8 * 2 * LANES * LANES,
                bytes_accessed=BLOCKS * 2 * LANES * LANES * 2,
                transcendentals=0,
            ),
        )(src, pat, received, weights, after)
        return out, top, bottom, gap

    whole, hs_rest, us_rest, token = call(
        first_rest,
        [shape(LEVELS, CX, CY), band(3), band(3), shape(8, LANES)],
        [
            field_buf(LEVELS), field_buf(LEVELS),
            band_buf(3), band_buf(3), pltpu.SemaphoreType.DMA((2,)),
        ],
        [VM] * 8,
        out_specs=[VM, HBM, HBM, VM],
    )(coeff, state, upper, lower, one, three, hd, ud)

    out, top, bottom, gap = exchange(series, token)
    lower, upper = shifted(top, "gx", -1), shifted(bottom, "gx", 1)
    packed = shape(BAND, LANES)
    one, three = call(
        pack_second, [packed, packed], [pltpu.VMEM((SUB - 1, 16, CY), F32)], [VM] * 3
    )(out, upper, lower)
    one, three = paired(one, "gy", 1), paired(three, "gy", 3)

    series, final0, hx, ux, coeff = call(
        second_cone,
        [shape(SUB, CX, CY, dtype=BF16), shape(CX, CY), band(3), band(3), numbers],
        [
            field_buf(3), field_buf(3), band_buf(SUB), band_buf(SUB),
            band_buf(4), band_buf(3), band_buf(3), pltpu.VMEM((SUB - 1, 16, CY), F32),
            pltpu.SemaphoreType.DMA((3,)),
        ],
        [HBM] + [VM] * 6 + [HBM, HBM],
    )(fixed, out, upper, lower, one, three, gap, hs, us)

    whole, token = call(
        second_rest,
        [shape(LEVELS, CX, CY), shape(8, LANES)],
        [
            field_buf(SUB), field_buf(SUB),
            band_buf(3), band_buf(3), pltpu.SemaphoreType.DMA((2,)),
        ],
        [VM, VM, VM, HBM, HBM, VM, pl.BlockSpec(memory_space=pl.ANY)],
        out_specs=[pl.BlockSpec((SUB, CX, CY), lambda i: (0, 0, 0)), VM],
        grid=(1,),
        input_output_aliases={6: 0},
    )(coeff, hx, ux, hs_rest, us_rest, final0, whole)

    out, _, _, gap = exchange(series, token)
    (forcing,) = call(finish, [shape(SUB, CX, CY)], [], [VM] * 3)(out, land_mask, gap)
    return whole[None], forcing[None]


def solution(mesh):
    placed = (
        P("comp", None, "gx", "gy"),
        P("comp", None, "gx", "gy"),
        P("comp", None),
        P("comp", None),
        P("comp", "gx", "gy"),
        P("gx", "gy"),
        P("gx", "gy"),
        P("comp", ("gx", "gy"), None, None),
        P("comp", "gx", "gy", None),
        P("comp", "gx", "gy", None),
    )
    return jax.shard_map(
        per_device,
        mesh=mesh,
        in_specs=placed,
        out_specs=(P("comp", None, "gx", "gy"), P("comp", None, "gx", "gy")),
        check_vma=False,
    )
```

```python
import jax
import jax.numpy as jnp
from jax import lax
from jax.experimental import pallas as pl
from jax.experimental.pallas import tpu as pltpu
from jax.sharding import PartitionSpec as P

F32 = jnp.float32
BF16 = jnp.bfloat16
SUB = 6
LEVELS = 16
CX = 32
CY = 512
LANES = 128
OWN_TILES = CY // LANES
COLS = CY + LANES
ROWS = CX + 32
BAND = CX + 16
PATTERNS = 32
BLOCKS = CX * OWN_TILES
VMEM_LIMIT = 12 * 1024 * 1024
EDGE_GRANT = 60 * 1024 * 1024

N_FIELDS = LEVELS + 3 + SUB - 1
AT_COUPLING, AT_LAND, AT_MASK, AT_GUESS = LEVELS, LEVELS + 1, LEVELS + 2, LEVELS + 3
PACK_LANES = 256

VM = pl.BlockSpec(memory_space=pltpu.VMEM)
SM = pl.BlockSpec(memory_space=pltpu.SMEM)
HBM = pl.BlockSpec(memory_space=pltpu.HBM)


def shape(*dims, dtype=F32):
    return jax.ShapeDtypeStruct(dims, dtype)


def call(body, outs, scratch, ins, out_specs=None, grant=VMEM_LIMIT, **kw):
    return pl.pallas_call(
        body,
        out_shape=outs,
        in_specs=ins,
        out_specs=[VM] * len(outs) if out_specs is None else out_specs,
        scratch_shapes=scratch,
        compiler_params=pltpu.CompilerParams(vmem_limit_bytes=grant),
        **kw,
    )


def iotas():
    row = lax.broadcasted_iota(jnp.int32, (8, LANES), 0)
    lane = lax.broadcasted_iota(jnp.int32, (8, LANES), 1)
    return row, lane


def roll_lanes(x, shift):
    shift %= LANES
    return x if shift == 0 else pltpu.roll(x, shift, 1)


def pack_columns(fields, one, three, even):
    _, lane = iotas()
    groups = PACK_LANES // LANES if len(fields) > 16 else 1
    for tile in range(6):
        for g in range(groups):
            left = jnp.zeros((8, LANES), F32)
            right = jnp.zeros((8, LANES), F32)
            for f in range(g * 16, min(len(fields), g * 16 + 16)):
                at = (f % 16) * 8
                head, tail = fields[f](tile)
                left = jnp.where((lane >= at) & (lane < at + 8), roll_lanes(head, at), left)
                right = jnp.where((lane >= at) & (lane < at + 8), roll_lanes(tail, at + 8), right)
            span = (slice(tile * 8, tile * 8 + 8), slice(g * LANES, (g + 1) * LANES))
            one[span] = jnp.where(even, right, left)
            three[span] = jnp.where(even, left, right)


def side_halos(one, three, even, first, last, tile, g):
    span = (slice(tile * 8, tile * 8 + 8), slice(g * LANES, (g + 1) * LANES))
    a, b = one[span], three[span]
    right = jnp.where(last, 0.0, jnp.where(even, a, b))
    left = jnp.where(first, 0.0, jnp.where(even, b, a))
    return right, left


def side_tile(right, left, f, lane):
    at = (f % 16) * 8
    return jnp.where(
        lane < 6,
        roll_lanes(right, -at),
        jnp.where(lane >= LANES - 6, roll_lanes(left, LANES - 8 - at), 0.0),
    )


def place_sides(dst_of, fields, one, three, even, first, last):
    _, lane = iotas()
    for tile in range(6):
        packs = {}
        for f in fields:
            g = f // 16
            if g not in packs:
                packs[g] = side_halos(one, three, even, first, last, tile, g)
            dst_of(f, tile, side_tile(*packs[g], f, lane))


def place_rows(dst, own, upper, lower):
    dst[8:16, :CY] = upper
    dst[16 : 16 + CX, :CY] = own
    dst[16 + CX : 24 + CX, :CY] = lower


def zero_pads(ref, count):
    for l in range(count):
        ref[l, 0:8, :] = jnp.zeros((8, COLS), F32)
        ref[l, ROWS - 8 : ROWS, :] = jnp.zeros((8, COLS), F32)


def position():
    gy = lax.axis_index("gy")
    return gy % 2 == 0, gy == 0, gy == lax.axis_size("gy") - 1


class Strip:
    def __init__(self, r, first, last):
        self.r = r
        row, lane = iotas()
        self.row_first, self.row_last = row == 0, row == 7
        self.lane_first, self.lane_last = lane == 0, lane == LANES - 1
        self.inside = ((lane < 6) & jnp.logical_not(last)) | (
            (lane >= LANES - 6) & jnp.logical_not(first)
        )

    def load(self, ref, l, shift=0):
        rows = slice(self.r * 8 + shift, self.r * 8 + shift + 8)
        return [ref[l, rows, k * LANES : (k + 1) * LANES] for k in range(OWN_TILES + 1)]

    def spread(self, ref, l, d):
        x = self.load(ref, l)
        above = self.load(ref, l, -8)
        below = self.load(ref, l, 8)
        out = []
        n = len(x)
        for k in range(n):
            c = x[k]
            up = pltpu.roll(jnp.where(self.row_last, above[k], c), 1, 0)
            down = pltpu.roll(jnp.where(self.row_first, below[k], c), 7, 0)
            left = pltpu.roll(jnp.where(self.lane_last, x[k - 1], c), 1, 1)
            right = pltpu.roll(jnp.where(self.lane_first, x[(k + 1) % n], c), LANES - 1, 1)
            out.append(c + d * (((up + down) + (left + right)) - 4.0 * c))
        return out

    def store(self, ref, l, values):
        rows = slice(self.r * 8, self.r * 8 + 8)
        for k, v in enumerate(values):
            if k == OWN_TILES:
                v = jnp.where(self.inside, v, 0.0)
            ref[l, rows, k * LANES : (k + 1) * LANES] = v

    def save(self, ref, l, values):
        rows = slice(self.r * 8 - 8, self.r * 8)
        for k, v in enumerate(values):
            ref[l, rows, k * LANES : (k + 1) * LANES] = v

    def recall(self, ref, l):
        return self.load(ref, l, -8)


def flux_between(mix, lower, upper):
    return [mix * (a - b) for a, b in zip(lower, upper)]


def added(a, b):
    return [x + y for x, y in zip(a, b)]


def less(a, b):
    return [x - y for x, y in zip(a, b)]


def surface(v, f, c, m, ml, ocean):
    new, emitted = [], []
    for vk, fk, ck, mk, lk in zip(v, f, c, m, ml):
        mf = mk * fk
        flux = ck * (vk - (mf + lk))
        warmed = vk + ck * mf
        new.append(jnp.where(ocean, warmed, vk - flux))
        emitted.append(jnp.where(ocean, mk * warmed, flux))
    return new, emitted


def coefficient_place(i):
    rows, cols = i // 5 * 8, i % 5 * LANES
    return slice(rows, rows + 8), slice(cols, cols + LANES)


class Rows:
    def __init__(self, ref, start):
        self.ref, self.start = ref, start

    def __getitem__(self, l):
        return self.ref[self.start + l]


def coefficients(coeff):
    return Rows(coeff, 0), Rows(coeff, LEVELS)


def strips(t):
    return (1, 7) if t < SUB - 1 else (2, 6)


def write_series(series, emitted):
    for t in range(SUB):
        for half in range(CX // 16):
            rows = slice(8 + half * 16, 24 + half * 16)
            series[t, half * 16 : half * 16 + 16, :] = emitted[t, rows, :CY].astype(BF16)


AUX = 3 + SUB - 1


def aux_slots():
    n = 0
    for a in range(AUX):
        for i in range(SUB - 1 if a < 3 else SUB - 1 - (a - 3)):
            yield a, i, n // 2, n % 2
            n += 1


def first_edges(
    state, guess, coupling, land, mask,
    to_lower, to_upper,
    head, tail, ints, short, sems,
):
    n = 0
    copies = []

    def copy(src, dst):
        nonlocal n
        c = pltpu.make_async_copy(src, dst, sems.at[n])
        c.start()
        copies.append(c)
        n += 1

    for side, msg, buf in ((0, to_lower, head), (1, to_upper, tail)):
        rows = pl.ds(side * (CX - 8), 8)
        copy(state.at[:, rows, :], msg)
        copy(coupling.at[rows, :], buf.at[0])
        copy(land.at[rows, :], buf.at[1])
        copy(mask.at[rows, :], ints.at[side])
        copy(guess.at[pl.ds(0, SUB - 1), pl.ds(side * (CX - 16), 16), :], short.at[side])
    for c in copies:
        c.wait()
    for side, buf in ((0, head), (1, tail)):
        buf[2] = ints[side].astype(F32)
        for t in range(SUB - 1):
            rows16 = short[side, t].astype(F32)
            buf[3 + t] = rows16[8:] if side else rows16[:8]
    for a, i, tile, spare in aux_slots():
        to_lower[tile, 6 + spare : 7 + spare, :] = head[a, i : i + 1, :]
        to_upper[tile, spare : spare + 1, :] = tail[a, 7 - i : 8 - i, :]


def pack_first(
    state, guess, coupling, land, mask, upper, lower, before,
    aux, one, three,
):
    del before
    even, _, _ = position()
    aux[...] = jnp.zeros_like(aux)
    for a, i, tile, spare in aux_slots():
        aux[a, 7 - i : 8 - i, :] = upper[tile, spare : spare + 1, :]
        aux[a, 8 + i : 9 + i, :] = lower[tile, 6 + spare : 7 + spare, :]

    def field(f):
        def of(tile):
            rows = slice(0, 8)
            if tile in (0, 5):
                if f < LEVELS:
                    block = upper.at[f] if tile == 0 else lower.at[f]
                else:
                    block = aux.at[f - LEVELS]
                    rows = slice(0, 8) if tile == 0 else slice(8, 16)
            else:
                rows = slice(tile * 8 - 8, tile * 8)
                if f < LEVELS:
                    block = state.at[f]
                elif f == AT_COUPLING:
                    block = coupling
                elif f == AT_LAND:
                    block = land
                elif f == AT_MASK:
                    block = mask
                else:
                    block = guess.at[f - AT_GUESS]
                    base = (tile - 1) // 2 * 16
                    part = slice((tile - 1) % 2 * 8, (tile - 1) % 2 * 8 + 8)
                    head = block[base : base + 16, :LANES].astype(F32)[part]
                    tail = block[base : base + 16, CY - LANES :].astype(F32)[part]
                    return head, tail
            head, tail = block[rows, :LANES], block[rows, CY - LANES :]
            return head.astype(F32), tail.astype(F32)

        return of

    pack_columns([field(f) for f in range(N_FIELDS)], one, three, even)


CONE = SUB + 1


def first_cone(
    coeff, state, guess, coupling, land, mask, upper, lower, aux, one, three, beside,
    series, hd, ud, hs_out, us_out, fixed_out,
    s0, s1, g, emitted, hs, us, fixed, sems,
):
    del beside
    diff, mix = coefficients(coeff)
    writes = []

    def write(src, dst):
        c = pltpu.make_async_copy(src, dst, sems.at[len(writes)])
        c.start()
        writes.append(c)

    even, first, last = position()
    ocean = lax.axis_index("comp") == 1
    zero_pads(s0, CONE)
    zero_pads(s1, CONE - 1)
    for l in range(CONE):
        place_rows(s0.at[l], state[l], upper[l], lower[l])

    def rows_of(ref, k, f, own):
        ref[k, 0:8, :CY] = aux[f - LEVELS, 0:8, :]
        ref[k, 8 : 8 + CX, :CY] = own
        ref[k, 8 + CX : 16 + CX, :CY] = aux[f - LEVELS, 8:16, :]

    rows_of(fixed, 0, AT_COUPLING, coupling[...])
    rows_of(fixed, 1, AT_MASK, mask[...].astype(F32))
    rows_of(fixed, 2, AT_LAND, land[...])
    for t in range(SUB - 1):
        rows_of(g, t, AT_GUESS + t, guess[t].astype(F32))
    g[SUB - 1, 8 : 8 + CX, :CY] = guess[SUB - 1].astype(F32)

    side = slice(CY, COLS)
    slot = {AT_COUPLING: 0, AT_MASK: 1, AT_LAND: 2}

    def put(f, tile, value):
        rows = slice(tile * 8, tile * 8 + 8)
        if f < LEVELS:
            s0[f, tile * 8 + 8 : tile * 8 + 16, side] = value
        elif f < AT_GUESS:
            fixed[slot[f], rows, side] = value
        else:
            g[f - AT_GUESS, rows, side] = value

    fields = [*range(CONE), *range(LEVELS, N_FIELDS)]
    place_sides(put, fields, one, three, even, first, last)
    g[SUB - 1, :, side] = jnp.zeros((BAND, LANES), F32)
    fixed[2] = (1.0 - fixed[1]) * fixed[2]
    for l in range(SUB):
        for i, start in ((l, 0), (SUB + l, LEVELS)):
            rows, cols = coefficient_place(i)
            fixed[3, rows, cols] = coeff[start + l]
    write(fixed, fixed_out)

    for t in range(SUB):
        src, dst = (s0, s1) if t % 2 == 0 else (s1, s0)

        for r in range(*strips(t)):
            strip = Strip(r, first, last)
            h = strip.spread(src, 0, diff[0])
            u_prev = None
            for l in range(SUB - t):
                h_next = strip.spread(src, l + 1, diff[l + 1])
                u = flux_between(mix[l], h_next, h)
                v = added(h, u)
                if l == t and t < 3:
                    strip.save(us, t, v)
                    if t:
                        strip.save(hs, t - 1, h)
                if u_prev is not None:
                    v = less(v, u_prev)
                if l == 0:
                    c, m, ml = (strip.recall(fixed, i) for i in range(3))
                    v, e = surface(v, strip.recall(g, t), c, m, ml, ocean)
                    strip.save(emitted, t, e[:OWN_TILES])
                if t < SUB - 1:
                    strip.store(dst, l, v)
                h, u_prev = h_next, u
            strip.save(hd, t, h)
            strip.save(ud, t, u_prev)
            if t == 3:
                strip.save(hs, 2, h)
        if t < 3:
            write(us.at[t], us_out.at[t])
        if 0 < t < 4:
            write(hs.at[t - 1], hs_out.at[t - 1])

    write_series(series, emitted)
    for c in writes:
        c.wait()


def first_rest(
    coeff, state, upper, lower, one, three, hd, ud,
    final, hs_out, us_out, token,
    s0, s1, hs, us, sems,
):
    diff, mix = coefficients(coeff)
    token[...] = jnp.zeros_like(token)
    even, first, last = position()
    zero_pads(s0, LEVELS)
    zero_pads(s1, LEVELS)
    for l in range(CONE, LEVELS):
        place_rows(s0.at[l], state[l], upper[l], lower[l])

    def put(f, tile, value):
        s0[f, tile * 8 + 8 : tile * 8 + 16, CY:COLS] = value

    place_sides(put, list(range(CONE, LEVELS)), one, three, even, first, last)

    for t in range(SUB):
        src, dst = (s0, s1) if t % 2 == 0 else (s1, s0)

        for r in range(*strips(t)):
            strip = Strip(r, first, last)
            h = strip.recall(hd, t)
            u_prev = strip.recall(ud, t)
            for l in range(SUB - t, LEVELS):
                if l < LEVELS - 1:
                    h_next = strip.spread(src, l + 1, diff[l + 1])
                    u = flux_between(mix[l], h_next, h)
                    v = added(h, u)
                else:
                    h_next = u = None
                    v = h
                if l == t and t >= 3:
                    strip.save(us, t - 3, v)
                    strip.save(hs, t - 3, h)
                v = less(v, u_prev)
                if t < SUB - 1:
                    strip.store(dst, l, v)
                elif l >= SUB:
                    rows = slice(r * 8 - 16, r * 8 - 8)
                    for k in range(OWN_TILES):
                        final[l, rows, k * LANES : (k + 1) * LANES] = v[k]
                h, u_prev = h_next, u
    writes = [
        pltpu.make_async_copy(hs, hs_out, sems.at[0]),
        pltpu.make_async_copy(us, us_out, sems.at[1]),
    ]
    for c in writes:
        c.start()
    for c in writes:
        c.wait()


def balance(
    diff, mix, src, pat, weights, mask, after,
    out, wet, coeff,
    m, z, b, sem, *totals,
):
    del after
    for l in range(LEVELS):
        coeff[l] = jnp.full((8, LANES), diff[l], F32)
    for l in range(LEVELS - 1):
        coeff[LEVELS + l] = jnp.full((8, LANES), mix[l], F32)
    coeff[2 * LEVELS - 1] = jnp.zeros((8, LANES), F32)
    count = jnp.zeros((8, LANES), F32)
    for part in range(CX // 8):
        for j in range(OWN_TILES):
            v = mask[part * 8 : part * 8 + 8, j * LANES : (j + 1) * LANES].astype(F32)
            count += v
            m[pl.ds(part * 8 * OWN_TILES + j, 8, stride=OWN_TILES), :] = v
    _, lane = iotas()
    count = jnp.sum(count, axis=(0, 1), keepdims=True)
    wet[...] = jnp.where(lane[:1] == SUB, count, 0.0)
    blocks = m[...].astype(BF16)

    @pl.loop(0, PATTERNS, unroll=8)
    def _(p):
        z[p] = lax.dot_general(
            blocks, weights[p], (((1,), (1,)), ((), ())), preferred_element_type=F32
        )

    for j in range(OWN_TILES):
        totals[j][...] = jnp.zeros_like(totals[j])

    @pl.loop(0, CX, unroll=4)
    def _(r):
        for k in range(2):
            for j in range(OWN_TILES):
                row = pl.ds(src[j, k, r], 1)
                line = z[pat[j, k, r], pl.ds(r * OWN_TILES + j, 1), :]
                totals[j][row, :] = totals[j][row, :] + line

    m[...] = m[...] - ((totals[0][...] + totals[1][...]) + (totals[2][...] + totals[3][...]))
    for part in range(CX // 8):
        for j in range(OWN_TILES):
            v = m[pl.ds(part * 8 * OWN_TILES + j, 8, stride=OWN_TILES), :]
            b[part * 8 : part * 8 + 8, j * LANES : (j + 1) * LANES] = v
    c = pltpu.make_async_copy(b, out, sem)
    c.start()
    c.wait()


def share_rows(series, factor, wet, rows):
    partial = [jnp.zeros((8, LANES), F32) for _ in range(SUB)]
    for half in range(CX // 16):
        for j in range(OWN_TILES):
            cols = slice(j * LANES, (j + 1) * LANES)
            f = factor[half * 16 : half * 16 + 16, cols]
            for t in range(SUB):
                p = f * series[t, half * 16 : half * 16 + 16, cols].astype(F32)
                partial[t] += p[:8] + p[8:]
    row, lane = iotas()
    total = jnp.zeros((8, LANES), F32)
    for t, value in enumerate(partial):
        total = jnp.where(row == t, jnp.sum(value, axis=0, keepdims=True), total)
    total = jnp.sum(total, axis=1, keepdims=True)
    total = jnp.sum(jnp.where(row == lane, total, 0.0), axis=0, keepdims=True) + wet[...]
    for k in range(rows.shape[0]):
        rows[k] = total


def losses(
    received, factor, wet, before,
    gap, token,
    rows, sem,
):
    del before
    token[...] = jnp.zeros_like(token)
    share_rows(received, factor, wet, rows)
    c = pltpu.make_async_copy(rows, gap, sem)
    c.start()
    c.wait()


def edge_slots():
    for t, tile, start in ((0, 0, 0), (2, 0, 5), (1, 1, 0), (3, 1, 4), (4, 1, 6)):
        yield t, SUB - 1 - t, tile, start


def regrid(
    src, pat, received, weights_in, before,
    out, top, bottom,
    x, y, weights, sem,
):
    del before
    read = pltpu.make_async_copy(weights_in, weights, sem)
    read.start()
    for half in range(CX // 16):
        for j in range(OWN_TILES):
            cols = slice(j * LANES, (j + 1) * LANES)
            for t in range(SUB):
                v16 = received[t, half * 16 : half * 16 + 16, cols].astype(F32)
                for part in range(2):
                    row = half * 16 + part * 8
                    start = (row * OWN_TILES + j) * 8 + t
                    x[pl.ds(start, 8, stride=OWN_TILES * 8), :] = v16[part * 8 : part * 8 + 8]
    read.wait()
    for r in range(CX):
        for j in range(OWN_TILES):
            a, w = [], []
            for k in range(2):
                start = pl.multiple_of(src[j, k, r] * 8, 8)
                a.append(x[pl.ds(start, 8), :].astype(BF16))
                w.append(weights[pat[j, k, r]])
            product = jnp.dot(
                jnp.concatenate(a, 1), jnp.concatenate(w, 0), preferred_element_type=F32
            )
            y[pl.ds(r * OWN_TILES + j, 8, stride=BLOCKS), :] = product

    for part in range(CX // 8):
        for j in range(OWN_TILES):
            cols = slice(j * LANES, (j + 1) * LANES)
            for t in range(SUB):
                start = t * BLOCKS + part * 8 * OWN_TILES + j
                out[t, part * 8 : part * 8 + 8, cols] = y[pl.ds(start, 8, stride=OWN_TILES), :]
    top[1, 7:8, :] = jnp.zeros((1, CY), F32)
    bottom[1, 7:8, :] = jnp.zeros((1, CY), F32)
    for t, n, tile, start in edge_slots():
        top[tile, start : start + n, :] = out[t, 0:n, :]
        bottom[tile, start : start + n, :] = out[t, CX - n : CX, :]


def halo_rows(halo, upper, lower):
    halo[...] = jnp.zeros_like(halo)
    for t, n, tile, start in edge_slots():
        halo[t, 8 - n : 8, :] = upper[tile, start : start + n, :]
        halo[t, 8 : 8 + n, :] = lower[tile, start : start + n, :]


def pack_second(out, upper, lower, one, three, halo):
    even, _, _ = position()
    halo_rows(halo, upper, lower)

    def field(t):
        def of(tile):
            if tile in (0, 5):
                block, rows = halo.at[t], slice(0, 8) if tile == 0 else slice(8, 16)
            else:
                block, rows = out.at[t], slice(tile * 8 - 8, tile * 8)
            return block[rows, :LANES], block[rows, CY - LANES :]

        return of

    pack_columns([field(t) for t in range(SUB - 1)], one, three, even)


def gap_means(gap, start, count):
    total = jnp.sum(gap[pl.ds(start, count)], axis=0)
    lane = lax.broadcasted_iota(jnp.int32, (1, LANES), 1)
    wet = jnp.sum(jnp.where(lane == SUB, total, 0.0), axis=1, keepdims=True)
    return [
        jnp.sum(jnp.where(lane == t, total, 0.0), axis=1, keepdims=True) / wet for t in range(SUB)
    ]


def second_cone(
    fixed_in, regridded, upper, lower, one, three, gap, hs_in, us_in,
    series, final0, hx, ux, coeff,
    s0, s1, g, emitted, fixed, hs, us, halo, sems,
):
    reads = []
    pairs = ((us_in, us), (fixed_in, fixed), (hs_in, hs))
    for i, (src, dst) in enumerate(pairs):
        reads.append(pltpu.make_async_copy(src, dst, sems.at[i]))
        reads[-1].start()
    even, first, last = position()
    ocean = lax.axis_index("comp") == 1
    zero_pads(s0, 3)
    zero_pads(s1, 3)
    halo_rows(halo, upper, lower)
    for t in range(SUB):
        if t < SUB - 1:
            g[t, 0:8, :CY] = halo[t, 0:8, :]
            g[t, 8 + CX : 16 + CX, :CY] = halo[t, 8:16, :]
        g[t, 8 : 8 + CX, :CY] = regridded[t]

    def put(f, tile, value):
        g[f, tile * 8 : tile * 8 + 8, CY:COLS] = value

    place_sides(put, list(range(SUB - 1)), one, three, even, first, last)
    g[SUB - 1, :, CY:COLS] = jnp.zeros((BAND, LANES), F32)
    means = [jnp.broadcast_to(v, (8, LANES)) for v in gap_means(gap, 0, gap.shape[0])]
    for c in reads:
        c.wait()
    for l in range(SUB):
        for i, start in ((l, 0), (SUB + l, LEVELS)):
            coeff[start + l] = fixed[(3, *coefficient_place(i))]
    diff, mix = coefficients(coeff)

    for t in range(SUB):
        src, dst = (s0, s1) if t % 2 == 0 else (s1, s0)

        for r in range(*strips(t)):
            strip = Strip(r, first, last)
            h = strip.spread(src, 0, diff[0]) if t else None
            u_prev = None
            for l in range(min(t, SUB - 1 - t) + 1):
                if l < t:
                    if l + 1 < t:
                        h_next = strip.spread(src, l + 1, diff[l + 1])
                    else:
                        h_next = strip.recall(hs, t - 1)
                    u = flux_between(mix[l], h_next, h)
                    v = added(h, u)
                else:
                    v = strip.recall(us, t)
                if u_prev is not None:
                    v = less(v, u_prev)
                if l == 0:
                    c, m, ml = (strip.recall(fixed, i) for i in range(3))
                    f = [a + b * means[t] for a, b in zip(strip.recall(g, t), m)]
                    v, e = surface(v, f, c, m, ml, ocean)
                    strip.save(emitted, t, e[:OWN_TILES])
                    if t == SUB - 1:
                        rows = slice(r * 8 - 16, r * 8 - 8)
                        for k in range(OWN_TILES):
                            final0[rows, k * LANES : (k + 1) * LANES] = v[k]
                if t < SUB - 1:
                    strip.store(dst, l, v)
                if l < t:
                    h, u_prev = h_next, u
            if t >= 3:
                strip.save(hx, t - 3, h)
                strip.save(ux, t - 3, u_prev)

    write_series(series, emitted)


def second_rest(
    coeff, hx, ux, hs_in, us_in, final0, series, factor, wet, whole,
    final, token, gap,
    s0, s1, hs, us, shares, sems,
):
    del whole
    share_rows(series, factor, wet, shares)
    send = pltpu.make_async_copy(shares, gap, sems.at[2])
    send.start()
    diff, mix = coefficients(coeff)
    reads = [
        pltpu.make_async_copy(us_in, us, sems.at[0]),
        pltpu.make_async_copy(hs_in, hs, sems.at[1]),
    ]
    for c in reads:
        c.start()
    token[...] = jnp.zeros_like(token)
    gy = lax.axis_index("gy")
    first, last = gy == 0, gy == lax.axis_size("gy") - 1
    zero_pads(s0, SUB)
    zero_pads(s1, SUB)
    final[0] = final0[...]
    for c in reads:
        c.wait()
    for t in range(3, SUB):
        src, dst = (s0, s1) if t % 2 == 0 else (s1, s0)

        for r in range(*strips(t)):
            strip = Strip(r, first, last)
            h = strip.recall(hx, t - 3)
            u_prev = strip.recall(ux, t - 3)
            for l in range(SUB - t, t + 1):
                if l < t:
                    if l + 1 < t:
                        h_next = strip.spread(src, l + 1, diff[l + 1])
                    else:
                        h_next = strip.recall(hs, t - 3)
                    u = flux_between(mix[l], h_next, h)
                    v = added(h, u)
                    h = h_next
                else:
                    u = None
                    v = strip.recall(us, t - 3)
                v = less(v, u_prev)
                u_prev = u
                if t < SUB - 1:
                    strip.store(dst, l, v)
                else:
                    rows = slice(r * 8 - 16, r * 8 - 8)
                    for k in range(OWN_TILES):
                        final[l, rows, k * LANES : (k + 1) * LANES] = v[k]
    send.wait()


def finish(regridded, mask, gap, forcing):
    peers = gap.shape[0] // 2
    start = (1 - lax.axis_index("comp")) * peers
    for t, mean in enumerate(gap_means(gap, start, peers)):
        forcing[t] = regridded[t] + mask[...].astype(F32) * mean


def shifted(value, axis, by):
    n = lax.axis_size(axis)
    return lax.ppermute(value, axis, [(i, (i + by) % n) for i in range(n)])


def paired(value, axis, mask):
    return lax.ppermute(value, axis, [(i, i ^ mask) for i in range(lax.axis_size(axis))])


def per_device(
    state, guess, diffusion, mixing, coupling, land_temp, land_mask, weights, source_block, pattern
):
    state, guess, diff, mix, coupling = state[0], guess[0], diffusion[0], mixing[0], coupling[0]
    weights = weights[0]
    src = source_block[0].transpose(1, 2, 0)
    pat = pattern[0].transpose(1, 2, 0)
    band = lambda n: shape(n, BAND, COLS)
    field_buf = lambda n: pltpu.VMEM((n, ROWS, COLS), F32)
    band_buf = lambda n: pltpu.VMEM((n, BAND, COLS), F32)
    numbers = shape(2 * LEVELS, 8, LANES)

    message = shape(LEVELS, 8, CY)
    to_lower, to_upper = call(
        first_edges,
        [message, message],
        [
            pltpu.VMEM((AUX, 8, CY), F32),
            pltpu.VMEM((AUX, 8, CY), F32),
            pltpu.VMEM((2, 8, CY), jnp.int32),
            pltpu.VMEM((2, SUB - 1, 16, CY), BF16),
            pltpu.SemaphoreType.DMA((10,)),
        ],
        [HBM] * 5,
        grant=EDGE_GRANT,
    )(state, guess, coupling, land_temp, land_mask)
    state, guess, coupling, land_temp, mask, table, src, pat, to_lower, to_upper = (
        lax.optimization_barrier(
            (
                state, guess, coupling, land_temp, land_mask, weights, src, pat,
                to_lower, to_upper,
            )
        )
    )
    lower, upper = shifted(to_lower, "gx", -1), shifted(to_upper, "gx", 1)
    factor, wet, coeff = call(
        balance,
        [shape(CX, CY), shape(1, LANES), shape(2 * LEVELS, 8, LANES)],
        [
            pltpu.VMEM((BLOCKS, LANES), F32),
            pltpu.VMEM((PATTERNS, BLOCKS, LANES), F32),
            pltpu.VMEM((CX, CY), F32),
            pltpu.SemaphoreType.DMA(()),
            *[pltpu.VMEM((BLOCKS, LANES), F32)] * OWN_TILES,
        ],
        [SM, SM, SM, SM, VM, VM, VM],
        out_specs=[HBM, VM, VM],
    )(diff, mix, src, pat, table, mask, to_lower)
    other = paired(factor, "comp", 1)
    packed = shape(BAND, PACK_LANES)
    aux, one, three = call(pack_first, [shape(AUX, 16, CY), packed, packed], [], [VM] * 8)(
        state, guess, coupling, land_temp, mask, upper, lower, wet
    )
    one, three = paired(one, "gy", 1), paired(three, "gy", 3)

    series, hd, ud, hs, us, fixed = call(
        first_cone,
        [
            shape(SUB, CX, CY, dtype=BF16), band(SUB), band(SUB),
            band(3), band(3), band(4),
        ],
        [
            field_buf(CONE), field_buf(CONE), band_buf(SUB), band_buf(SUB),
            band_buf(3), band_buf(3), band_buf(4), pltpu.SemaphoreType.DMA((7,)),
        ],
        [VM] * 11 + [pl.BlockSpec(memory_space=pl.ANY)],
        out_specs=[VM] * 3 + [HBM] * 3,
    )(coeff, state, guess, coupling, land_temp, mask, upper, lower, aux, one, three, other)

    def regridded(received, before):
        edges = shape(2, 8, CY)
        return call(
            regrid,
            [shape(SUB, CX, CY), edges, edges],
            [
                pltpu.VMEM((BLOCKS * 8, LANES), F32),
                pltpu.VMEM((BLOCKS * 8, LANES), F32),
                pltpu.VMEM((PATTERNS, LANES, LANES), BF16),
                pltpu.SemaphoreType.DMA(()),
            ],
            [SM, SM, VM, HBM, VM],
            cost_estimate=pl.CostEstimate(
                flops=2 * BLOCKS * 8 * 2 * LANES * LANES,
                bytes_accessed=BLOCKS * 2 * LANES * LANES * 2,
                transcendentals=0,
            ),
        )(src, pat, received, weights, before)

    whole, hs_rest, us_rest, token = call(
        first_rest,
        [shape(LEVELS, CX, CY), band(3), band(3), shape(8, LANES)],
        [
            field_buf(LEVELS), field_buf(LEVELS),
            band_buf(3), band_buf(3), pltpu.SemaphoreType.DMA((2,)),
        ],
        [VM] * 8,
        out_specs=[VM, HBM, HBM, VM],
    )(coeff, state, upper, lower, one, three, hd, ud)

    received = paired(series, "comp", 1)
    peers = lax.axis_size(("gx", "gy"))
    gap, after = call(
        losses,
        [shape(peers, 1, LANES), shape(8, LANES)],
        [pltpu.VMEM((peers, 1, LANES), F32), pltpu.SemaphoreType.DMA(())],
        [VM, VM, VM, VM],
        out_specs=[HBM, VM],
    )(received, factor, wet, token)
    gap = lax.all_to_all(gap, ("gx", "gy"), 0, 0)
    out, top, bottom = regridded(received, after)
    lower, upper = shifted(top, "gx", -1), shifted(bottom, "gx", 1)
    packed = shape(BAND, LANES)
    one, three = call(
        pack_second, [packed, packed], [pltpu.VMEM((SUB - 1, 16, CY), F32)], [VM] * 3
    )(out, upper, lower)
    one, three = paired(one, "gy", 1), paired(three, "gy", 3)

    series, final0, hx, ux, coeff = call(
        second_cone,
        [shape(SUB, CX, CY, dtype=BF16), shape(CX, CY), band(3), band(3), numbers],
        [
            field_buf(3), field_buf(3), band_buf(SUB), band_buf(SUB),
            band_buf(4), band_buf(3), band_buf(3), pltpu.VMEM((SUB - 1, 16, CY), F32),
            pltpu.SemaphoreType.DMA((3,)),
        ],
        [HBM] + [VM] * 6 + [HBM, HBM],
    )(fixed, out, upper, lower, one, three, gap, hs, us)

    everyone = shape(2 * peers, 1, LANES)
    whole, token, gap = call(
        second_rest,
        [shape(LEVELS, CX, CY), shape(8, LANES), everyone],
        [
            field_buf(SUB), field_buf(SUB), band_buf(3), band_buf(3),
            pltpu.VMEM(everyone.shape, F32), pltpu.SemaphoreType.DMA((3,)),
        ],
        [VM, VM, VM, HBM, HBM, VM, VM, VM, VM, pl.BlockSpec(memory_space=pl.ANY)],
        out_specs=[pl.BlockSpec((SUB, CX, CY), lambda i: (0, 0, 0)), VM, HBM],
        grid=(1,),
        input_output_aliases={9: 0},
    )(coeff, hx, ux, hs_rest, us_rest, final0, series, other, wet, whole)

    received = paired(series, "comp", 1)
    gap = lax.all_to_all(gap, ("comp", "gx", "gy"), 0, 0)
    out, _, _ = regridded(received, token)
    (forcing,) = call(finish, [shape(SUB, CX, CY)], [], [VM] * 3)(out, land_mask, gap)
    return whole[None], forcing[None]


def solution(mesh):
    placed = (
        P("comp", None, "gx", "gy"),
        P("comp", None, "gx", "gy"),
        P("comp", None),
        P("comp", None),
        P("comp", "gx", "gy"),
        P("gx", "gy"),
        P("gx", "gy"),
        P("comp", ("gx", "gy"), None, None),
        P("comp", "gx", "gy", None),
        P("comp", "gx", "gy", None),
    )
    return jax.shard_map(
        per_device,
        mesh=mesh,
        in_specs=placed,
        out_specs=(P("comp", None, "gx", "gy"), P("comp", None, "gx", "gy")),
        check_vma=False,
    )
```

```python
import jax
import jax.numpy as jnp
from jax import lax
from jax.experimental import pallas as pl
from jax.experimental.pallas import tpu as pltpu
from jax.sharding import PartitionSpec as P

F32 = jnp.float32
BF16 = jnp.bfloat16
SUB = 6
LEVELS = 16
CX = 32
CY = 512
LANES = 128
OWN_TILES = CY // LANES
COLS = CY + LANES
ROWS = CX + 32
BAND = CX + 16
PATTERNS = 32
BLOCKS = CX * OWN_TILES
VMEM_LIMIT = 12 * 1024 * 1024
EDGE_GRANT = 60 * 1024 * 1024

N_FIELDS = LEVELS + 3 + SUB - 1
AT_COUPLING, AT_LAND, AT_MASK, AT_GUESS = LEVELS, LEVELS + 1, LEVELS + 2, LEVELS + 3
PACK_LANES = 256

VM = pl.BlockSpec(memory_space=pltpu.VMEM)
SM = pl.BlockSpec(memory_space=pltpu.SMEM)
HBM = pl.BlockSpec(memory_space=pltpu.HBM)


def shape(*dims, dtype=F32):
    return jax.ShapeDtypeStruct(dims, dtype)


def call(body, outs, scratch, ins, out_specs=None, grant=VMEM_LIMIT, **kw):
    return pl.pallas_call(
        body,
        out_shape=outs,
        in_specs=ins,
        out_specs=[VM] * len(outs) if out_specs is None else out_specs,
        scratch_shapes=scratch,
        compiler_params=pltpu.CompilerParams(vmem_limit_bytes=grant),
        **kw,
    )


def iotas():
    row = lax.broadcasted_iota(jnp.int32, (8, LANES), 0)
    lane = lax.broadcasted_iota(jnp.int32, (8, LANES), 1)
    return row, lane


def roll_lanes(x, shift):
    shift %= LANES
    return x if shift == 0 else pltpu.roll(x, shift, 1)


def pack_columns(fields, one, three, even):
    _, lane = iotas()
    groups = PACK_LANES // LANES if len(fields) > 16 else 1
    for tile in range(6):
        for g in range(groups):
            left = jnp.zeros((8, LANES), F32)
            right = jnp.zeros((8, LANES), F32)
            for f in range(g * 16, min(len(fields), g * 16 + 16)):
                at = (f % 16) * 8
                head, tail = fields[f](tile)
                left = jnp.where((lane >= at) & (lane < at + 8), roll_lanes(head, at), left)
                right = jnp.where((lane >= at) & (lane < at + 8), roll_lanes(tail, at + 8), right)
            span = (slice(tile * 8, tile * 8 + 8), slice(g * LANES, (g + 1) * LANES))
            one[span] = jnp.where(even, right, left)
            three[span] = jnp.where(even, left, right)


def side_halos(one, three, even, first, last, tile, g):
    span = (slice(tile * 8, tile * 8 + 8), slice(g * LANES, (g + 1) * LANES))
    a, b = one[span], three[span]
    right = jnp.where(last, 0.0, jnp.where(even, a, b))
    left = jnp.where(first, 0.0, jnp.where(even, b, a))
    return right, left


def side_tile(right, left, f, lane):
    at = (f % 16) * 8
    return jnp.where(
        lane < 6,
        roll_lanes(right, -at),
        jnp.where(lane >= LANES - 6, roll_lanes(left, LANES - 8 - at), 0.0),
    )


def place_sides(dst_of, fields, one, three, even, first, last):
    _, lane = iotas()
    for tile in range(6):
        packs = {}
        for f in fields:
            g = f // 16
            if g not in packs:
                packs[g] = side_halos(one, three, even, first, last, tile, g)
            dst_of(f, tile, side_tile(*packs[g], f, lane))


def place_rows(dst, own, upper, lower):
    dst[8:16, :CY] = upper
    dst[16 : 16 + CX, :CY] = own
    dst[16 + CX : 24 + CX, :CY] = lower


def zero_pads(ref, count):
    for l in range(count):
        ref[l, 0:8, :] = jnp.zeros((8, COLS), F32)
        ref[l, ROWS - 8 : ROWS, :] = jnp.zeros((8, COLS), F32)


def position():
    gy = lax.axis_index("gy")
    return gy % 2 == 0, gy == 0, gy == lax.axis_size("gy") - 1


class Strip:
    def __init__(self, r, first, last):
        self.r = r
        row, lane = iotas()
        self.row_first, self.row_last = row == 0, row == 7
        self.lane_first, self.lane_last = lane == 0, lane == LANES - 1
        self.inside = ((lane < 6) & jnp.logical_not(last)) | (
            (lane >= LANES - 6) & jnp.logical_not(first)
        )

    def load(self, ref, l, shift=0):
        rows = slice(self.r * 8 + shift, self.r * 8 + shift + 8)
        return [ref[l, rows, k * LANES : (k + 1) * LANES] for k in range(OWN_TILES + 1)]

    def spread(self, ref, l, d):
        x = self.load(ref, l)
        above = self.load(ref, l, -8)
        below = self.load(ref, l, 8)
        out = []
        n = len(x)
        for k in range(n):
            c = x[k]
            up = pltpu.roll(jnp.where(self.row_last, above[k], c), 1, 0)
            down = pltpu.roll(jnp.where(self.row_first, below[k], c), 7, 0)
            left = pltpu.roll(jnp.where(self.lane_last, x[k - 1], c), 1, 1)
            right = pltpu.roll(jnp.where(self.lane_first, x[(k + 1) % n], c), LANES - 1, 1)
            out.append(c + d * (((up + down) + (left + right)) - 4.0 * c))
        return out

    def store(self, ref, l, values):
        rows = slice(self.r * 8, self.r * 8 + 8)
        for k, v in enumerate(values):
            if k == OWN_TILES:
                v = jnp.where(self.inside, v, 0.0)
            ref[l, rows, k * LANES : (k + 1) * LANES] = v

    def save(self, ref, l, values):
        rows = slice(self.r * 8 - 8, self.r * 8)
        for k, v in enumerate(values):
            ref[l, rows, k * LANES : (k + 1) * LANES] = v

    def recall(self, ref, l):
        return self.load(ref, l, -8)


def flux_between(mix, lower, upper):
    return [mix * (a - b) for a, b in zip(lower, upper)]


def added(a, b):
    return [x + y for x, y in zip(a, b)]


def less(a, b):
    return [x - y for x, y in zip(a, b)]


def surface(v, f, c, m, ml, ocean):
    new, emitted = [], []
    for vk, fk, ck, mk, lk in zip(v, f, c, m, ml):
        mf = mk * fk
        flux = ck * (vk - (mf + lk))
        warmed = vk + ck * mf
        new.append(jnp.where(ocean, warmed, vk - flux))
        emitted.append(jnp.where(ocean, mk * warmed, flux))
    return new, emitted


def coefficient_place(i):
    rows, cols = i // 5 * 8, i % 5 * LANES
    return slice(rows, rows + 8), slice(cols, cols + LANES)


class Rows:
    def __init__(self, ref, start):
        self.ref, self.start = ref, start

    def __getitem__(self, l):
        return self.ref[self.start + l]


def coefficients(coeff):
    return Rows(coeff, 0), Rows(coeff, LEVELS)


def strips(t):
    return (1, 7) if t < SUB - 1 else (2, 6)


def write_series(series, emitted):
    for t in range(SUB):
        for half in range(CX // 16):
            rows = slice(8 + half * 16, 24 + half * 16)
            series[t, half * 16 : half * 16 + 16, :] = emitted[t, rows, :CY].astype(BF16)


AUX = 3 + SUB - 1


def aux_slots():
    n = 0
    for a in range(AUX):
        for i in range(SUB - 1 if a < 3 else SUB - 1 - (a - 3)):
            yield a, i, n // 2, n % 2
            n += 1


def first_edges(
    state, guess, coupling, land, mask,
    to_lower, to_upper,
    head, tail, ints, short, sems,
):
    n = 0
    copies = []

    def copy(src, dst):
        nonlocal n
        c = pltpu.make_async_copy(src, dst, sems.at[n])
        c.start()
        copies.append(c)
        n += 1

    for side, msg, buf in ((0, to_lower, head), (1, to_upper, tail)):
        rows = pl.ds(side * (CX - 8), 8)
        copy(state.at[:, rows, :], msg)
        copy(coupling.at[rows, :], buf.at[0])
        copy(land.at[rows, :], buf.at[1])
        copy(mask.at[rows, :], ints.at[side])
        copy(guess.at[pl.ds(0, SUB - 1), pl.ds(side * (CX - 16), 16), :], short.at[side])
    for c in copies:
        c.wait()
    for side, buf in ((0, head), (1, tail)):
        buf[2] = ints[side].astype(F32)
        for t in range(SUB - 1):
            rows16 = short[side, t].astype(F32)
            buf[3 + t] = rows16[8:] if side else rows16[:8]
    for a, i, tile, spare in aux_slots():
        to_lower[tile, 6 + spare : 7 + spare, :] = head[a, i : i + 1, :]
        to_upper[tile, spare : spare + 1, :] = tail[a, 7 - i : 8 - i, :]


def pack_first(
    state, guess, coupling, land, mask, upper, lower, before,
    aux, one, three,
):
    del before
    even, _, _ = position()
    aux[...] = jnp.zeros_like(aux)
    for a, i, tile, spare in aux_slots():
        aux[a, 7 - i : 8 - i, :] = upper[tile, spare : spare + 1, :]
        aux[a, 8 + i : 9 + i, :] = lower[tile, 6 + spare : 7 + spare, :]

    def field(f):
        def of(tile):
            rows = slice(0, 8)
            if tile in (0, 5):
                if f < LEVELS:
                    block = upper.at[f] if tile == 0 else lower.at[f]
                else:
                    block = aux.at[f - LEVELS]
                    rows = slice(0, 8) if tile == 0 else slice(8, 16)
            else:
                rows = slice(tile * 8 - 8, tile * 8)
                if f < LEVELS:
                    block = state.at[f]
                elif f == AT_COUPLING:
                    block = coupling
                elif f == AT_LAND:
                    block = land
                elif f == AT_MASK:
                    block = mask
                else:
                    block = guess.at[f - AT_GUESS]
                    base = (tile - 1) // 2 * 16
                    part = slice((tile - 1) % 2 * 8, (tile - 1) % 2 * 8 + 8)
                    head = block[base : base + 16, :LANES].astype(F32)[part]
                    tail = block[base : base + 16, CY - LANES :].astype(F32)[part]
                    return head, tail
            head, tail = block[rows, :LANES], block[rows, CY - LANES :]
            return head.astype(F32), tail.astype(F32)

        return of

    pack_columns([field(f) for f in range(N_FIELDS)], one, three, even)


CONE = SUB + 1


def first_cone(
    coeff, state, guess, coupling, land, mask, upper, lower, aux, one, three, beside,
    series, hd, ud, hs_out, us_out, fixed_out,
    s0, s1, g, emitted, hs, us, fixed, sems,
):
    del beside
    diff, mix = coefficients(coeff)
    writes = []

    def write(src, dst):
        c = pltpu.make_async_copy(src, dst, sems.at[len(writes)])
        c.start()
        writes.append(c)

    even, first, last = position()
    ocean = lax.axis_index("comp") == 1
    zero_pads(s0, CONE)
    zero_pads(s1, CONE - 1)
    for l in range(CONE):
        place_rows(s0.at[l], state[l], upper[l], lower[l])

    def rows_of(ref, k, f, own):
        ref[k, 0:8, :CY] = aux[f - LEVELS, 0:8, :]
        ref[k, 8 : 8 + CX, :CY] = own
        ref[k, 8 + CX : 16 + CX, :CY] = aux[f - LEVELS, 8:16, :]

    rows_of(fixed, 0, AT_COUPLING, coupling[...])
    rows_of(fixed, 1, AT_MASK, mask[...].astype(F32))
    rows_of(fixed, 2, AT_LAND, land[...])
    for t in range(SUB - 1):
        rows_of(g, t, AT_GUESS + t, guess[t].astype(F32))
    g[SUB - 1, 8 : 8 + CX, :CY] = guess[SUB - 1].astype(F32)

    side = slice(CY, COLS)
    slot = {AT_COUPLING: 0, AT_MASK: 1, AT_LAND: 2}

    def put(f, tile, value):
        rows = slice(tile * 8, tile * 8 + 8)
        if f < LEVELS:
            s0[f, tile * 8 + 8 : tile * 8 + 16, side] = value
        elif f < AT_GUESS:
            fixed[slot[f], rows, side] = value
        else:
            g[f - AT_GUESS, rows, side] = value

    fields = [*range(CONE), *range(LEVELS, N_FIELDS)]
    place_sides(put, fields, one, three, even, first, last)
    g[SUB - 1, :, side] = jnp.zeros((BAND, LANES), F32)
    fixed[2] = (1.0 - fixed[1]) * fixed[2]
    for l in range(SUB):
        for i, start in ((l, 0), (SUB + l, LEVELS)):
            rows, cols = coefficient_place(i)
            fixed[3, rows, cols] = coeff[start + l]
    write(fixed, fixed_out)

    for t in range(SUB):
        src, dst = (s0, s1) if t % 2 == 0 else (s1, s0)

        for r in range(*strips(t)):
            strip = Strip(r, first, last)
            h = strip.spread(src, 0, diff[0])
            u_prev = None
            for l in range(SUB - t):
                h_next = strip.spread(src, l + 1, diff[l + 1])
                u = flux_between(mix[l], h_next, h)
                v = added(h, u)
                if l == t and t < 3:
                    strip.save(us, t, v)
                    if t:
                        strip.save(hs, t - 1, h)
                if u_prev is not None:
                    v = less(v, u_prev)
                if l == 0:
                    c, m, ml = (strip.recall(fixed, i) for i in range(3))
                    v, e = surface(v, strip.recall(g, t), c, m, ml, ocean)
                    strip.save(emitted, t, e[:OWN_TILES])
                if t < SUB - 1:
                    strip.store(dst, l, v)
                h, u_prev = h_next, u
            strip.save(hd, t, h)
            strip.save(ud, t, u_prev)
            if t == 3:
                strip.save(hs, 2, h)
        if t < 3:
            write(us.at[t], us_out.at[t])
        if 0 < t < 4:
            write(hs.at[t - 1], hs_out.at[t - 1])

    write_series(series, emitted)
    for c in writes:
        c.wait()


def first_rest(
    coeff, state, upper, lower, one, three, hd, ud,
    final, hs_out, us_out, token,
    s0, s1, hs, us, sems,
):
    diff, mix = coefficients(coeff)
    token[...] = jnp.zeros_like(token)
    even, first, last = position()
    zero_pads(s0, LEVELS)
    zero_pads(s1, LEVELS)
    for l in range(CONE, LEVELS):
        place_rows(s0.at[l], state[l], upper[l], lower[l])

    def put(f, tile, value):
        s0[f, tile * 8 + 8 : tile * 8 + 16, CY:COLS] = value

    place_sides(put, list(range(CONE, LEVELS)), one, three, even, first, last)

    for t in range(SUB):
        src, dst = (s0, s1) if t % 2 == 0 else (s1, s0)

        for r in range(*strips(t)):
            strip = Strip(r, first, last)
            h = strip.recall(hd, t)
            u_prev = strip.recall(ud, t)
            for l in range(SUB - t, LEVELS):
                if l < LEVELS - 1:
                    h_next = strip.spread(src, l + 1, diff[l + 1])
                    u = flux_between(mix[l], h_next, h)
                    v = added(h, u)
                else:
                    h_next = u = None
                    v = h
                if l == t and t >= 3:
                    strip.save(us, t - 3, v)
                    if t > 3:
                        strip.save(hs, t - 4, h)
                v = less(v, u_prev)
                if t < SUB - 1:
                    strip.store(dst, l, v)
                elif l >= SUB:
                    rows = slice(r * 8 - 16, r * 8 - 8)
                    for k in range(OWN_TILES):
                        final[l, rows, k * LANES : (k + 1) * LANES] = v[k]
                h, u_prev = h_next, u
    writes = [
        pltpu.make_async_copy(hs, hs_out, sems.at[0]),
        pltpu.make_async_copy(us, us_out, sems.at[1]),
    ]
    for c in writes:
        c.start()
    for c in writes:
        c.wait()


def balance(
    diff, mix, src, pat, weights, mask, after,
    out, wet, coeff,
    m, z, b, sem, *totals,
):
    del after
    for l in range(LEVELS):
        coeff[l] = jnp.full((8, LANES), diff[l], F32)
    for l in range(LEVELS - 1):
        coeff[LEVELS + l] = jnp.full((8, LANES), mix[l], F32)
    coeff[2 * LEVELS - 1] = jnp.zeros((8, LANES), F32)
    count = jnp.zeros((8, LANES), F32)
    for part in range(CX // 8):
        for j in range(OWN_TILES):
            v = mask[part * 8 : part * 8 + 8, j * LANES : (j + 1) * LANES].astype(F32)
            count += v
            m[pl.ds(part * 8 * OWN_TILES + j, 8, stride=OWN_TILES), :] = v
    _, lane = iotas()
    count = jnp.sum(count, axis=(0, 1), keepdims=True)
    wet[...] = jnp.where(lane[:1] == SUB, count, 0.0)
    blocks = m[...].astype(BF16)

    @pl.loop(0, PATTERNS, unroll=8)
    def _(p):
        z[p] = lax.dot_general(
            blocks, weights[p], (((1,), (1,)), ((), ())), preferred_element_type=F32
        )

    for j in range(OWN_TILES):
        totals[j][...] = jnp.zeros_like(totals[j])

    @pl.loop(0, CX, unroll=4)
    def _(r):
        for k in range(2):
            for j in range(OWN_TILES):
                row = pl.ds(src[j, k, r], 1)
                line = z[pat[j, k, r], pl.ds(r * OWN_TILES + j, 1), :]
                totals[j][row, :] = totals[j][row, :] + line

    m[...] = m[...] - ((totals[0][...] + totals[1][...]) + (totals[2][...] + totals[3][...]))
    for part in range(CX // 8):
        for j in range(OWN_TILES):
            v = m[pl.ds(part * 8 * OWN_TILES + j, 8, stride=OWN_TILES), :]
            b[part * 8 : part * 8 + 8, j * LANES : (j + 1) * LANES] = v
    c = pltpu.make_async_copy(b, out, sem)
    c.start()
    c.wait()


def share_rows(series, factor, wet, rows):
    partial = [jnp.zeros((8, LANES), F32) for _ in range(SUB)]
    for half in range(CX // 16):
        for j in range(OWN_TILES):
            cols = slice(j * LANES, (j + 1) * LANES)
            f = factor[half * 16 : half * 16 + 16, cols]
            for t in range(SUB):
                p = f * series[t, half * 16 : half * 16 + 16, cols].astype(F32)
                partial[t] += p[:8] + p[8:]
    row, lane = iotas()
    total = jnp.zeros((8, LANES), F32)
    for t, value in enumerate(partial):
        total = jnp.where(row == t, jnp.sum(value, axis=0, keepdims=True), total)
    total = jnp.sum(total, axis=1, keepdims=True)
    total = jnp.sum(jnp.where(row == lane, total, 0.0), axis=0, keepdims=True) + wet[...]
    for k in range(rows.shape[0]):
        rows[k] = jnp.broadcast_to(total, rows.shape[1:])


def losses(
    received, factor, wet, before,
    gap, token,
    rows, sem,
):
    del before
    token[...] = jnp.zeros_like(token)
    share_rows(received, factor, wet, rows)
    c = pltpu.make_async_copy(rows, gap, sem)
    c.start()
    c.wait()


def edge_slots():
    for t, tile, start in ((0, 0, 0), (2, 0, 5), (1, 1, 0), (3, 1, 4), (4, 1, 6)):
        yield t, SUB - 1 - t, tile, start


def regrid(
    src, pat, received, weights_in, before,
    out, top, bottom,
    x, y, weights, sem,
):
    del before
    read = pltpu.make_async_copy(weights_in, weights, sem)
    read.start()
    for half in range(CX // 16):
        for j in range(OWN_TILES):
            cols = slice(j * LANES, (j + 1) * LANES)
            for t in range(SUB):
                v16 = received[t, half * 16 : half * 16 + 16, cols].astype(F32)
                for part in range(2):
                    row = half * 16 + part * 8
                    start = (row * OWN_TILES + j) * 8 + t
                    x[pl.ds(start, 8, stride=OWN_TILES * 8), :] = v16[part * 8 : part * 8 + 8]
    read.wait()
    for r in range(CX):
        for j in range(OWN_TILES):
            a, w = [], []
            for k in range(2):
                start = pl.multiple_of(src[j, k, r] * 8, 8)
                a.append(x[pl.ds(start, 8), :].astype(BF16))
                w.append(weights[pat[j, k, r]])
            product = jnp.dot(
                jnp.concatenate(a, 1), jnp.concatenate(w, 0), preferred_element_type=F32
            )
            y[pl.ds(r * OWN_TILES + j, 8, stride=BLOCKS), :] = product

    for part in range(CX // 8):
        for j in range(OWN_TILES):
            cols = slice(j * LANES, (j + 1) * LANES)
            for t in range(SUB):
                start = t * BLOCKS + part * 8 * OWN_TILES + j
                out[t, part * 8 : part * 8 + 8, cols] = y[pl.ds(start, 8, stride=OWN_TILES), :]
    top[1, 7:8, :] = jnp.zeros((1, CY), F32)
    bottom[1, 7:8, :] = jnp.zeros((1, CY), F32)
    for t, n, tile, start in edge_slots():
        top[tile, start : start + n, :] = out[t, 0:n, :]
        bottom[tile, start : start + n, :] = out[t, CX - n : CX, :]


def halo_rows(halo, upper, lower):
    halo[...] = jnp.zeros_like(halo)
    for t, n, tile, start in edge_slots():
        halo[t, 8 - n : 8, :] = upper[tile, start : start + n, :]
        halo[t, 8 : 8 + n, :] = lower[tile, start : start + n, :]


def pack_second(out, upper_in, lower_in, one, three, halo, upper, lower, sems):
    reads = [
        pltpu.make_async_copy(upper_in, upper, sems.at[0]),
        pltpu.make_async_copy(lower_in, lower, sems.at[1]),
    ]
    for c in reads:
        c.start()
    for c in reads:
        c.wait()
    even, _, _ = position()
    halo_rows(halo, upper, lower)

    def field(t):
        def of(tile):
            if tile in (0, 5):
                block, rows = halo.at[t], slice(0, 8) if tile == 0 else slice(8, 16)
            else:
                block, rows = out.at[t], slice(tile * 8 - 8, tile * 8)
            return block[rows, :LANES], block[rows, CY - LANES :]

        return of

    pack_columns([field(t) for t in range(SUB - 1)], one, three, even)


def gap_means(gap, start, count):
    total = jnp.sum(gap[pl.ds(start, count), 0:1], axis=0)
    lane = lax.broadcasted_iota(jnp.int32, (1, LANES), 1)
    wet = jnp.sum(jnp.where(lane == SUB, total, 0.0), axis=1, keepdims=True)
    return [
        jnp.sum(jnp.where(lane == t, total, 0.0), axis=1, keepdims=True) / wet for t in range(SUB)
    ]


def second_cone(
    fixed_in, regridded, upper_in, lower_in, one_in, three_in, gap_in, hs_in, us_in,
    series, final0, hx, ux, coeff,
    s0, s1, g, emitted, fixed, hs, us, halo, upper, lower, one, three, gap, sems,
):
    reads = []
    pairs = (
        (upper_in, upper), (lower_in, lower), (one_in, one), (three_in, three), (gap_in, gap),
        (us_in, us), (fixed_in, fixed), (hs_in, hs),
    )
    for i, (src, dst) in enumerate(pairs):
        reads.append(pltpu.make_async_copy(src, dst, sems.at[i]))
        reads[-1].start()
    even, first, last = position()
    ocean = lax.axis_index("comp") == 1
    zero_pads(s0, 3)
    zero_pads(s1, 3)
    for t in range(SUB):
        g[t, 8 : 8 + CX, :CY] = regridded[t]
    for c in reads[:5]:
        c.wait()
    halo_rows(halo, upper, lower)
    for t in range(SUB):
        if t < SUB - 1:
            g[t, 0:8, :CY] = halo[t, 0:8, :]
            g[t, 8 + CX : 16 + CX, :CY] = halo[t, 8:16, :]

    def put(f, tile, value):
        g[f, tile * 8 : tile * 8 + 8, CY:COLS] = value

    place_sides(put, list(range(SUB - 1)), one, three, even, first, last)
    g[SUB - 1, :, CY:COLS] = jnp.zeros((BAND, LANES), F32)
    means = [jnp.broadcast_to(v, (8, LANES)) for v in gap_means(gap, 0, gap.shape[0])]
    for c in reads[5:]:
        c.wait()
    for l in range(SUB):
        for i, start in ((l, 0), (SUB + l, LEVELS)):
            coeff[start + l] = fixed[(3, *coefficient_place(i))]
    diff, mix = coefficients(coeff)

    for t in range(SUB):
        src, dst = (s0, s1) if t % 2 == 0 else (s1, s0)

        for r in range(*strips(t)):
            strip = Strip(r, first, last)
            h = strip.spread(src, 0, diff[0]) if t else None
            u_prev = None
            for l in range(min(t, SUB - 1 - t) + 1):
                if l < t:
                    if l + 1 < t:
                        h_next = strip.spread(src, l + 1, diff[l + 1])
                    else:
                        h_next = strip.recall(hs, t - 1)
                    u = flux_between(mix[l], h_next, h)
                    v = added(h, u)
                else:
                    v = strip.recall(us, t)
                if u_prev is not None:
                    v = less(v, u_prev)
                if l == 0:
                    c, m, ml = (strip.recall(fixed, i) for i in range(3))
                    f = [a + b * means[t] for a, b in zip(strip.recall(g, t), m)]
                    v, e = surface(v, f, c, m, ml, ocean)
                    strip.save(emitted, t, e[:OWN_TILES])
                    if t == SUB - 1:
                        rows = slice(r * 8 - 16, r * 8 - 8)
                        for k in range(OWN_TILES):
                            final0[rows, k * LANES : (k + 1) * LANES] = v[k]
                if t < SUB - 1:
                    strip.store(dst, l, v)
                if l < t:
                    h, u_prev = h_next, u
            if t >= 3:
                strip.save(hx, t - 3, h)
                strip.save(ux, t - 3, u_prev)

    write_series(series, emitted)


def second_rest(
    coeff, hx, ux, hs_in, us_in, final0, series, factor, wet, whole,
    final, token, gap,
    s0, s1, hs, us, shares, sems,
):
    del whole
    share_rows(series, factor, wet, shares)
    send = pltpu.make_async_copy(shares, gap, sems.at[2])
    send.start()
    diff, mix = coefficients(coeff)
    reads = [
        pltpu.make_async_copy(us_in, us, sems.at[0]),
        pltpu.make_async_copy(hs_in, hs, sems.at[1]),
    ]
    for c in reads:
        c.start()
    token[...] = jnp.zeros_like(token)
    gy = lax.axis_index("gy")
    first, last = gy == 0, gy == lax.axis_size("gy") - 1
    zero_pads(s0, SUB)
    zero_pads(s1, SUB)
    final[0] = final0[...]
    for c in reads:
        c.wait()
    for t in range(3, SUB):
        src, dst = (s0, s1) if t % 2 == 0 else (s1, s0)

        for r in range(*strips(t)):
            strip = Strip(r, first, last)
            h = strip.recall(hx, t - 3)
            u_prev = strip.recall(ux, t - 3)
            for l in range(SUB - t, t + 1):
                if l < t:
                    if l + 1 < t:
                        h_next = strip.spread(src, l + 1, diff[l + 1])
                    else:
                        h_next = strip.recall(hs, t - 4)
                    u = flux_between(mix[l], h_next, h)
                    v = added(h, u)
                    h = h_next
                else:
                    u = None
                    v = strip.recall(us, t - 3)
                v = less(v, u_prev)
                u_prev = u
                if t < SUB - 1:
                    strip.store(dst, l, v)
                else:
                    rows = slice(r * 8 - 16, r * 8 - 8)
                    for k in range(OWN_TILES):
                        final[l, rows, k * LANES : (k + 1) * LANES] = v[k]
    send.wait()


def finish(regridded, mask, gap, forcing):
    peers = gap.shape[0] // 2
    start = (1 - lax.axis_index("comp")) * peers
    for t, mean in enumerate(gap_means(gap, start, peers)):
        forcing[t] = regridded[t] + mask[...].astype(F32) * mean


def shifted(value, axis, by):
    n = lax.axis_size(axis)
    return lax.ppermute(value, axis, [(i, (i + by) % n) for i in range(n)])


def paired(value, axis, mask):
    return lax.ppermute(value, axis, [(i, i ^ mask) for i in range(lax.axis_size(axis))])


def per_device(
    state, guess, diffusion, mixing, coupling, land_temp, land_mask, weights, source_block, pattern
):
    state, guess, diff, mix, coupling = state[0], guess[0], diffusion[0], mixing[0], coupling[0]
    weights = weights[0]
    src = source_block[0].transpose(1, 2, 0)
    pat = pattern[0].transpose(1, 2, 0)
    band = lambda n: shape(n, BAND, COLS)
    field_buf = lambda n: pltpu.VMEM((n, ROWS, COLS), F32)
    band_buf = lambda n: pltpu.VMEM((n, BAND, COLS), F32)
    numbers = shape(2 * LEVELS, 8, LANES)

    message = shape(LEVELS, 8, CY)
    to_lower, to_upper = call(
        first_edges,
        [message, message],
        [
            pltpu.VMEM((AUX, 8, CY), F32),
            pltpu.VMEM((AUX, 8, CY), F32),
            pltpu.VMEM((2, 8, CY), jnp.int32),
            pltpu.VMEM((2, SUB - 1, 16, CY), BF16),
            pltpu.SemaphoreType.DMA((10,)),
        ],
        [HBM] * 5,
        grant=EDGE_GRANT,
    )(state, guess, coupling, land_temp, land_mask)
    state, guess, coupling, land_temp, mask, table, src, pat, to_lower, to_upper = (
        lax.optimization_barrier(
            (
                state, guess, coupling, land_temp, land_mask, weights, src, pat,
                to_lower, to_upper,
            )
        )
    )
    lower, upper = shifted(to_lower, "gx", -1), shifted(to_upper, "gx", 1)
    factor, wet, coeff = call(
        balance,
        [shape(CX, CY), shape(1, LANES), shape(2 * LEVELS, 8, LANES)],
        [
            pltpu.VMEM((BLOCKS, LANES), F32),
            pltpu.VMEM((PATTERNS, BLOCKS, LANES), F32),
            pltpu.VMEM((CX, CY), F32),
            pltpu.SemaphoreType.DMA(()),
            *[pltpu.VMEM((BLOCKS, LANES), F32)] * OWN_TILES,
        ],
        [SM, SM, SM, SM, VM, VM, VM],
        out_specs=[HBM, VM, VM],
    )(diff, mix, src, pat, table, mask, to_lower)
    other = paired(factor, "comp", 1)
    packed = shape(BAND, PACK_LANES)
    aux, one, three = call(pack_first, [shape(AUX, 16, CY), packed, packed], [], [VM] * 8)(
        state, guess, coupling, land_temp, mask, upper, lower, wet
    )
    one, three = paired(one, "gy", 1), paired(three, "gy", 3)

    series, hd, ud, hs, us, fixed = call(
        first_cone,
        [
            shape(SUB, CX, CY, dtype=BF16), band(SUB), band(SUB),
            band(3), band(3), band(4),
        ],
        [
            field_buf(CONE), field_buf(CONE), band_buf(SUB), band_buf(SUB),
            band_buf(3), band_buf(3), band_buf(4), pltpu.SemaphoreType.DMA((7,)),
        ],
        [VM] * 11 + [pl.BlockSpec(memory_space=pl.ANY)],
        out_specs=[VM] * 3 + [HBM] * 3,
    )(coeff, state, guess, coupling, land_temp, mask, upper, lower, aux, one, three, other)

    def regridded(received, before):
        edges = shape(2, 8, CY)
        return call(
            regrid,
            [shape(SUB, CX, CY), edges, edges],
            [
                pltpu.VMEM((BLOCKS * 8, LANES), F32),
                pltpu.VMEM((BLOCKS * 8, LANES), F32),
                pltpu.VMEM((PATTERNS, LANES, LANES), BF16),
                pltpu.SemaphoreType.DMA(()),
            ],
            [SM, SM, VM, HBM, VM],
            cost_estimate=pl.CostEstimate(
                flops=2 * BLOCKS * 8 * 2 * LANES * LANES,
                bytes_accessed=BLOCKS * 2 * LANES * LANES * 2,
                transcendentals=0,
            ),
        )(src, pat, received, weights, before)

    whole, hs_rest, us_rest, token = call(
        first_rest,
        [shape(LEVELS, CX, CY), band(2), band(3), shape(8, LANES)],
        [
            field_buf(LEVELS), field_buf(LEVELS),
            band_buf(2), band_buf(3), pltpu.SemaphoreType.DMA((2,)),
        ],
        [VM] * 8,
        out_specs=[VM, HBM, HBM, VM],
    )(coeff, state, upper, lower, one, three, hd, ud)

    received = paired(series, "comp", 1)
    peers = lax.axis_size(("gx", "gy"))
    gap, after = call(
        losses,
        [shape(peers, 2, LANES), shape(8, LANES)],
        [pltpu.VMEM((peers, 2, LANES), F32), pltpu.SemaphoreType.DMA(())],
        [VM, VM, VM, VM],
        out_specs=[HBM, VM],
    )(received, factor, wet, token)
    gap = lax.all_to_all(gap, ("gx", "gy"), 0, 0)
    out, top, bottom = regridded(received, after)
    lower, upper = shifted(top, "gx", -1), shifted(bottom, "gx", 1)
    packed = shape(BAND, LANES)
    one, three = call(
        pack_second,
        [packed, packed],
        [
            pltpu.VMEM((SUB - 1, 16, CY), F32),
            pltpu.VMEM(upper.shape, F32),
            pltpu.VMEM(lower.shape, F32),
            pltpu.SemaphoreType.DMA((2,)),
        ],
        [VM, HBM, HBM],
    )(out, upper, lower)
    one, three = paired(one, "gy", 1), paired(three, "gy", 3)

    series, final0, hx, ux, coeff = call(
        second_cone,
        [shape(SUB, CX, CY, dtype=BF16), shape(CX, CY), band(3), band(3), numbers],
        [
            field_buf(3), field_buf(3), band_buf(SUB), band_buf(SUB),
            band_buf(4), band_buf(3), band_buf(3), pltpu.VMEM((SUB - 1, 16, CY), F32),
            *[pltpu.VMEM(v.shape, F32) for v in (upper, lower, one, three, gap)],
            pltpu.SemaphoreType.DMA((8,)),
        ],
        [HBM, VM] + [HBM] * 7,
    )(fixed, out, upper, lower, one, three, gap, hs, us)

    everyone = shape(2 * peers, 1, LANES)
    whole, token, gap = call(
        second_rest,
        [shape(LEVELS, CX, CY), shape(8, LANES), everyone],
        [
            field_buf(SUB), field_buf(SUB), band_buf(2), band_buf(3),
            pltpu.VMEM(everyone.shape, F32), pltpu.SemaphoreType.DMA((3,)),
        ],
        [VM, VM, VM, HBM, HBM, VM, VM, VM, VM, pl.BlockSpec(memory_space=pl.ANY)],
        out_specs=[pl.BlockSpec((SUB, CX, CY), lambda i: (0, 0, 0)), VM, HBM],
        grid=(1,),
        input_output_aliases={9: 0},
    )(coeff, hx, ux, hs_rest, us_rest, final0, series, other, wet, whole)

    received = paired(series, "comp", 1)
    gap = lax.all_to_all(gap, ("comp", "gx", "gy"), 0, 0)
    out, _, _ = regridded(received, token)
    (forcing,) = call(finish, [shape(SUB, CX, CY)], [], [VM] * 3)(out, land_mask, gap)
    return whole[None], forcing[None]


def solution(mesh):
    placed = (
        P("comp", None, "gx", "gy"),
        P("comp", None, "gx", "gy"),
        P("comp", None),
        P("comp", None),
        P("comp", "gx", "gy"),
        P("gx", "gy"),
        P("gx", "gy"),
        P("comp", ("gx", "gy"), None, None),
        P("comp", "gx", "gy", None),
        P("comp", "gx", "gy", None),
    )
    return jax.shard_map(
        per_device,
        mesh=mesh,
        in_specs=placed,
        out_specs=(P("comp", None, "gx", "gy"), P("comp", None, "gx", "gy")),
        check_vma=False,
    )
```

```python
import jax
import jax.numpy as jnp
from jax import lax
from jax.experimental import pallas as pl
from jax.experimental.pallas import tpu as pltpu
from jax.sharding import PartitionSpec as P

F32 = jnp.float32
BF16 = jnp.bfloat16
SUB = 6
LEVELS = 16
CX = 32
CY = 512
LANES = 128
OWN_TILES = CY // LANES
COLS = CY + LANES
ROWS = CX + 32
BAND = CX + 16
PATTERNS = 32
BLOCKS = CX * OWN_TILES
VMEM_LIMIT = 12 * 1024 * 1024
EDGE_GRANT = 60 * 1024 * 1024

N_FIELDS = LEVELS + 3 + SUB - 1
AT_COUPLING, AT_LAND, AT_MASK, AT_GUESS = LEVELS, LEVELS + 1, LEVELS + 2, LEVELS + 3
PACK_LANES = 256

VM = pl.BlockSpec(memory_space=pltpu.VMEM)
SM = pl.BlockSpec(memory_space=pltpu.SMEM)
HBM = pl.BlockSpec(memory_space=pltpu.HBM)


def shape(*dims, dtype=F32):
    return jax.ShapeDtypeStruct(dims, dtype)


def call(body, outs, scratch, ins, out_specs=None, grant=VMEM_LIMIT, **kw):
    return pl.pallas_call(
        body,
        out_shape=outs,
        in_specs=ins,
        out_specs=[VM] * len(outs) if out_specs is None else out_specs,
        scratch_shapes=scratch,
        compiler_params=pltpu.CompilerParams(vmem_limit_bytes=grant),
        **kw,
    )


def iotas():
    row = lax.broadcasted_iota(jnp.int32, (8, LANES), 0)
    lane = lax.broadcasted_iota(jnp.int32, (8, LANES), 1)
    return row, lane


def roll_lanes(x, shift):
    shift %= LANES
    return x if shift == 0 else pltpu.roll(x, shift, 1)


def pack_columns(fields, one, three, even):
    _, lane = iotas()
    groups = PACK_LANES // LANES if len(fields) > 16 else 1
    for tile in range(6):
        for g in range(groups):
            left = jnp.zeros((8, LANES), F32)
            right = jnp.zeros((8, LANES), F32)
            for f in range(g * 16, min(len(fields), g * 16 + 16)):
                at = (f % 16) * 8
                head, tail = fields[f](tile)
                left = jnp.where((lane >= at) & (lane < at + 8), roll_lanes(head, at), left)
                right = jnp.where((lane >= at) & (lane < at + 8), roll_lanes(tail, at + 8), right)
            span = (slice(tile * 8, tile * 8 + 8), slice(g * LANES, (g + 1) * LANES))
            one[span] = jnp.where(even, right, left)
            three[span] = jnp.where(even, left, right)


def side_halos(one, three, even, first, last, tile, g):
    span = (slice(tile * 8, tile * 8 + 8), slice(g * LANES, (g + 1) * LANES))
    a, b = one[span], three[span]
    right = jnp.where(last, 0.0, jnp.where(even, a, b))
    left = jnp.where(first, 0.0, jnp.where(even, b, a))
    return right, left


def side_tile(right, left, f, lane):
    at = (f % 16) * 8
    return jnp.where(
        lane < 6,
        roll_lanes(right, -at),
        jnp.where(lane >= LANES - 6, roll_lanes(left, LANES - 8 - at), 0.0),
    )


def place_sides(dst_of, fields, one, three, even, first, last):
    _, lane = iotas()
    for tile in range(6):
        packs = {}
        for f in fields:
            g = f // 16
            if g not in packs:
                packs[g] = side_halos(one, three, even, first, last, tile, g)
            dst_of(f, tile, side_tile(*packs[g], f, lane))


def place_rows(dst, own, upper, lower):
    dst[8:16, :CY] = upper
    dst[16 : 16 + CX, :CY] = own
    dst[16 + CX : 24 + CX, :CY] = lower


def zero_pads(ref, count):
    for l in range(count):
        ref[l, 0:8, :] = jnp.zeros((8, COLS), F32)
        ref[l, ROWS - 8 : ROWS, :] = jnp.zeros((8, COLS), F32)


def position():
    gy = lax.axis_index("gy")
    return gy % 2 == 0, gy == 0, gy == lax.axis_size("gy") - 1


class Strip:
    def __init__(self, r, first, last):
        self.r = r
        row, lane = iotas()
        self.row_first, self.row_last = row == 0, row == 7
        self.lane_first, self.lane_last = lane == 0, lane == LANES - 1
        self.inside = ((lane < 6) & jnp.logical_not(last)) | (
            (lane >= LANES - 6) & jnp.logical_not(first)
        )

    def load(self, ref, l, shift=0):
        rows = slice(self.r * 8 + shift, self.r * 8 + shift + 8)
        return [ref[l, rows, k * LANES : (k + 1) * LANES] for k in range(OWN_TILES + 1)]

    def spread(self, ref, l, d):
        x = self.load(ref, l)
        above = self.load(ref, l, -8)
        below = self.load(ref, l, 8)
        out = []
        n = len(x)
        for k in range(n):
            c = x[k]
            up = pltpu.roll(jnp.where(self.row_last, above[k], c), 1, 0)
            down = pltpu.roll(jnp.where(self.row_first, below[k], c), 7, 0)
            left = pltpu.roll(jnp.where(self.lane_last, x[k - 1], c), 1, 1)
            right = pltpu.roll(jnp.where(self.lane_first, x[(k + 1) % n], c), LANES - 1, 1)
            out.append(c + d * (((up + down) + (left + right)) - 4.0 * c))
        return out

    def store(self, ref, l, values):
        rows = slice(self.r * 8, self.r * 8 + 8)
        for k, v in enumerate(values):
            if k == OWN_TILES:
                v = jnp.where(self.inside, v, 0.0)
            ref[l, rows, k * LANES : (k + 1) * LANES] = v

    def save(self, ref, l, values):
        rows = slice(self.r * 8 - 8, self.r * 8)
        for k, v in enumerate(values):
            ref[l, rows, k * LANES : (k + 1) * LANES] = v

    def recall(self, ref, l):
        return self.load(ref, l, -8)


def flux_between(mix, lower, upper):
    return [mix * (a - b) for a, b in zip(lower, upper)]


def added(a, b):
    return [x + y for x, y in zip(a, b)]


def less(a, b):
    return [x - y for x, y in zip(a, b)]


def surface(v, f, c, m, ml, ocean):
    new, emitted = [], []
    for vk, fk, ck, mk, lk in zip(v, f, c, m, ml):
        mf = mk * fk
        flux = ck * (vk - (mf + lk))
        warmed = vk + ck * mf
        new.append(jnp.where(ocean, warmed, vk - flux))
        emitted.append(jnp.where(ocean, mk * warmed, flux))
    return new, emitted


def coefficient_place(i):
    rows, cols = i // 5 * 8, i % 5 * LANES
    return slice(rows, rows + 8), slice(cols, cols + LANES)


class Rows:
    def __init__(self, ref, start):
        self.ref, self.start = ref, start

    def __getitem__(self, l):
        return self.ref[self.start + l]


def coefficients(coeff):
    return Rows(coeff, 0), Rows(coeff, LEVELS)


def strips(t):
    return (1, 7) if t < SUB - 1 else (2, 6)


def write_series(series, emitted):
    for t in range(SUB):
        for half in range(CX // 16):
            rows = slice(8 + half * 16, 24 + half * 16)
            series[t, half * 16 : half * 16 + 16, :] = emitted[t, rows, :CY].astype(BF16)


AUX = 3 + SUB - 1


def aux_slots():
    n = 0
    for a in range(AUX):
        for i in range(SUB - 1 if a < 3 else SUB - 1 - (a - 3)):
            yield a, i, n // 2, n % 2
            n += 1


def first_edges(
    state, guess, coupling, land, mask,
    to_lower, to_upper,
    head, tail, ints, short, sems,
):
    n = 0
    copies = []

    def copy(src, dst):
        nonlocal n
        c = pltpu.make_async_copy(src, dst, sems.at[n])
        c.start()
        copies.append(c)
        n += 1

    for side, msg, buf in ((0, to_lower, head), (1, to_upper, tail)):
        rows = pl.ds(side * (CX - 8), 8)
        copy(state.at[:, rows, :], msg)
        copy(coupling.at[rows, :], buf.at[0])
        copy(land.at[rows, :], buf.at[1])
        copy(mask.at[rows, :], ints.at[side])
        copy(guess.at[pl.ds(0, SUB - 1), pl.ds(side * (CX - 16), 16), :], short.at[side])
    for c in copies:
        c.wait()
    for side, buf in ((0, head), (1, tail)):
        buf[2] = ints[side].astype(F32)
        for t in range(SUB - 1):
            rows16 = short[side, t].astype(F32)
            buf[3 + t] = rows16[8:] if side else rows16[:8]
    for a, i, tile, spare in aux_slots():
        to_lower[tile, 6 + spare : 7 + spare, :] = head[a, i : i + 1, :]
        to_upper[tile, spare : spare + 1, :] = tail[a, 7 - i : 8 - i, :]


def pack_first(
    state, guess, coupling, land, mask, upper, lower, before,
    aux, one, three,
):
    del before
    even, _, _ = position()
    aux[...] = jnp.zeros_like(aux)
    for a, i, tile, spare in aux_slots():
        aux[a, 7 - i : 8 - i, :] = upper[tile, spare : spare + 1, :]
        aux[a, 8 + i : 9 + i, :] = lower[tile, 6 + spare : 7 + spare, :]

    def field(f):
        def of(tile):
            rows = slice(0, 8)
            if tile in (0, 5):
                if f < LEVELS:
                    block = upper.at[f] if tile == 0 else lower.at[f]
                else:
                    block = aux.at[f - LEVELS]
                    rows = slice(0, 8) if tile == 0 else slice(8, 16)
            else:
                rows = slice(tile * 8 - 8, tile * 8)
                if f < LEVELS:
                    block = state.at[f]
                elif f == AT_COUPLING:
                    block = coupling
                elif f == AT_LAND:
                    block = land
                elif f == AT_MASK:
                    block = mask
                else:
                    block = guess.at[f - AT_GUESS]
                    base = (tile - 1) // 2 * 16
                    part = slice((tile - 1) % 2 * 8, (tile - 1) % 2 * 8 + 8)
                    head = block[base : base + 16, :LANES].astype(F32)[part]
                    tail = block[base : base + 16, CY - LANES :].astype(F32)[part]
                    return head, tail
            head, tail = block[rows, :LANES], block[rows, CY - LANES :]
            return head.astype(F32), tail.astype(F32)

        return of

    pack_columns([field(f) for f in range(N_FIELDS)], one, three, even)


CONE = SUB + 1


def first_cone(
    coeff, state, guess, coupling, land, mask, upper, lower, aux, one, three, beside,
    series, hd, ud, hs_out, us_out, fixed_out,
    s0, s1, g, emitted, hs, us, fixed, sems,
):
    del beside
    diff, mix = coefficients(coeff)
    writes = []

    def write(src, dst):
        c = pltpu.make_async_copy(src, dst, sems.at[len(writes)])
        c.start()
        writes.append(c)

    even, first, last = position()
    ocean = lax.axis_index("comp") == 1
    zero_pads(s0, CONE)
    zero_pads(s1, CONE - 1)
    for l in range(CONE):
        place_rows(s0.at[l], state[l], upper[l], lower[l])

    def rows_of(ref, k, f, own):
        ref[k, 0:8, :CY] = aux[f - LEVELS, 0:8, :]
        ref[k, 8 : 8 + CX, :CY] = own
        ref[k, 8 + CX : 16 + CX, :CY] = aux[f - LEVELS, 8:16, :]

    rows_of(fixed, 0, AT_COUPLING, coupling[...])
    rows_of(fixed, 1, AT_MASK, mask[...].astype(F32))
    rows_of(fixed, 2, AT_LAND, land[...])
    for t in range(SUB - 1):
        rows_of(g, t, AT_GUESS + t, guess[t].astype(F32))
    g[SUB - 1, 8 : 8 + CX, :CY] = guess[SUB - 1].astype(F32)

    side = slice(CY, COLS)
    slot = {AT_COUPLING: 0, AT_MASK: 1, AT_LAND: 2}

    def put(f, tile, value):
        rows = slice(tile * 8, tile * 8 + 8)
        if f < LEVELS:
            s0[f, tile * 8 + 8 : tile * 8 + 16, side] = value
        elif f < AT_GUESS:
            fixed[slot[f], rows, side] = value
        else:
            g[f - AT_GUESS, rows, side] = value

    fields = [*range(CONE), *range(LEVELS, N_FIELDS)]
    place_sides(put, fields, one, three, even, first, last)
    g[SUB - 1, :, side] = jnp.zeros((BAND, LANES), F32)
    fixed[2] = (1.0 - fixed[1]) * fixed[2]
    for l in range(SUB):
        for i, start in ((l, 0), (SUB + l, LEVELS)):
            rows, cols = coefficient_place(i)
            fixed[3, rows, cols] = coeff[start + l]
    write(fixed, fixed_out)

    for t in range(SUB):
        src, dst = (s0, s1) if t % 2 == 0 else (s1, s0)

        for r in range(*strips(t)):
            strip = Strip(r, first, last)
            h = strip.spread(src, 0, diff[0])
            u_prev = None
            for l in range(SUB - t):
                h_next = strip.spread(src, l + 1, diff[l + 1])
                u = flux_between(mix[l], h_next, h)
                v = added(h, u)
                if l == t and t < 3:
                    strip.save(us, t, v)
                    if t:
                        strip.save(hs, t - 1, h)
                if u_prev is not None:
                    v = less(v, u_prev)
                if l == 0:
                    c, m, ml = (strip.recall(fixed, i) for i in range(3))
                    v, e = surface(v, strip.recall(g, t), c, m, ml, ocean)
                    strip.save(emitted, t, e[:OWN_TILES])
                if t < SUB - 1:
                    strip.store(dst, l, v)
                h, u_prev = h_next, u
            strip.save(hd, t, h)
            strip.save(ud, t, u_prev)
            if t == 3:
                strip.save(hs, 2, h)
        if t < 3:
            write(us.at[t], us_out.at[t])
        if 0 < t < 4:
            write(hs.at[t - 1], hs_out.at[t - 1])

    write_series(series, emitted)
    for c in writes:
        c.wait()


def first_rest(
    coeff, state, upper, lower, one, three, hd, ud,
    final, hs_out, us_out, token,
    s0, s1, hs, us, sems,
):
    diff, mix = coefficients(coeff)
    token[...] = jnp.zeros_like(token)
    even, first, last = position()
    zero_pads(s0, LEVELS)
    zero_pads(s1, LEVELS)
    for l in range(CONE, LEVELS):
        place_rows(s0.at[l], state[l], upper[l], lower[l])

    def put(f, tile, value):
        s0[f, tile * 8 + 8 : tile * 8 + 16, CY:COLS] = value

    place_sides(put, list(range(CONE, LEVELS)), one, three, even, first, last)

    for t in range(SUB):
        src, dst = (s0, s1) if t % 2 == 0 else (s1, s0)

        for r in range(*strips(t)):
            strip = Strip(r, first, last)
            h = strip.recall(hd, t)
            u_prev = strip.recall(ud, t)
            for l in range(SUB - t, LEVELS):
                if l < LEVELS - 1:
                    h_next = strip.spread(src, l + 1, diff[l + 1])
                    u = flux_between(mix[l], h_next, h)
                    v = added(h, u)
                else:
                    h_next = u = None
                    v = h
                if l == t and t >= 3:
                    strip.save(us, t - 3, v)
                    strip.save(hs, t - 3, h)
                v = less(v, u_prev)
                if t < SUB - 1:
                    strip.store(dst, l, v)
                elif l >= SUB:
                    rows = slice(r * 8 - 16, r * 8 - 8)
                    for k in range(OWN_TILES):
                        final[l, rows, k * LANES : (k + 1) * LANES] = v[k]
                h, u_prev = h_next, u
    writes = [
        pltpu.make_async_copy(hs, hs_out, sems.at[0]),
        pltpu.make_async_copy(us, us_out, sems.at[1]),
    ]
    for c in writes:
        c.start()
    for c in writes:
        c.wait()


def balance(
    diff, mix, src, pat, weights, mask, after,
    out, wet, coeff,
    m, z, b, sem, *totals,
):
    del after
    for l in range(LEVELS):
        coeff[l] = jnp.full((8, LANES), diff[l], F32)
    for l in range(LEVELS - 1):
        coeff[LEVELS + l] = jnp.full((8, LANES), mix[l], F32)
    coeff[2 * LEVELS - 1] = jnp.zeros((8, LANES), F32)
    count = jnp.zeros((8, LANES), F32)
    for part in range(CX // 8):
        for j in range(OWN_TILES):
            v = mask[part * 8 : part * 8 + 8, j * LANES : (j + 1) * LANES].astype(F32)
            count += v
            m[pl.ds(part * 8 * OWN_TILES + j, 8, stride=OWN_TILES), :] = v
    _, lane = iotas()
    count = jnp.sum(count, axis=(0, 1), keepdims=True)
    wet[...] = jnp.where(lane[:1] == SUB, count, 0.0)
    blocks = m[...].astype(BF16)

    @pl.loop(0, PATTERNS, unroll=8)
    def _(p):
        z[p] = lax.dot_general(
            blocks, weights[p], (((1,), (1,)), ((), ())), preferred_element_type=F32
        )

    for j in range(OWN_TILES):
        totals[j][...] = jnp.zeros_like(totals[j])

    @pl.loop(0, CX, unroll=4)
    def _(r):
        for k in range(2):
            for j in range(OWN_TILES):
                row = pl.ds(src[j, k, r], 1)
                line = z[pat[j, k, r], pl.ds(r * OWN_TILES + j, 1), :]
                totals[j][row, :] = totals[j][row, :] + line

    m[...] = m[...] - ((totals[0][...] + totals[1][...]) + (totals[2][...] + totals[3][...]))
    for part in range(CX // 8):
        for j in range(OWN_TILES):
            v = m[pl.ds(part * 8 * OWN_TILES + j, 8, stride=OWN_TILES), :]
            b[part * 8 : part * 8 + 8, j * LANES : (j + 1) * LANES] = v
    c = pltpu.make_async_copy(b, out, sem)
    c.start()
    c.wait()


def share_rows(series, factor, wet, rows):
    partial = [jnp.zeros((8, LANES), F32) for _ in range(SUB)]
    for half in range(CX // 16):
        for j in range(OWN_TILES):
            cols = slice(j * LANES, (j + 1) * LANES)
            f = factor[half * 16 : half * 16 + 16, cols]
            for t in range(SUB):
                p = f * series[t, half * 16 : half * 16 + 16, cols].astype(F32)
                partial[t] += p[:8] + p[8:]
    row, lane = iotas()
    total = jnp.zeros((8, LANES), F32)
    for t, value in enumerate(partial):
        total = jnp.where(row == t, jnp.sum(value, axis=0, keepdims=True), total)
    total = jnp.sum(total, axis=1, keepdims=True)
    total = jnp.sum(jnp.where(row == lane, total, 0.0), axis=0, keepdims=True) + wet[...]
    for k in range(rows.shape[0]):
        rows[k] = total


def losses(
    received, factor, wet, before,
    gap, token,
    rows, sem,
):
    del before
    token[...] = jnp.zeros_like(token)
    share_rows(received, factor, wet, rows)
    c = pltpu.make_async_copy(rows, gap, sem)
    c.start()
    c.wait()


def edge_slots():
    for t, tile, start in ((0, 0, 0), (2, 0, 5), (1, 1, 0), (3, 1, 4), (4, 1, 6)):
        yield t, SUB - 1 - t, tile, start


def regrid(
    src, pat, received, weights_in, before,
    out, top, bottom,
    x, y, weights, sem,
):
    del before
    read = pltpu.make_async_copy(weights_in, weights, sem)
    read.start()
    for half in range(CX // 16):
        for j in range(OWN_TILES):
            cols = slice(j * LANES, (j + 1) * LANES)
            for t in range(SUB):
                v16 = received[t, half * 16 : half * 16 + 16, cols].astype(F32)
                for part in range(2):
                    row = half * 16 + part * 8
                    start = (row * OWN_TILES + j) * 8 + t
                    x[pl.ds(start, 8, stride=OWN_TILES * 8), :] = v16[part * 8 : part * 8 + 8]
    read.wait()
    for r in range(CX):
        for j in range(OWN_TILES):
            a, w = [], []
            for k in range(2):
                start = pl.multiple_of(src[j, k, r] * 8, 8)
                a.append(x[pl.ds(start, 8), :].astype(BF16))
                w.append(weights[pat[j, k, r]])
            product = jnp.dot(
                jnp.concatenate(a, 1), jnp.concatenate(w, 0), preferred_element_type=F32
            )
            y[pl.ds(r * OWN_TILES + j, 8, stride=BLOCKS), :] = product

    for part in range(CX // 8):
        for j in range(OWN_TILES):
            cols = slice(j * LANES, (j + 1) * LANES)
            for t in range(SUB):
                start = t * BLOCKS + part * 8 * OWN_TILES + j
                out[t, part * 8 : part * 8 + 8, cols] = y[pl.ds(start, 8, stride=OWN_TILES), :]
    top[1, 7:8, :] = jnp.zeros((1, CY), F32)
    bottom[1, 7:8, :] = jnp.zeros((1, CY), F32)
    for t, n, tile, start in edge_slots():
        top[tile, start : start + n, :] = out[t, 0:n, :]
        bottom[tile, start : start + n, :] = out[t, CX - n : CX, :]


def halo_rows(halo, upper, lower):
    halo[...] = jnp.zeros_like(halo)
    for t, n, tile, start in edge_slots():
        halo[t, 8 - n : 8, :] = upper[tile, start : start + n, :]
        halo[t, 8 : 8 + n, :] = lower[tile, start : start + n, :]


def pack_second(out, upper_in, lower_in, one, three, halo, upper, lower, sems):
    reads = [
        pltpu.make_async_copy(upper_in, upper, sems.at[0]),
        pltpu.make_async_copy(lower_in, lower, sems.at[1]),
    ]
    for c in reads:
        c.start()
    for c in reads:
        c.wait()
    even, _, _ = position()
    halo_rows(halo, upper, lower)

    def field(t):
        def of(tile):
            if tile in (0, 5):
                block, rows = halo.at[t], slice(0, 8) if tile == 0 else slice(8, 16)
            else:
                block, rows = out.at[t], slice(tile * 8 - 8, tile * 8)
            return block[rows, :LANES], block[rows, CY - LANES :]

        return of

    pack_columns([field(t) for t in range(SUB - 1)], one, three, even)


def gap_means(gap, start, count):
    total = jnp.sum(gap[pl.ds(start, count)], axis=0)
    lane = lax.broadcasted_iota(jnp.int32, (1, LANES), 1)
    wet = jnp.sum(jnp.where(lane == SUB, total, 0.0), axis=1, keepdims=True)
    return [
        jnp.sum(jnp.where(lane == t, total, 0.0), axis=1, keepdims=True) / wet for t in range(SUB)
    ]


def second_cone(
    fixed_in, regridded, upper_in, lower_in, one_in, three_in, gap_in, hs_in, us_in,
    series, final0, hx, ux, coeff,
    s0, s1, g, emitted, fixed, hs, us, halo, upper, lower, one, three, gap, sems,
):
    reads = []
    pairs = (
        (upper_in, upper), (lower_in, lower), (one_in, one), (three_in, three), (gap_in, gap),
        (us_in, us), (fixed_in, fixed), (hs_in, hs),
    )
    for i, (src, dst) in enumerate(pairs):
        reads.append(pltpu.make_async_copy(src, dst, sems.at[i]))
        reads[-1].start()
    even, first, last = position()
    ocean = lax.axis_index("comp") == 1
    zero_pads(s0, 3)
    zero_pads(s1, 3)
    for t in range(SUB):
        g[t, 8 : 8 + CX, :CY] = regridded[t]
    for c in reads[:5]:
        c.wait()
    halo_rows(halo, upper, lower)
    for t in range(SUB):
        if t < SUB - 1:
            g[t, 0:8, :CY] = halo[t, 0:8, :]
            g[t, 8 + CX : 16 + CX, :CY] = halo[t, 8:16, :]

    def put(f, tile, value):
        g[f, tile * 8 : tile * 8 + 8, CY:COLS] = value

    place_sides(put, list(range(SUB - 1)), one, three, even, first, last)
    g[SUB - 1, :, CY:COLS] = jnp.zeros((BAND, LANES), F32)
    means = [jnp.broadcast_to(v, (8, LANES)) for v in gap_means(gap, 0, gap.shape[0])]
    for c in reads[5:]:
        c.wait()
    for l in range(SUB):
        for i, start in ((l, 0), (SUB + l, LEVELS)):
            coeff[start + l] = fixed[(3, *coefficient_place(i))]
    diff, mix = coefficients(coeff)

    for t in range(SUB):
        src, dst = (s0, s1) if t % 2 == 0 else (s1, s0)

        for r in range(*strips(t)):
            strip = Strip(r, first, last)
            h = strip.spread(src, 0, diff[0]) if t else None
            u_prev = None
            for l in range(min(t, SUB - 1 - t) + 1):
                if l < t:
                    if l + 1 < t:
                        h_next = strip.spread(src, l + 1, diff[l + 1])
                    else:
                        h_next = strip.recall(hs, t - 1)
                    u = flux_between(mix[l], h_next, h)
                    v = added(h, u)
                else:
                    v = strip.recall(us, t)
                if u_prev is not None:
                    v = less(v, u_prev)
                if l == 0:
                    c, m, ml = (strip.recall(fixed, i) for i in range(3))
                    f = [a + b * means[t] for a, b in zip(strip.recall(g, t), m)]
                    v, e = surface(v, f, c, m, ml, ocean)
                    strip.save(emitted, t, e[:OWN_TILES])
                    if t == SUB - 1:
                        rows = slice(r * 8 - 16, r * 8 - 8)
                        for k in range(OWN_TILES):
                            final0[rows, k * LANES : (k + 1) * LANES] = v[k]
                if t < SUB - 1:
                    strip.store(dst, l, v)
                if l < t:
                    h, u_prev = h_next, u
            if t >= 3:
                strip.save(hx, t - 3, h)
                strip.save(ux, t - 3, u_prev)

    write_series(series, emitted)


def second_rest(
    coeff, hx, ux, hs_in, us_in, final0, series, factor, wet, whole,
    final, token, gap,
    s0, s1, hs, us, shares, sems,
):
    del whole
    share_rows(series, factor, wet, shares)
    send = pltpu.make_async_copy(shares, gap, sems.at[2])
    send.start()
    diff, mix = coefficients(coeff)
    reads = [
        pltpu.make_async_copy(us_in, us, sems.at[0]),
        pltpu.make_async_copy(hs_in, hs, sems.at[1]),
    ]
    for c in reads:
        c.start()
    token[...] = jnp.zeros_like(token)
    gy = lax.axis_index("gy")
    first, last = gy == 0, gy == lax.axis_size("gy") - 1
    zero_pads(s0, SUB)
    zero_pads(s1, SUB)
    final[0] = final0[...]
    for c in reads:
        c.wait()
    for t in range(3, SUB):
        src, dst = (s0, s1) if t % 2 == 0 else (s1, s0)

        for r in range(*strips(t)):
            strip = Strip(r, first, last)
            h = strip.recall(hx, t - 3)
            u_prev = strip.recall(ux, t - 3)
            for l in range(SUB - t, t + 1):
                if l < t:
                    if l + 1 < t:
                        h_next = strip.spread(src, l + 1, diff[l + 1])
                    else:
                        h_next = strip.recall(hs, t - 3)
                    u = flux_between(mix[l], h_next, h)
                    v = added(h, u)
                    h = h_next
                else:
                    u = None
                    v = strip.recall(us, t - 3)
                v = less(v, u_prev)
                u_prev = u
                if t < SUB - 1:
                    strip.store(dst, l, v)
                else:
                    rows = slice(r * 8 - 16, r * 8 - 8)
                    for k in range(OWN_TILES):
                        final[l, rows, k * LANES : (k + 1) * LANES] = v[k]
    send.wait()


def finish(regridded, mask, gap, forcing):
    peers = gap.shape[0] // 2
    start = (1 - lax.axis_index("comp")) * peers
    for t, mean in enumerate(gap_means(gap, start, peers)):
        forcing[t] = regridded[t] + mask[...].astype(F32) * mean


def shifted(value, axis, by):
    n = lax.axis_size(axis)
    return lax.ppermute(value, axis, [(i, (i + by) % n) for i in range(n)])


def paired(value, axis, mask):
    return lax.ppermute(value, axis, [(i, i ^ mask) for i in range(lax.axis_size(axis))])


def per_device(
    state, guess, diffusion, mixing, coupling, land_temp, land_mask, weights, source_block, pattern
):
    state, guess, diff, mix, coupling = state[0], guess[0], diffusion[0], mixing[0], coupling[0]
    weights = weights[0]
    src = source_block[0].transpose(1, 2, 0)
    pat = pattern[0].transpose(1, 2, 0)
    band = lambda n: shape(n, BAND, COLS)
    field_buf = lambda n: pltpu.VMEM((n, ROWS, COLS), F32)
    band_buf = lambda n: pltpu.VMEM((n, BAND, COLS), F32)
    numbers = shape(2 * LEVELS, 8, LANES)

    message = shape(LEVELS, 8, CY)
    to_lower, to_upper = call(
        first_edges,
        [message, message],
        [
            pltpu.VMEM((AUX, 8, CY), F32),
            pltpu.VMEM((AUX, 8, CY), F32),
            pltpu.VMEM((2, 8, CY), jnp.int32),
            pltpu.VMEM((2, SUB - 1, 16, CY), BF16),
            pltpu.SemaphoreType.DMA((10,)),
        ],
        [HBM] * 5,
        grant=EDGE_GRANT,
    )(state, guess, coupling, land_temp, land_mask)
    state, guess, coupling, land_temp, mask, table, src, pat, to_lower, to_upper = (
        lax.optimization_barrier(
            (
                state, guess, coupling, land_temp, land_mask, weights, src, pat,
                to_lower, to_upper,
            )
        )
    )
    lower, upper = shifted(to_lower, "gx", -1), shifted(to_upper, "gx", 1)
    factor, wet, coeff = call(
        balance,
        [shape(CX, CY), shape(1, LANES), shape(2 * LEVELS, 8, LANES)],
        [
            pltpu.VMEM((BLOCKS, LANES), F32),
            pltpu.VMEM((PATTERNS, BLOCKS, LANES), F32),
            pltpu.VMEM((CX, CY), F32),
            pltpu.SemaphoreType.DMA(()),
            *[pltpu.VMEM((BLOCKS, LANES), F32)] * OWN_TILES,
        ],
        [SM, SM, SM, SM, VM, VM, VM],
        out_specs=[HBM, VM, VM],
    )(diff, mix, src, pat, table, mask, to_lower)
    other = paired(factor, "comp", 1)
    packed = shape(BAND, PACK_LANES)
    aux, one, three = call(pack_first, [shape(AUX, 16, CY), packed, packed], [], [VM] * 8)(
        state, guess, coupling, land_temp, mask, upper, lower, wet
    )
    one, three = paired(one, "gy", 1), paired(three, "gy", 3)

    series, hd, ud, hs, us, fixed = call(
        first_cone,
        [
            shape(SUB, CX, CY, dtype=BF16), band(SUB), band(SUB),
            band(3), band(3), band(4),
        ],
        [
            field_buf(CONE), field_buf(CONE), band_buf(SUB), band_buf(SUB),
            band_buf(3), band_buf(3), band_buf(4), pltpu.SemaphoreType.DMA((7,)),
        ],
        [VM] * 11 + [pl.BlockSpec(memory_space=pl.ANY)],
        out_specs=[VM] * 3 + [HBM] * 3,
    )(coeff, state, guess, coupling, land_temp, mask, upper, lower, aux, one, three, other)

    def regridded(received, before):
        edges = shape(2, 8, CY)
        return call(
            regrid,
            [shape(SUB, CX, CY), edges, edges],
            [
                pltpu.VMEM((BLOCKS * 8, LANES), F32),
                pltpu.VMEM((BLOCKS * 8, LANES), F32),
                pltpu.VMEM((PATTERNS, LANES, LANES), BF16),
                pltpu.SemaphoreType.DMA(()),
            ],
            [SM, SM, VM, HBM, VM],
            cost_estimate=pl.CostEstimate(
                flops=2 * BLOCKS * 8 * 2 * LANES * LANES,
                bytes_accessed=BLOCKS * 2 * LANES * LANES * 2,
                transcendentals=0,
            ),
        )(src, pat, received, weights, before)

    whole, hs_rest, us_rest, token = call(
        first_rest,
        [shape(LEVELS, CX, CY), band(3), band(3), shape(8, LANES)],
        [
            field_buf(LEVELS), field_buf(LEVELS),
            band_buf(3), band_buf(3), pltpu.SemaphoreType.DMA((2,)),
        ],
        [VM] * 8,
        out_specs=[VM, HBM, HBM, VM],
    )(coeff, state, upper, lower, one, three, hd, ud)

    received = paired(series, "comp", 1)
    peers = lax.axis_size(("gx", "gy"))
    gap, after = call(
        losses,
        [shape(peers, 1, LANES), shape(8, LANES)],
        [pltpu.VMEM((peers, 1, LANES), F32), pltpu.SemaphoreType.DMA(())],
        [VM, VM, VM, VM],
        out_specs=[HBM, VM],
    )(received, factor, wet, token)
    gap = lax.all_to_all(gap, ("gx", "gy"), 0, 0)
    out, top, bottom = regridded(received, after)
    lower, upper = shifted(top, "gx", -1), shifted(bottom, "gx", 1)
    packed = shape(BAND, LANES)
    one, three = call(
        pack_second,
        [packed, packed],
        [
            pltpu.VMEM((SUB - 1, 16, CY), F32),
            pltpu.VMEM(upper.shape, F32),
            pltpu.VMEM(lower.shape, F32),
            pltpu.SemaphoreType.DMA((2,)),
        ],
        [VM, HBM, HBM],
    )(out, upper, lower)
    one, three = paired(one, "gy", 1), paired(three, "gy", 3)

    series, final0, hx, ux, coeff = call(
        second_cone,
        [shape(SUB, CX, CY, dtype=BF16), shape(CX, CY), band(3), band(3), numbers],
        [
            field_buf(3), field_buf(3), band_buf(SUB), band_buf(SUB),
            band_buf(4), band_buf(3), band_buf(3), pltpu.VMEM((SUB - 1, 16, CY), F32),
            *[pltpu.VMEM(v.shape, F32) for v in (upper, lower, one, three, gap)],
            pltpu.SemaphoreType.DMA((8,)),
        ],
        [HBM, VM] + [HBM] * 7,
    )(fixed, out, upper, lower, one, three, gap, hs, us)

    everyone = shape(2 * peers, 1, LANES)
    whole, token, gap = call(
        second_rest,
        [shape(LEVELS, CX, CY), shape(8, LANES), everyone],
        [
            field_buf(SUB), field_buf(SUB), band_buf(3), band_buf(3),
            pltpu.VMEM(everyone.shape, F32), pltpu.SemaphoreType.DMA((3,)),
        ],
        [VM, VM, VM, HBM, HBM, VM, VM, VM, VM, pl.BlockSpec(memory_space=pl.ANY)],
        out_specs=[pl.BlockSpec((SUB, CX, CY), lambda i: (0, 0, 0)), VM, HBM],
        grid=(1,),
        input_output_aliases={9: 0},
    )(coeff, hx, ux, hs_rest, us_rest, final0, series, other, wet, whole)

    received = paired(series, "comp", 1)
    gap = lax.all_to_all(gap, ("comp", "gx", "gy"), 0, 0)
    out, _, _ = regridded(received, token)
    (forcing,) = call(finish, [shape(SUB, CX, CY)], [], [VM] * 3)(out, land_mask, gap)
    return whole[None], forcing[None]


def solution(mesh):
    placed = (
        P("comp", None, "gx", "gy"),
        P("comp", None, "gx", "gy"),
        P("comp", None),
        P("comp", None),
        P("comp", "gx", "gy"),
        P("gx", "gy"),
        P("gx", "gy"),
        P("comp", ("gx", "gy"), None, None),
        P("comp", "gx", "gy", None),
        P("comp", "gx", "gy", None),
    )
    return jax.shard_map(
        per_device,
        mesh=mesh,
        in_specs=placed,
        out_specs=(P("comp", None, "gx", "gy"), P("comp", None, "gx", "gy")),
        check_vma=False,
    )
```

```python
import jax
import jax.numpy as jnp
from jax import lax
from jax.experimental import pallas as pl
from jax.experimental.pallas import tpu as pltpu
from jax.sharding import PartitionSpec as P

F32 = jnp.float32
BF16 = jnp.bfloat16
SUB = 6
LEVELS = 16
CX = 32
CY = 512
LANES = 128
OWN_TILES = CY // LANES
COLS = CY + LANES
ROWS = CX + 32
BAND = CX + 16
PATTERNS = 32
BLOCKS = CX * OWN_TILES
VMEM_LIMIT = 12 * 1024 * 1024
EDGE_GRANT = 60 * 1024 * 1024

N_FIELDS = LEVELS + 3 + SUB - 1
AT_COUPLING, AT_LAND, AT_MASK, AT_GUESS = LEVELS, LEVELS + 1, LEVELS + 2, LEVELS + 3
PACK_LANES = 256

VM = pl.BlockSpec(memory_space=pltpu.VMEM)
SM = pl.BlockSpec(memory_space=pltpu.SMEM)
HBM = pl.BlockSpec(memory_space=pltpu.HBM)


def shape(*dims, dtype=F32):
    return jax.ShapeDtypeStruct(dims, dtype)


def call(body, outs, scratch, ins, out_specs=None, grant=VMEM_LIMIT, **kw):
    return pl.pallas_call(
        body,
        out_shape=outs,
        in_specs=ins,
        out_specs=[VM] * len(outs) if out_specs is None else out_specs,
        scratch_shapes=scratch,
        compiler_params=pltpu.CompilerParams(vmem_limit_bytes=grant),
        **kw,
    )


def iotas():
    row = lax.broadcasted_iota(jnp.int32, (8, LANES), 0)
    lane = lax.broadcasted_iota(jnp.int32, (8, LANES), 1)
    return row, lane


def roll_lanes(x, shift):
    shift %= LANES
    return x if shift == 0 else pltpu.roll(x, shift, 1)


def pack_columns(fields, one, three, even):
    _, lane = iotas()
    groups = PACK_LANES // LANES if len(fields) > 16 else 1
    for tile in range(6):
        for g in range(groups):
            left = jnp.zeros((8, LANES), F32)
            right = jnp.zeros((8, LANES), F32)
            for f in range(g * 16, min(len(fields), g * 16 + 16)):
                at = (f % 16) * 8
                head, tail = fields[f](tile)
                left = jnp.where((lane >= at) & (lane < at + 8), roll_lanes(head, at), left)
                right = jnp.where((lane >= at) & (lane < at + 8), roll_lanes(tail, at + 8), right)
            span = (slice(tile * 8, tile * 8 + 8), slice(g * LANES, (g + 1) * LANES))
            one[span] = jnp.where(even, right, left)
            three[span] = jnp.where(even, left, right)


def side_halos(one, three, even, first, last, tile, g):
    span = (slice(tile * 8, tile * 8 + 8), slice(g * LANES, (g + 1) * LANES))
    a, b = one[span], three[span]
    right = jnp.where(last, 0.0, jnp.where(even, a, b))
    left = jnp.where(first, 0.0, jnp.where(even, b, a))
    return right, left


def side_tile(right, left, f, lane):
    at = (f % 16) * 8
    return jnp.where(
        lane < 6,
        roll_lanes(right, -at),
        jnp.where(lane >= LANES - 6, roll_lanes(left, LANES - 8 - at), 0.0),
    )


def place_sides(dst_of, fields, one, three, even, first, last):
    _, lane = iotas()
    for tile in range(6):
        packs = {}
        for f in fields:
            g = f // 16
            if g not in packs:
                packs[g] = side_halos(one, three, even, first, last, tile, g)
            dst_of(f, tile, side_tile(*packs[g], f, lane))


def place_rows(dst, own, upper, lower):
    dst[8:16, :CY] = upper
    dst[16 : 16 + CX, :CY] = own
    dst[16 + CX : 24 + CX, :CY] = lower


def zero_pads(ref, count):
    for l in range(count):
        ref[l, 0:8, :] = jnp.zeros((8, COLS), F32)
        ref[l, ROWS - 8 : ROWS, :] = jnp.zeros((8, COLS), F32)


def position():
    gy = lax.axis_index("gy")
    return gy % 2 == 0, gy == 0, gy == lax.axis_size("gy") - 1


class Strip:
    def __init__(self, r, first, last):
        self.r = r
        row, lane = iotas()
        self.row_first, self.row_last = row == 0, row == 7
        self.lane_first, self.lane_last = lane == 0, lane == LANES - 1
        self.inside = ((lane < 6) & jnp.logical_not(last)) | (
            (lane >= LANES - 6) & jnp.logical_not(first)
        )

    def load(self, ref, l, shift=0):
        rows = slice(self.r * 8 + shift, self.r * 8 + shift + 8)
        return [ref[l, rows, k * LANES : (k + 1) * LANES] for k in range(OWN_TILES + 1)]

    def spread(self, ref, l, d):
        x = self.load(ref, l)
        above = self.load(ref, l, -8)
        below = self.load(ref, l, 8)
        out = []
        n = len(x)
        for k in range(n):
            c = x[k]
            up = pltpu.roll(jnp.where(self.row_last, above[k], c), 1, 0)
            down = pltpu.roll(jnp.where(self.row_first, below[k], c), 7, 0)
            left = pltpu.roll(jnp.where(self.lane_last, x[k - 1], c), 1, 1)
            right = pltpu.roll(jnp.where(self.lane_first, x[(k + 1) % n], c), LANES - 1, 1)
            out.append(c + d * (((up + down) + (left + right)) - 4.0 * c))
        return out

    def store(self, ref, l, values):
        rows = slice(self.r * 8, self.r * 8 + 8)
        for k, v in enumerate(values):
            if k == OWN_TILES:
                v = jnp.where(self.inside, v, 0.0)
            ref[l, rows, k * LANES : (k + 1) * LANES] = v

    def save(self, ref, l, values):
        rows = slice(self.r * 8 - 8, self.r * 8)
        for k, v in enumerate(values):
            ref[l, rows, k * LANES : (k + 1) * LANES] = v

    def recall(self, ref, l):
        return self.load(ref, l, -8)


def flux_between(mix, lower, upper):
    return [mix * (a - b) for a, b in zip(lower, upper)]


def added(a, b):
    return [x + y for x, y in zip(a, b)]


def less(a, b):
    return [x - y for x, y in zip(a, b)]


def surface(v, f, c, m, ml, ocean):
    new, emitted = [], []
    for vk, fk, ck, mk, lk in zip(v, f, c, m, ml):
        mf = mk * fk
        flux = ck * (vk - (mf + lk))
        warmed = vk + ck * mf
        new.append(jnp.where(ocean, warmed, vk - flux))
        emitted.append(jnp.where(ocean, mk * warmed, flux))
    return new, emitted


def coefficient_place(i):
    rows, cols = i // 5 * 8, i % 5 * LANES
    return slice(rows, rows + 8), slice(cols, cols + LANES)


class Rows:
    def __init__(self, ref, start):
        self.ref, self.start = ref, start

    def __getitem__(self, l):
        return self.ref[self.start + l]


def coefficients(coeff):
    return Rows(coeff, 0), Rows(coeff, LEVELS)


def strips(t):
    return (1, 7) if t < SUB - 1 else (2, 6)


def write_series(series, emitted):
    for t in range(SUB):
        for half in range(CX // 16):
            rows = slice(8 + half * 16, 24 + half * 16)
            series[t, half * 16 : half * 16 + 16, :] = emitted[t, rows, :CY].astype(BF16)


AUX = 3 + SUB - 1


def aux_slots():
    n = 0
    for a in range(AUX):
        for i in range(SUB - 1 if a < 3 else SUB - 1 - (a - 3)):
            yield a, i, n // 2, n % 2
            n += 1


def first_edges(
    state, guess, coupling, land, mask,
    to_lower, to_upper,
    head, tail, ints, short, sems,
):
    n = 0
    copies = []

    def copy(src, dst):
        nonlocal n
        c = pltpu.make_async_copy(src, dst, sems.at[n])
        c.start()
        copies.append(c)
        n += 1

    for side, msg, buf in ((0, to_lower, head), (1, to_upper, tail)):
        rows = pl.ds(side * (CX - 8), 8)
        copy(state.at[:, rows, :], msg)
        copy(coupling.at[rows, :], buf.at[0])
        copy(land.at[rows, :], buf.at[1])
        copy(mask.at[rows, :], ints.at[side])
        copy(guess.at[pl.ds(0, SUB - 1), pl.ds(side * (CX - 16), 16), :], short.at[side])
    for c in copies[1:5] + copies[6:]:
        c.wait()
    for side, buf in ((0, head), (1, tail)):
        buf[2] = ints[side].astype(F32)
        for t in range(SUB - 1):
            rows16 = short[side, t].astype(F32)
            buf[3 + t] = rows16[8:] if side else rows16[:8]
    for c in (copies[0], copies[5]):
        c.wait()
    for a, i, tile, spare in aux_slots():
        to_lower[tile, 6 + spare : 7 + spare, :] = head[a, i : i + 1, :]
        to_upper[tile, spare : spare + 1, :] = tail[a, 7 - i : 8 - i, :]


def pack_first(
    state, guess, coupling, land, mask, upper, lower, before,
    aux, one, three,
):
    del before
    even, _, _ = position()
    aux[...] = jnp.zeros_like(aux)
    for a, i, tile, spare in aux_slots():
        aux[a, 7 - i : 8 - i, :] = upper[tile, spare : spare + 1, :]
        aux[a, 8 + i : 9 + i, :] = lower[tile, 6 + spare : 7 + spare, :]

    def field(f):
        def of(tile):
            rows = slice(0, 8)
            if tile in (0, 5):
                if f < LEVELS:
                    block = upper.at[f] if tile == 0 else lower.at[f]
                else:
                    block = aux.at[f - LEVELS]
                    rows = slice(0, 8) if tile == 0 else slice(8, 16)
            else:
                rows = slice(tile * 8 - 8, tile * 8)
                if f < LEVELS:
                    block = state.at[f]
                elif f == AT_COUPLING:
                    block = coupling
                elif f == AT_LAND:
                    block = land
                elif f == AT_MASK:
                    block = mask
                else:
                    block = guess.at[f - AT_GUESS]
                    base = (tile - 1) // 2 * 16
                    part = slice((tile - 1) % 2 * 8, (tile - 1) % 2 * 8 + 8)
                    head = block[base : base + 16, :LANES].astype(F32)[part]
                    tail = block[base : base + 16, CY - LANES :].astype(F32)[part]
                    return head, tail
            head, tail = block[rows, :LANES], block[rows, CY - LANES :]
            return head.astype(F32), tail.astype(F32)

        return of

    pack_columns([field(f) for f in range(N_FIELDS)], one, three, even)


CONE = SUB + 1


def first_cone(
    coeff, state, guess, coupling, land, mask, upper, lower, aux, one, three, beside,
    series, hd, ud, hs_out, us_out, fixed_out,
    s0, s1, g, emitted, hs, us, fixed, sems,
):
    del beside
    diff, mix = coefficients(coeff)
    writes = []

    def write(src, dst):
        c = pltpu.make_async_copy(src, dst, sems.at[len(writes)])
        c.start()
        writes.append(c)

    even, first, last = position()
    ocean = lax.axis_index("comp") == 1
    zero_pads(s0, CONE)
    zero_pads(s1, CONE - 1)
    for l in range(CONE):
        place_rows(s0.at[l], state[l], upper[l], lower[l])

    def rows_of(ref, k, f, own):
        ref[k, 0:8, :CY] = aux[f - LEVELS, 0:8, :]
        ref[k, 8 : 8 + CX, :CY] = own
        ref[k, 8 + CX : 16 + CX, :CY] = aux[f - LEVELS, 8:16, :]

    rows_of(fixed, 0, AT_COUPLING, coupling[...])
    rows_of(fixed, 1, AT_MASK, mask[...].astype(F32))
    rows_of(fixed, 2, AT_LAND, land[...])
    for t in range(SUB - 1):
        rows_of(g, t, AT_GUESS + t, guess[t].astype(F32))
    g[SUB - 1, 8 : 8 + CX, :CY] = guess[SUB - 1].astype(F32)

    side = slice(CY, COLS)
    slot = {AT_COUPLING: 0, AT_MASK: 1, AT_LAND: 2}

    def put(f, tile, value):
        rows = slice(tile * 8, tile * 8 + 8)
        if f < LEVELS:
            s0[f, tile * 8 + 8 : tile * 8 + 16, side] = value
        elif f < AT_GUESS:
            fixed[slot[f], rows, side] = value
        else:
            g[f - AT_GUESS, rows, side] = value

    fields = [*range(CONE), *range(LEVELS, N_FIELDS)]
    place_sides(put, fields, one, three, even, first, last)
    g[SUB - 1, :, side] = jnp.zeros((BAND, LANES), F32)
    fixed[2] = (1.0 - fixed[1]) * fixed[2]
    for l in range(SUB):
        for i, start in ((l, 0), (SUB + l, LEVELS)):
            rows, cols = coefficient_place(i)
            fixed[3, rows, cols] = coeff[start + l]
    write(fixed, fixed_out)

    for t in range(SUB):
        src, dst = (s0, s1) if t % 2 == 0 else (s1, s0)

        for r in range(*strips(t)):
            strip = Strip(r, first, last)
            h = strip.spread(src, 0, diff[0])
            u_prev = None
            for l in range(SUB - t):
                h_next = strip.spread(src, l + 1, diff[l + 1])
                u = flux_between(mix[l], h_next, h)
                v = added(h, u)
                if l == t and t < 3:
                    strip.save(us, t, v)
                    if t:
                        strip.save(hs, t - 1, h)
                if u_prev is not None:
                    v = less(v, u_prev)
                if l == 0:
                    c, m, ml = (strip.recall(fixed, i) for i in range(3))
                    v, e = surface(v, strip.recall(g, t), c, m, ml, ocean)
                    strip.save(emitted, t, e[:OWN_TILES])
                if t < SUB - 1:
                    strip.store(dst, l, v)
                h, u_prev = h_next, u
            strip.save(hd, t, h)
            strip.save(ud, t, u_prev)
            if t == 3:
                strip.save(hs, 2, h)
        if t < 3:
            write(us.at[t], us_out.at[t])
        if 0 < t < 4:
            write(hs.at[t - 1], hs_out.at[t - 1])

    write_series(series, emitted)
    for c in writes:
        c.wait()


def first_rest(
    coeff, state, upper, lower, one, three, hd, ud,
    final, hs_out, us_out, token,
    s0, s1, hs, us, sems,
):
    diff, mix = coefficients(coeff)
    token[...] = jnp.zeros_like(token)
    even, first, last = position()
    zero_pads(s0, LEVELS)
    zero_pads(s1, LEVELS)
    for l in range(CONE, LEVELS):
        place_rows(s0.at[l], state[l], upper[l], lower[l])

    def put(f, tile, value):
        s0[f, tile * 8 + 8 : tile * 8 + 16, CY:COLS] = value

    place_sides(put, list(range(CONE, LEVELS)), one, three, even, first, last)

    for t in range(SUB):
        src, dst = (s0, s1) if t % 2 == 0 else (s1, s0)

        for r in range(*strips(t)):
            strip = Strip(r, first, last)
            h = strip.recall(hd, t)
            u_prev = strip.recall(ud, t)
            for l in range(SUB - t, LEVELS):
                if l < LEVELS - 1:
                    h_next = strip.spread(src, l + 1, diff[l + 1])
                    u = flux_between(mix[l], h_next, h)
                    v = added(h, u)
                else:
                    h_next = u = None
                    v = h
                if l == t and t >= 3:
                    strip.save(us, t - 3, v)
                    strip.save(hs, t - 3, h)
                v = less(v, u_prev)
                if t < SUB - 1:
                    strip.store(dst, l, v)
                elif l >= SUB:
                    rows = slice(r * 8 - 16, r * 8 - 8)
                    for k in range(OWN_TILES):
                        final[l, rows, k * LANES : (k + 1) * LANES] = v[k]
                h, u_prev = h_next, u
    writes = [
        pltpu.make_async_copy(hs, hs_out, sems.at[0]),
        pltpu.make_async_copy(us, us_out, sems.at[1]),
    ]
    for c in writes:
        c.start()
    for c in writes:
        c.wait()


def balance(
    diff, mix, src, pat, weights, mask, after,
    out, wet, coeff,
    m, z, b, sem, *totals,
):
    del after
    for l in range(LEVELS):
        coeff[l] = jnp.full((8, LANES), diff[l], F32)
    for l in range(LEVELS - 1):
        coeff[LEVELS + l] = jnp.full((8, LANES), mix[l], F32)
    coeff[2 * LEVELS - 1] = jnp.zeros((8, LANES), F32)
    count = jnp.zeros((8, LANES), F32)
    for part in range(CX // 8):
        for j in range(OWN_TILES):
            v = mask[part * 8 : part * 8 + 8, j * LANES : (j + 1) * LANES].astype(F32)
            count += v
            m[pl.ds(part * 8 * OWN_TILES + j, 8, stride=OWN_TILES), :] = v
    _, lane = iotas()
    count = jnp.sum(count, axis=(0, 1), keepdims=True)
    wet[...] = jnp.where(lane[:1] == SUB, count, 0.0)
    blocks = m[...].astype(BF16)

    @pl.loop(0, PATTERNS, unroll=8)
    def _(p):
        z[p] = lax.dot_general(
            blocks, weights[p], (((1,), (1,)), ((), ())), preferred_element_type=F32
        )

    for j in range(OWN_TILES):
        totals[j][...] = jnp.zeros_like(totals[j])

    @pl.loop(0, CX, unroll=4)
    def _(r):
        for k in range(2):
            for j in range(OWN_TILES):
                row = pl.ds(src[j, k, r], 1)
                line = z[pat[j, k, r], pl.ds(r * OWN_TILES + j, 1), :]
                totals[j][row, :] = totals[j][row, :] + line

    m[...] = m[...] - ((totals[0][...] + totals[1][...]) + (totals[2][...] + totals[3][...]))
    for part in range(CX // 8):
        for j in range(OWN_TILES):
            v = m[pl.ds(part * 8 * OWN_TILES + j, 8, stride=OWN_TILES), :]
            b[part * 8 : part * 8 + 8, j * LANES : (j + 1) * LANES] = v
    c = pltpu.make_async_copy(b, out, sem)
    c.start()
    c.wait()


def share_rows(series, factor, wet, rows):
    partial = [jnp.zeros((8, LANES), F32) for _ in range(SUB)]
    for half in range(CX // 16):
        for j in range(OWN_TILES):
            cols = slice(j * LANES, (j + 1) * LANES)
            f = factor[half * 16 : half * 16 + 16, cols]
            for t in range(SUB):
                p = f * series[t, half * 16 : half * 16 + 16, cols].astype(F32)
                partial[t] += p[:8] + p[8:]
    row, lane = iotas()
    total = jnp.zeros((8, LANES), F32)
    for t, value in enumerate(partial):
        total = jnp.where(row == t, jnp.sum(value, axis=0, keepdims=True), total)
    total = jnp.sum(total, axis=1, keepdims=True)
    total = jnp.sum(jnp.where(row == lane, total, 0.0), axis=0, keepdims=True) + wet[...]
    for k in range(rows.shape[0]):
        rows[k] = total


def losses(
    received, factor, wet, before,
    gap, token,
    rows, sem,
):
    del before
    token[...] = jnp.zeros_like(token)
    share_rows(received, factor, wet, rows)
    c = pltpu.make_async_copy(rows, gap, sem)
    c.start()
    c.wait()


def edge_slots():
    for t, tile, start in ((0, 0, 0), (2, 0, 5), (1, 1, 0), (3, 1, 4), (4, 1, 6)):
        yield t, SUB - 1 - t, tile, start


def regrid(
    src, pat, received, weights_in, before,
    out, top, bottom,
    x, y, weights, sem,
):
    del before
    read = pltpu.make_async_copy(weights_in, weights, sem)
    read.start()
    for half in range(CX // 16):
        for j in range(OWN_TILES):
            cols = slice(j * LANES, (j + 1) * LANES)
            for t in range(SUB):
                v16 = received[t, half * 16 : half * 16 + 16, cols].astype(F32)
                for part in range(2):
                    row = half * 16 + part * 8
                    start = (row * OWN_TILES + j) * 8 + t
                    x[pl.ds(start, 8, stride=OWN_TILES * 8), :] = v16[part * 8 : part * 8 + 8]
    read.wait()
    for r in range(CX):
        for j in range(OWN_TILES):
            a, w = [], []
            for k in range(2):
                start = pl.multiple_of(src[j, k, r] * 8, 8)
                a.append(x[pl.ds(start, 8), :].astype(BF16))
                w.append(weights[pat[j, k, r]])
            product = jnp.dot(
                jnp.concatenate(a, 1), jnp.concatenate(w, 0), preferred_element_type=F32
            )
            y[pl.ds(r * OWN_TILES + j, 8, stride=BLOCKS), :] = product

    for part in range(CX // 8):
        for j in range(OWN_TILES):
            cols = slice(j * LANES, (j + 1) * LANES)
            for t in range(SUB):
                start = t * BLOCKS + part * 8 * OWN_TILES + j
                out[t, part * 8 : part * 8 + 8, cols] = y[pl.ds(start, 8, stride=OWN_TILES), :]
    top[1, 7:8, :] = jnp.zeros((1, CY), F32)
    bottom[1, 7:8, :] = jnp.zeros((1, CY), F32)
    for t, n, tile, start in edge_slots():
        top[tile, start : start + n, :] = out[t, 0:n, :]
        bottom[tile, start : start + n, :] = out[t, CX - n : CX, :]


def halo_rows(halo, upper, lower):
    halo[...] = jnp.zeros_like(halo)
    for t, n, tile, start in edge_slots():
        halo[t, 8 - n : 8, :] = upper[tile, start : start + n, :]
        halo[t, 8 : 8 + n, :] = lower[tile, start : start + n, :]


def pack_second(out, upper_in, lower_in, one, three, halo, upper, lower, sems):
    reads = [
        pltpu.make_async_copy(upper_in, upper, sems.at[0]),
        pltpu.make_async_copy(lower_in, lower, sems.at[1]),
    ]
    for c in reads:
        c.start()
    for c in reads:
        c.wait()
    even, _, _ = position()
    halo_rows(halo, upper, lower)

    def field(t):
        def of(tile):
            if tile in (0, 5):
                block, rows = halo.at[t], slice(0, 8) if tile == 0 else slice(8, 16)
            else:
                block, rows = out.at[t], slice(tile * 8 - 8, tile * 8)
            return block[rows, :LANES], block[rows, CY - LANES :]

        return of

    pack_columns([field(t) for t in range(SUB - 1)], one, three, even)


def gap_means(gap, start, count):
    total = jnp.sum(gap[pl.ds(start, count)], axis=0)
    lane = lax.broadcasted_iota(jnp.int32, (1, LANES), 1)
    wet = jnp.sum(jnp.where(lane == SUB, total, 0.0), axis=1, keepdims=True)
    return [
        jnp.sum(jnp.where(lane == t, total, 0.0), axis=1, keepdims=True) / wet for t in range(SUB)
    ]


def second_cone(
    fixed_in, regridded, upper_in, lower_in, one_in, three_in, gap_in, hs_in, us_in,
    series, final0, hx, ux, coeff,
    s0, s1, g, emitted, fixed, hs, us, halo, upper, lower, one, three, gap, sems,
):
    reads = []
    pairs = (
        (upper_in, upper), (lower_in, lower), (one_in, one), (three_in, three), (gap_in, gap),
        (us_in, us), (fixed_in, fixed), (hs_in, hs),
    )
    for i, (src, dst) in enumerate(pairs):
        reads.append(pltpu.make_async_copy(src, dst, sems.at[i]))
        reads[-1].start()
    even, first, last = position()
    ocean = lax.axis_index("comp") == 1
    zero_pads(s0, 3)
    zero_pads(s1, 3)
    for t in range(SUB):
        g[t, 8 : 8 + CX, :CY] = regridded[t]
    for c in reads[:5]:
        c.wait()
    halo_rows(halo, upper, lower)
    for t in range(SUB):
        if t < SUB - 1:
            g[t, 0:8, :CY] = halo[t, 0:8, :]
            g[t, 8 + CX : 16 + CX, :CY] = halo[t, 8:16, :]

    def put(f, tile, value):
        g[f, tile * 8 : tile * 8 + 8, CY:COLS] = value

    place_sides(put, list(range(SUB - 1)), one, three, even, first, last)
    g[SUB - 1, :, CY:COLS] = jnp.zeros((BAND, LANES), F32)
    means = [jnp.broadcast_to(v, (8, LANES)) for v in gap_means(gap, 0, gap.shape[0])]
    for c in reads[5:]:
        c.wait()
    for l in range(SUB):
        for i, start in ((l, 0), (SUB + l, LEVELS)):
            coeff[start + l] = fixed[(3, *coefficient_place(i))]
    diff, mix = coefficients(coeff)

    for t in range(SUB):
        src, dst = (s0, s1) if t % 2 == 0 else (s1, s0)

        for r in range(*strips(t)):
            strip = Strip(r, first, last)
            h = strip.spread(src, 0, diff[0]) if t else None
            u_prev = None
            for l in range(min(t, SUB - 1 - t) + 1):
                if l < t:
                    if l + 1 < t:
                        h_next = strip.spread(src, l + 1, diff[l + 1])
                    else:
                        h_next = strip.recall(hs, t - 1)
                    u = flux_between(mix[l], h_next, h)
                    v = added(h, u)
                else:
                    v = strip.recall(us, t)
                if u_prev is not None:
                    v = less(v, u_prev)
                if l == 0:
                    c, m, ml = (strip.recall(fixed, i) for i in range(3))
                    f = [a + b * means[t] for a, b in zip(strip.recall(g, t), m)]
                    v, e = surface(v, f, c, m, ml, ocean)
                    strip.save(emitted, t, e[:OWN_TILES])
                    if t == SUB - 1:
                        rows = slice(r * 8 - 16, r * 8 - 8)
                        for k in range(OWN_TILES):
                            final0[rows, k * LANES : (k + 1) * LANES] = v[k]
                if t < SUB - 1:
                    strip.store(dst, l, v)
                if l < t:
                    h, u_prev = h_next, u
            if t >= 3:
                strip.save(hx, t - 3, h)
                strip.save(ux, t - 3, u_prev)

    write_series(series, emitted)


def second_rest(
    coeff, hx, ux, hs_in, us_in, final0, series, factor, wet, whole,
    final, token, gap,
    s0, s1, hs, us, shares, sems,
):
    del whole
    share_rows(series, factor, wet, shares)
    send = pltpu.make_async_copy(shares, gap, sems.at[2])
    send.start()
    diff, mix = coefficients(coeff)
    reads = [
        pltpu.make_async_copy(us_in, us, sems.at[0]),
        pltpu.make_async_copy(hs_in, hs, sems.at[1]),
    ]
    for c in reads:
        c.start()
    token[...] = jnp.zeros_like(token)
    gy = lax.axis_index("gy")
    first, last = gy == 0, gy == lax.axis_size("gy") - 1
    zero_pads(s0, SUB)
    zero_pads(s1, SUB)
    final[0] = final0[...]
    for c in reads:
        c.wait()
    for t in range(3, SUB):
        src, dst = (s0, s1) if t % 2 == 0 else (s1, s0)

        for r in range(*strips(t)):
            strip = Strip(r, first, last)
            h = strip.recall(hx, t - 3)
            u_prev = strip.recall(ux, t - 3)
            for l in range(SUB - t, t + 1):
                if l < t:
                    if l + 1 < t:
                        h_next = strip.spread(src, l + 1, diff[l + 1])
                    else:
                        h_next = strip.recall(hs, t - 3)
                    u = flux_between(mix[l], h_next, h)
                    v = added(h, u)
                    h = h_next
                else:
                    u = None
                    v = strip.recall(us, t - 3)
                v = less(v, u_prev)
                u_prev = u
                if t < SUB - 1:
                    strip.store(dst, l, v)
                else:
                    rows = slice(r * 8 - 16, r * 8 - 8)
                    for k in range(OWN_TILES):
                        final[l, rows, k * LANES : (k + 1) * LANES] = v[k]
    send.wait()


def finish(regridded, mask, gap, forcing):
    peers = gap.shape[0] // 2
    start = (1 - lax.axis_index("comp")) * peers
    for t, mean in enumerate(gap_means(gap, start, peers)):
        forcing[t] = regridded[t] + mask[...].astype(F32) * mean


def shifted(value, axis, by):
    n = lax.axis_size(axis)
    return lax.ppermute(value, axis, [(i, (i + by) % n) for i in range(n)])


def paired(value, axis, mask):
    return lax.ppermute(value, axis, [(i, i ^ mask) for i in range(lax.axis_size(axis))])


def per_device(
    state, guess, diffusion, mixing, coupling, land_temp, land_mask, weights, source_block, pattern
):
    state, guess, diff, mix, coupling = state[0], guess[0], diffusion[0], mixing[0], coupling[0]
    weights = weights[0]
    src = source_block[0].transpose(1, 2, 0)
    pat = pattern[0].transpose(1, 2, 0)
    band = lambda n: shape(n, BAND, COLS)
    field_buf = lambda n: pltpu.VMEM((n, ROWS, COLS), F32)
    band_buf = lambda n: pltpu.VMEM((n, BAND, COLS), F32)
    numbers = shape(2 * LEVELS, 8, LANES)

    message = shape(LEVELS, 8, CY)
    to_lower, to_upper = call(
        first_edges,
        [message, message],
        [
            pltpu.VMEM((AUX, 8, CY), F32),
            pltpu.VMEM((AUX, 8, CY), F32),
            pltpu.VMEM((2, 8, CY), jnp.int32),
            pltpu.VMEM((2, SUB - 1, 16, CY), BF16),
            pltpu.SemaphoreType.DMA((10,)),
        ],
        [HBM] * 5,
        grant=EDGE_GRANT,
    )(state, guess, coupling, land_temp, land_mask)
    state, guess, coupling, land_temp, mask, table, src, pat, to_lower, to_upper = (
        lax.optimization_barrier(
            (
                state, guess, coupling, land_temp, land_mask, weights, src, pat,
                to_lower, to_upper,
            )
        )
    )
    lower, upper = shifted(to_lower, "gx", -1), shifted(to_upper, "gx", 1)
    factor, wet, coeff = call(
        balance,
        [shape(CX, CY), shape(1, LANES), shape(2 * LEVELS, 8, LANES)],
        [
            pltpu.VMEM((BLOCKS, LANES), F32),
            pltpu.VMEM((PATTERNS, BLOCKS, LANES), F32),
            pltpu.VMEM((CX, CY), F32),
            pltpu.SemaphoreType.DMA(()),
            *[pltpu.VMEM((BLOCKS, LANES), F32)] * OWN_TILES,
        ],
        [SM, SM, SM, SM, VM, VM, VM],
        out_specs=[HBM, VM, VM],
    )(diff, mix, src, pat, table, mask, to_lower)
    other = paired(factor, "comp", 1)
    packed = shape(BAND, PACK_LANES)
    aux, one, three = call(pack_first, [shape(AUX, 16, CY), packed, packed], [], [VM] * 8)(
        state, guess, coupling, land_temp, mask, upper, lower, wet
    )
    one, three = paired(one, "gy", 1), paired(three, "gy", 3)

    series, hd, ud, hs, us, fixed = call(
        first_cone,
        [
            shape(SUB, CX, CY, dtype=BF16), band(SUB), band(SUB),
            band(3), band(3), band(4),
        ],
        [
            field_buf(CONE), field_buf(CONE), band_buf(SUB), band_buf(SUB),
            band_buf(3), band_buf(3), band_buf(4), pltpu.SemaphoreType.DMA((7,)),
        ],
        [VM] * 11 + [pl.BlockSpec(memory_space=pl.ANY)],
        out_specs=[VM] * 3 + [HBM] * 3,
    )(coeff, state, guess, coupling, land_temp, mask, upper, lower, aux, one, three, other)

    def regridded(received, before):
        edges = shape(2, 8, CY)
        return call(
            regrid,
            [shape(SUB, CX, CY), edges, edges],
            [
                pltpu.VMEM((BLOCKS * 8, LANES), F32),
                pltpu.VMEM((BLOCKS * 8, LANES), F32),
                pltpu.VMEM((PATTERNS, LANES, LANES), BF16),
                pltpu.SemaphoreType.DMA(()),
            ],
            [SM, SM, VM, HBM, VM],
            cost_estimate=pl.CostEstimate(
                flops=2 * BLOCKS * 8 * 2 * LANES * LANES,
                bytes_accessed=BLOCKS * 2 * LANES * LANES * 2,
                transcendentals=0,
            ),
        )(src, pat, received, weights, before)

    whole, hs_rest, us_rest, token = call(
        first_rest,
        [shape(LEVELS, CX, CY), band(3), band(3), shape(8, LANES)],
        [
            field_buf(LEVELS), field_buf(LEVELS),
            band_buf(3), band_buf(3), pltpu.SemaphoreType.DMA((2,)),
        ],
        [VM] * 8,
        out_specs=[VM, HBM, HBM, VM],
    )(coeff, state, upper, lower, one, three, hd, ud)

    received = paired(series, "comp", 1)
    peers = lax.axis_size(("gx", "gy"))
    gap, after = call(
        losses,
        [shape(peers, 1, LANES), shape(8, LANES)],
        [pltpu.VMEM((peers, 1, LANES), F32), pltpu.SemaphoreType.DMA(())],
        [VM, VM, VM, VM],
        out_specs=[HBM, VM],
    )(received, factor, wet, token)
    gap = lax.all_to_all(gap, ("gx", "gy"), 0, 0)
    out, top, bottom = regridded(received, after)
    lower, upper = shifted(top, "gx", -1), shifted(bottom, "gx", 1)
    packed = shape(BAND, LANES)
    one, three = call(
        pack_second,
        [packed, packed],
        [
            pltpu.VMEM((SUB - 1, 16, CY), F32),
            pltpu.VMEM(upper.shape, F32),
            pltpu.VMEM(lower.shape, F32),
            pltpu.SemaphoreType.DMA((2,)),
        ],
        [VM, HBM, HBM],
    )(out, upper, lower)
    one, three = paired(one, "gy", 1), paired(three, "gy", 3)

    series, final0, hx, ux, coeff = call(
        second_cone,
        [shape(SUB, CX, CY, dtype=BF16), shape(CX, CY), band(3), band(3), numbers],
        [
            field_buf(3), field_buf(3), band_buf(SUB), band_buf(SUB),
            band_buf(4), band_buf(3), band_buf(3), pltpu.VMEM((SUB - 1, 16, CY), F32),
            *[pltpu.VMEM(v.shape, F32) for v in (upper, lower, one, three, gap)],
            pltpu.SemaphoreType.DMA((8,)),
        ],
        [HBM, VM] + [HBM] * 7,
    )(fixed, out, upper, lower, one, three, gap, hs, us)

    everyone = shape(2 * peers, 1, LANES)
    whole, token, gap = call(
        second_rest,
        [shape(LEVELS, CX, CY), shape(8, LANES), everyone],
        [
            field_buf(SUB), field_buf(SUB), band_buf(3), band_buf(3),
            pltpu.VMEM(everyone.shape, F32), pltpu.SemaphoreType.DMA((3,)),
        ],
        [VM, VM, VM, HBM, HBM, VM, VM, VM, VM, pl.BlockSpec(memory_space=pl.ANY)],
        out_specs=[pl.BlockSpec((SUB, CX, CY), lambda i: (0, 0, 0)), VM, HBM],
        grid=(1,),
        input_output_aliases={9: 0},
    )(coeff, hx, ux, hs_rest, us_rest, final0, series, other, wet, whole)

    received = paired(series, "comp", 1)
    gap = lax.all_to_all(gap, ("comp", "gx", "gy"), 0, 0)
    out, _, _ = regridded(received, token)
    (forcing,) = call(finish, [shape(SUB, CX, CY)], [], [VM] * 3)(out, land_mask, gap)
    return whole[None], forcing[None]


def solution(mesh):
    placed = (
        P("comp", None, "gx", "gy"),
        P("comp", None, "gx", "gy"),
        P("comp", None),
        P("comp", None),
        P("comp", "gx", "gy"),
        P("gx", "gy"),
        P("gx", "gy"),
        P("comp", ("gx", "gy"), None, None),
        P("comp", "gx", "gy", None),
        P("comp", "gx", "gy", None),
    )
    return jax.shard_map(
        per_device,
        mesh=mesh,
        in_specs=placed,
        out_specs=(P("comp", None, "gx", "gy"), P("comp", None, "gx", "gy")),
        check_vma=False,
    )
```
